256 devices in a mesh: dp: 16 (over z, core), own: 16 (over x, y).
Axes of the slice: x: 4, y: 4, z: 8, core: 2. Of those that a mesh axis runs over, the one named last changes fastest.
Arguments:
- tokens: bfloat16 [512, 256, 1024], P(('dp', 'own')), may hold values from -6 to 6
- cotangent: bfloat16 [512, 256, 1024], P(('dp', 'own')), may hold values from -6 to 6
- lengths: int32 [512], P(('dp', 'own')), may hold values from 1 to 256, as said below
- norm_gain: float32 [1024], replicated, may hold values from 0.1 to 12
- weight_in: bfloat16 [1024, 4096], P('own'), may hold values from -0.1875 to 0.1875
- weight_out: bfloat16 [1024, 1024], P('own'), may hold values from -0.1875 to 0.1875
- moment_in: float32 [1024, 4096], P('own'), may hold values from -6 to 6
- square_in: float32 [1024, 4096], P('own'), may hold values from 0.25 to 4
- moment_out: float32 [1024, 1024], P('own'), may hold values from -6 to 6
- square_out: float32 [1024, 1024], P('own'), may hold values from 0.25 to 4
Outputs:
- new_weight_in: float32 [1024, 4096], P('own')
- new_moment_in: float32 [1024, 4096], P('own')
- new_square_in: float32 [1024, 4096], P('own')
- new_weight_out: float32 [1024, 1024], P('own')
- new_moment_out: float32 [1024, 1024], P('own')
- new_square_out: float32 [1024, 1024], P('own')
The draws below stay inside these ranges and needn't reach their ends.
Inputs may be any that keep to these rules, and one draw needn't show every extreme that they name: `lengths`: the live events of a history are its first ones; some history holds 256.
All inputs are finite; a program needn't handle non-finite values.
Results may differ from the reference program's by a relative error of at most 0.004.
Values may be sent and summed in bfloat16 or wider, within the bound.
No kernel may reach another device: no remote copies, remote signals or barrier semaphores. Data moves between devices by JAX's collectives and lax.ppermute only.
A program may use at most 128 MiB of HBM per device.

```python
import math
import jax
import jax.numpy as jnp
from jax import lax

D = 1024
HEADS = 4
BLK = 256
SEQ_DEV = 2
SEQS = 512
N_DP = 16
N_OWN = 16


def draw_lengths(key, part):
    key = jax.random.fold_in(key, 5)
    slot_index = jnp.arange(SEQS, dtype=jnp.int32)
    group_index = slot_index // SEQ_DEV // N_OWN
    ceiling = 1 + (BLK - 1) * (group_index + 1) // N_DP
    raw_draw = jax.random.randint(key, (SEQS,), 0, 1 << 20, dtype=jnp.int32)
    drawn = 1 + raw_draw % ceiling
    return jnp.where(slot_index == SEQS - 1, BLK, drawn).astype(jnp.int32)


def draw_norm_gain(key, part):
    key = jax.random.fold_in(key, 7)
    ramp = jnp.arange(D, dtype=jnp.float32) / D
    spread = jax.random.uniform(key, (D,), jnp.float32)
    return 0.3 * jnp.exp(ramp * jnp.log(3.0) + spread * jnp.log(4.0))


def block_scale(rng, shape, cuts, low, top_value):
    level, own = 1.0, jax.random.fold_in(rng, 6)
    for dim, blocks in cuts:
        steps = jnp.exp(jax.random.uniform(jax.random.fold_in(own, dim), (blocks,), jnp.float32, low / len(cuts), top_value / len(cuts)))
        level = level * jnp.repeat(steps, shape[dim] // blocks).reshape([-1 if axis == dim else 1 for axis in range(len(shape))])
    return level


def gaussian(key, shape, scale, most, cuts=(), held_as=jnp.bfloat16):
    values = scale * jax.random.normal(key, shape, jnp.float32)
    if cuts:
        values = values * block_scale(key, shape, cuts, -0.22, 0.18)
    return jnp.clip(values, -most, most).astype(held_as)


def setup_inputs(seed: int = 0) -> dict:
    seeds = jax.random.split(jax.random.key(seed), 11)
    return {
        "tokens": gaussian(seeds[0], (SEQS, BLK, D), 1.0, 6.0, ((0, 256),)),
        "cotangent": gaussian(seeds[1], (SEQS, BLK, D), 1.0, 6.0, ((0, 256),)),
        "lengths": draw_lengths(jax.random.fold_in(seeds[10], 71), 0),
        "norm_gain": draw_norm_gain(jax.random.fold_in(seeds[10], 71), 0),
        "weight_in": gaussian(seeds[4], (D, 4 * D), D ** -0.5, 0.1875, ((0, 16),)),
        "weight_out": gaussian(seeds[5], (D, D), D ** -0.5, 0.1875, ((0, 16),)),
        "moment_in": gaussian(seeds[6], (D, 4 * D), 1.0, 6.0, ((0, 16),), jnp.float32),
        "square_in": jnp.clip(jnp.exp(math.log(4.0) - 2.7725887 * jax.random.uniform(seeds[7], (D, 4 * D), jnp.float32) ** block_scale(seeds[7], (D, 4 * D), ((0, 16),), -0.2, 0.2)), 0.25, 4.0),
        "moment_out": gaussian(seeds[8], (D, D), 1.0, 6.0, ((0, 16),), jnp.float32),
        "square_out": jnp.clip(jnp.exp(math.log(4.0) - 2.7725887 * jax.random.uniform(seeds[9], (D, D), jnp.float32) ** block_scale(seeds[9], (D, D), ((0, 16),), -0.2, 0.2)), 0.25, 4.0),
    }


norm_eps = 1e-06
beta_first = 0.9
beta_second = 0.95
learn_rate = 0.01
step_number = 10.0
update_eps = 1e-08
ratio_eps = 1e-06

def rms_scale(values):
    return values * lax.rsqrt(lax.optimization_barrier(jnp.mean(values * values, axis=-1, keepdims=True)) + norm_eps)

def slot_loss(projected, cot_masked, length, weight_full):
    row_count = projected.shape[0]
    activated = jax.nn.silu(projected)
    gating, values, queries, key_part = jnp.split(activated, 4, axis=1)
    head_width = values.shape[1] // HEADS
    values = values.astype(jnp.bfloat16).reshape(row_count, HEADS, head_width)
    queries = queries.astype(jnp.bfloat16).reshape(row_count, HEADS, head_width)
    key_part = key_part.astype(jnp.bfloat16).reshape(row_count, HEADS, head_width)
    scores = jnp.einsum('qhd,khd->hqk', queries.astype(jnp.float32), key_part.astype(jnp.float32)) * head_width ** (-0.5)
    row_index = jnp.arange(row_count, dtype=jnp.int32)
    allowed = (row_index[None, :] <= row_index[:, None]) & (row_index[:, None] < length)
    attention = (jax.nn.silu(scores) * allowed.astype(scores.dtype)[None, :, :] / BLK).astype(jnp.bfloat16)
    mixed = jnp.einsum('hqk,khd->qhd', attention.astype(jnp.float32), values.astype(jnp.float32)).reshape(row_count, -1)
    gated = (rms_scale(mixed) * gating).astype(jnp.bfloat16)
    output = jnp.dot(gated, weight_full, preferred_element_type=jnp.float32)
    return (jnp.sum(output * cot_masked.astype(output.dtype)), gated)

def slot_backward(projected, cot_masked, length, weight_full):

    def inner_loss(proj_rows):
        return slot_loss(proj_rows, cot_masked, length, weight_full)
    loss_value, pullback, gated = jax.vjp(inner_loss, projected, has_aux=True)
    grads = pullback(jnp.ones_like(loss_value))
    return (grads[0], gated)

def device_terms(tok_block, cot_block, len_block, norm_gain, weight_in, weight_out):
    slot_count, block_rows, model_width = tok_block.shape
    normed = (rms_scale(tok_block.astype(jnp.float32)) * norm_gain).astype(jnp.bfloat16)
    normed_rows = normed.reshape(slot_count * block_rows, model_width)
    projected = jnp.dot(normed_rows, weight_in, preferred_element_type=jnp.float32)
    projected = projected.reshape(slot_count, block_rows, -1)
    row_index = jnp.arange(block_rows, dtype=jnp.int32)
    live_rows = row_index[None, :] < len_block[:, None]
    cot_masked = jnp.where(live_rows[:, :, None], cot_block, jnp.zeros_like(cot_block))

    def one_slot(slot_items):
        return slot_backward(slot_items[0], slot_items[1], slot_items[2], weight_out)
    grad_projected, gated = lax.map(one_slot, (projected, cot_masked, len_block))
    grad_rows = grad_projected.reshape(slot_count * block_rows, -1).astype(jnp.bfloat16)
    term_in = jnp.dot(normed_rows.T, grad_rows, preferred_element_type=jnp.float32)
    term_out = jnp.dot(gated.reshape(-1, model_width).T, cot_masked.reshape(-1, model_width), preferred_element_type=jnp.float32)
    return (term_in, term_out)

def adam_parts(gradient, moment, square, clip_factor):
    scaled = gradient * clip_factor
    new_moment = beta_first * moment + (1.0 - beta_first) * scaled
    new_square = beta_second * square + (1.0 - beta_second) * scaled * scaled
    update = new_moment / (1.0 - beta_first ** step_number) / (jnp.sqrt(new_square / (1.0 - beta_second ** step_number)) + update_eps)
    return (new_moment, new_square, update)

def trust_step(weight, update, weight_sq, update_sq):
    trust_ratio = jnp.sqrt(weight_sq) / (jnp.sqrt(update_sq) + ratio_eps)
    return weight.astype(jnp.float32) - learn_rate * trust_ratio[:, None] * update

def row_sums(values):
    return lax.optimization_barrier(jnp.sum(values * values, axis=1))

def reference(tokens, cotangent, lengths, norm_gain, weight_in, weight_out, moment_in, square_in, moment_out, square_out):
    device_count = N_DP * N_OWN
    model_width = tokens.shape[2]
    tok_dev = tokens.reshape(device_count, SEQ_DEV, BLK, model_width)
    cot_dev = cotangent.reshape(device_count, SEQ_DEV, BLK, model_width)
    len_dev = lengths.reshape(device_count, SEQ_DEV)

    def accumulate(running, dev_items):
        term_in, term_out = device_terms(dev_items[0], dev_items[1], dev_items[2], norm_gain, weight_in, weight_out)
        rounded_in = lax.optimization_barrier(term_in.astype(jnp.bfloat16))
        rounded_out = lax.optimization_barrier(term_out.astype(jnp.bfloat16))
        return ((running[0] + rounded_in.astype(jnp.float32), running[1] + rounded_out.astype(jnp.float32)), 0)
    zero_totals = (jnp.zeros(weight_in.shape, jnp.float32), jnp.zeros(weight_out.shape, jnp.float32))
    totals, unused = lax.scan(accumulate, zero_totals, (tok_dev, cot_dev, len_dev))
    grad_in, grad_out = totals
    square_total = jnp.sum(grad_in * grad_in) + jnp.sum(grad_out * grad_out)
    clip_factor = jnp.minimum(1.0, jnp.sqrt(5.0 * model_width * model_width / (square_total + norm_eps)))
    new_moment_in, new_square_in, update_in = adam_parts(grad_in, moment_in, square_in, clip_factor)
    new_moment_out, new_square_out, update_out = adam_parts(grad_out, moment_out, square_out, clip_factor)
    weight_in_f = weight_in.astype(jnp.float32)
    weight_out_f = weight_out.astype(jnp.float32)
    new_weight_in = trust_step(weight_in_f, update_in, row_sums(weight_in_f), row_sums(update_in))
    new_weight_out = trust_step(weight_out_f, update_out, row_sums(weight_out_f), row_sums(update_out))
    return (new_weight_in, new_moment_in, new_square_in, new_weight_out, new_moment_out, new_square_out)
```

```python
import jax
import jax.numpy as jnp
from jax import lax
from jax.experimental import pallas as pl
from jax.experimental.pallas import tpu as pltpu
from jax.sharding import Mesh
from jax.sharding import PartitionSpec as P

BLK = 256
HEAD_WIDTH = 256

norm_eps = 1e-06
beta_first = 0.9
beta_second = 0.95
learn_rate = 0.01
step_number = 10.0
update_eps = 1e-08
ratio_eps = 1e-06

OWN = ("x", "y")
SWAP = ((0, 1), (1, 0))


def rms_scale(values):
    return values * lax.rsqrt(jnp.mean(values * values, axis=-1, keepdims=True) + norm_eps)


def sigmoid(values):
    return 1.0 / (1.0 + jnp.exp(-values))


def allowed_mask(length):
    row = lax.broadcasted_iota(jnp.int32, (BLK, BLK), 0)
    col = lax.broadcasted_iota(jnp.int32, (BLK, BLK), 1)
    return ((col <= row) & (row < length)).astype(jnp.float32) * (1.0 / BLK)


def dot_nt(left, right):
    return lax.dot_general(
        left, right, (((1,), (1,)), ((), ())), preferred_element_type=jnp.float32
    )


def dot_tn(left, right):
    return lax.dot_general(
        left, right, (((0,), (0,)), ((), ())), preferred_element_type=jnp.float32
    )


def forward_kernel(lengths, normed, weight, projected, scores, mixed):
    width = weight.shape[1] // 4
    proj = jnp.dot(normed[0], weight[...], preferred_element_type=jnp.float32)
    projected[0] = proj
    rest = proj[:, width:]
    rest = (rest * sigmoid(rest)).astype(jnp.bfloat16)
    allowed = allowed_mask(lengths[pl.program_id(0)])
    for head in range(width // HEAD_WIDTH):
        start = head * HEAD_WIDTH
        values = rest[:, start : start + HEAD_WIDTH]
        queries = rest[:, width + start : width + start + HEAD_WIDTH]
        key_part = rest[:, 2 * width + start : 2 * width + start + HEAD_WIDTH]
        score = dot_nt(queries, key_part) * HEAD_WIDTH ** (-0.5)
        scores[0, head] = score
        attention = (score * sigmoid(score) * allowed).astype(jnp.bfloat16)
        mixed[0, :, start : start + HEAD_WIDTH] = jnp.dot(
            attention, values, preferred_element_type=jnp.float32
        )


def stats_kernel(masked, weight_out, projected, mixed, grad_gated, stats):
    grad = dot_nt(masked[0], weight_out[...]).astype(jnp.bfloat16)
    grad_gated[0] = grad
    proj = projected[0]
    mix = mixed[0]
    square = jnp.sum(mix * mix, axis=1, keepdims=True)
    cross = jnp.sum(
        grad.astype(jnp.float32) * (proj * sigmoid(proj)) * mix, axis=1, keepdims=True
    )
    lane = lax.broadcasted_iota(jnp.int32, (BLK, 128), 1)
    stats[0] = jnp.where(lane == 0, square, cross)


def backward_kernel(
    lengths, projected, scores, mixed, grad_gated, stats, stats_other, gated, grad_proj
):
    width = mixed.shape[2]
    model_width = 2 * width
    total = stats[0] + stats_other[0]
    inv = lax.rsqrt(total[:, 0:1] / model_width + norm_eps)
    back = inv * inv * inv * (total[:, 1:2] / model_width)
    allowed = allowed_mask(lengths[pl.program_id(0)])

    proj = projected[0, :, :width]
    sig = sigmoid(proj)
    gating = proj * sig
    mix = mixed[0]
    grad = grad_gated[0].astype(jnp.float32)
    scaled = mix * inv
    gated[0] = (scaled * gating).astype(jnp.bfloat16)
    grad_proj[0, :, :width] = (grad * scaled * (sig + gating * (1.0 - sig))).astype(jnp.bfloat16)
    grad_mixed = (inv * (grad * gating) - mix * back).astype(jnp.bfloat16)

    for head in range(width // HEAD_WIDTH):
        start = head * HEAD_WIDTH
        acts, slopes = [], []
        for part in (1, 2, 3):
            block = projected[0, :, part * width + start : part * width + start + HEAD_WIDTH]
            sig = sigmoid(block)
            act = block * sig
            acts.append(act.astype(jnp.bfloat16))
            slopes.append(sig + act * (1.0 - sig))
        values, queries, key_part = acts
        score = scores[0, head]
        sig = sigmoid(score)
        act = score * sig
        attention = (act * allowed).astype(jnp.bfloat16)
        grad_head = grad_mixed[:, start : start + HEAD_WIDTH]
        grad_att = dot_nt(grad_head, values).astype(jnp.bfloat16).astype(jnp.float32)
        grad_score = (
            grad_att * allowed * (sig + act * (1.0 - sig)) * HEAD_WIDTH ** (-0.5)
        ).astype(jnp.bfloat16)
        grads = (
            dot_tn(attention, grad_head),
            jnp.dot(grad_score, key_part, preferred_element_type=jnp.float32),
            dot_tn(grad_score, queries),
        )
        for part in (1, 2, 3):
            held = grads[part - 1].astype(jnp.bfloat16).astype(jnp.float32)
            grad_proj[0, :, part * width + start : part * width + start + HEAD_WIDTH] = (
                held * slopes[part - 1]
            ).astype(jnp.bfloat16)


def row_block(*dims):
    return pl.BlockSpec((1, *dims), lambda i, *_: (i,) + (0,) * len(dims))


def whole_block(*dims):
    return pl.BlockSpec(dims, lambda i, *_: (0,) * len(dims))


VMEM_LIMIT = 48 * 1024 * 1024


def attention_forward(lengths, normed, weight):
    count, rows, depth = normed.shape
    columns = weight.shape[1]
    width = columns // 4
    heads = width // HEAD_WIDTH
    return pl.pallas_call(
        forward_kernel,
        grid_spec=pltpu.PrefetchScalarGridSpec(
            num_scalar_prefetch=1,
            grid=(count,),
            in_specs=[row_block(rows, depth), whole_block(depth, columns)],
            out_specs=[
                row_block(rows, columns),
                row_block(heads, rows, rows),
                row_block(rows, width),
            ],
        ),
        out_shape=[
            jax.ShapeDtypeStruct((count, rows, columns), jnp.float32),
            jax.ShapeDtypeStruct((count, heads, rows, rows), jnp.float32),
            jax.ShapeDtypeStruct((count, rows, width), jnp.float32),
        ],
        compiler_params=pltpu.CompilerParams(vmem_limit_bytes=VMEM_LIMIT),
        name="attention_forward",
    )(lengths, normed, weight)


def norm_stats(masked, weight_out, projected, mixed):
    count, rows, model_width = masked.shape
    width = weight_out.shape[0]
    return pl.pallas_call(
        stats_kernel,
        grid=(count,),
        in_specs=[
            row_block(rows, model_width),
            whole_block(width, model_width),
            row_block(rows, width),
            row_block(rows, width),
        ],
        out_specs=[row_block(rows, width), row_block(rows, 128)],
        out_shape=[
            jax.ShapeDtypeStruct((count, rows, width), jnp.bfloat16),
            jax.ShapeDtypeStruct((count, rows, 128), jnp.float32),
        ],
        compiler_params=pltpu.CompilerParams(vmem_limit_bytes=VMEM_LIMIT),
        name="norm_stats",
    )(masked, weight_out, projected, mixed)


def attention_backward(lengths, projected, scores, mixed, grad_gated, stats, stats_other):
    count, rows, columns = projected.shape
    width = columns // 4
    heads = width // HEAD_WIDTH
    return pl.pallas_call(
        backward_kernel,
        grid_spec=pltpu.PrefetchScalarGridSpec(
            num_scalar_prefetch=1,
            grid=(count,),
            in_specs=[
                row_block(rows, columns),
                row_block(heads, rows, rows),
                row_block(rows, width),
                row_block(rows, width),
                row_block(rows, 128),
                pl.BlockSpec((1, rows, 128), lambda i, *_: ((i + count // 2) % count, 0, 0)),
            ],
            out_specs=[row_block(rows, width), row_block(rows, columns)],
        ),
        out_shape=[
            jax.ShapeDtypeStruct((count, rows, width), jnp.bfloat16),
            jax.ShapeDtypeStruct((count, rows, columns), jnp.bfloat16),
        ],
        compiler_params=pltpu.CompilerParams(vmem_limit_bytes=VMEM_LIMIT),
        name="attention_backward",
    )(lengths, projected, scores, mixed, grad_gated, stats, stats_other)


def adam_parts(gradient, moment, square, clip_factor):
    scaled = gradient * clip_factor
    new_moment = beta_first * moment + (1.0 - beta_first) * scaled
    new_square = beta_second * square + (1.0 - beta_second) * scaled * scaled
    update = (
        new_moment
        / (1.0 - beta_first**step_number)
        / (jnp.sqrt(new_square / (1.0 - beta_second**step_number)) + update_eps)
    )
    return (new_moment, new_square, update)


def trust_step(weight, update):
    weight = weight.astype(jnp.float32)
    weight_sq = jnp.sum(weight * weight, axis=1, keepdims=True)
    update_sq = jnp.sum(update * update, axis=1, keepdims=True)
    trust_ratio = jnp.sqrt(weight_sq) / (jnp.sqrt(update_sq) + ratio_eps)
    return weight - learn_rate * trust_ratio * update


def swap_cores(values):
    return lax.ppermute(values, "c", SWAP)


def in_core_order(core, mine, other, axis):
    first = jnp.where(core == 0, mine, other)
    second = jnp.where(core == 0, other, mine)
    return jnp.stack([first, second], axis=axis)


def exchange(blocks, axes):
    return lax.all_to_all(blocks, axes, 0, 0, tiled=True)


def per_device(
    tokens,
    cotangent,
    lengths,
    norm_gain,
    weight_in,
    weight_out,
    moment_in,
    square_in,
    moment_out,
    square_out,
):
    slots, rows, model_width = tokens.shape
    half = model_width // 2
    core = lax.axis_index("c")
    owners = lax.axis_size(OWN)
    planes = lax.axis_size("z")
    owned = weight_in.shape[0]

    weight_out_full = lax.all_gather(weight_out, OWN, axis=0, tiled=True)
    mine = lax.dynamic_index_in_dim(
        weight_in.reshape(owned, 4, 2, half), core, axis=2, keepdims=False
    ).reshape(owned, 4 * half)
    weight_cols = exchange(
        jnp.broadcast_to(mine[None], (owners, *mine.shape)).reshape(owners * owned, -1), OWN
    )

    normed = (rms_scale(tokens.astype(jnp.float32)) * norm_gain).astype(jnp.bfloat16)
    row_index = jnp.arange(rows, dtype=jnp.int32)
    live = row_index[None, :] < lengths[:, None]
    masked = jnp.where(live[:, :, None], cotangent, jnp.zeros_like(cotangent))
    normed = jnp.concatenate([normed, swap_cores(normed)], axis=0)
    masked = jnp.concatenate([masked, swap_cores(masked)], axis=0)
    lengths = jnp.concatenate([lengths, swap_cores(lengths)], axis=0)

    projected, scores, mixed = attention_forward(lengths, normed, weight_cols)
    weight_rows = lax.dynamic_slice_in_dim(weight_out_full, core * half, half, axis=0)
    grad_gated, stats = norm_stats(masked, weight_rows, projected, mixed)
    gated, grad_proj = attention_backward(
        lengths, projected, scores, mixed, grad_gated, stats, swap_cores(stats)
    )

    normed_rows = normed.reshape(-1, model_width)
    masked_rows = masked.reshape(-1, model_width)
    term_in = dot_tn(normed_rows, grad_proj.reshape(normed_rows.shape[0], -1)).astype(jnp.bfloat16)
    term_out = dot_tn(gated.reshape(-1, half), masked_rows).astype(jnp.bfloat16)
    columns = term_out.reshape(half, 2, half)
    keep = lax.dynamic_index_in_dim(columns, core, axis=1, keepdims=False)
    give = lax.dynamic_index_in_dim(columns, 1 - core, axis=1, keepdims=False)
    term_out = in_core_order(core, keep, swap_cores(give), 0).reshape(model_width, half)

    term = jnp.concatenate([term_in, term_out], axis=1)
    part = jnp.sum(
        exchange(term, OWN).reshape(owners, owned, -1).astype(jnp.float32), axis=0
    ).astype(jnp.bfloat16)
    piece = jnp.sum(
        exchange(part, "z").reshape(planes, owned // planes, -1).astype(jnp.float32), axis=0
    ).astype(jnp.bfloat16)
    shard = exchange(
        jnp.broadcast_to(piece[None], (planes, *piece.shape)).reshape(owned, -1), "z"
    )
    grad = in_core_order(core, shard.reshape(owned, 5, half), swap_cores(shard).reshape(owned, 5, half), 2)
    grad = grad.astype(jnp.float32)
    grad_in = grad[:, :4].reshape(owned, 4 * model_width)
    grad_out = grad[:, 4].reshape(owned, model_width)

    local_square = jnp.sum(grad * grad)
    squares = exchange(jnp.broadcast_to(local_square, (owners, 8, 128)).reshape(-1, 128), OWN)
    square_total = jnp.sum(squares.reshape(owners, 8, 128)[:, 0, 0])
    clip_factor = jnp.minimum(
        1.0, jnp.sqrt(5.0 * model_width * model_width / (square_total + norm_eps))
    )
    new_moment_in, new_square_in, update_in = adam_parts(grad_in, moment_in, square_in, clip_factor)
    new_moment_out, new_square_out, update_out = adam_parts(
        grad_out, moment_out, square_out, clip_factor
    )
    return (
        trust_step(weight_in, update_in),
        new_moment_in,
        new_square_in,
        trust_step(weight_out, update_out),
        new_moment_out,
        new_square_out,
    )


def solution(mesh):
    fine = Mesh(mesh.devices.reshape(8, 2, 4, 4), ("z", "c", "x", "y"))
    histories = ("z", "c", "x", "y")
    placed = (
        P(histories, None, None),
        P(histories, None, None),
        P(histories),
        P(),
        P(OWN, None),
        P(OWN, None),
        P(OWN, None),
        P(OWN, None),
        P(OWN, None),
        P(OWN, None),
    )
    return jax.shard_map(
        per_device,
        mesh=fine,
        in_specs=placed,
        out_specs=(P(OWN, None),) * 6,
        check_vma=False,
    )
```

```python
import functools

import jax
import jax.numpy as jnp
from jax import lax
from jax.experimental import pallas as pl
from jax.experimental.pallas import tpu as pltpu
from jax.sharding import Mesh
from jax.sharding import PartitionSpec as P

BLK = 256
HEAD_WIDTH = 256

norm_eps = 1e-06
beta_first = 0.9
beta_second = 0.95
learn_rate = 0.01
step_number = 10.0
update_eps = 1e-08
ratio_eps = 1e-06

OWN = ("x", "y")
SWAP = ((0, 1), (1, 0))

LINKS = (("x", 1), ("y", 1), ("x", 3), ("y", 3))
LINK_MASKS = (0b0100, 0b0001, 0b1100, 0b0011)


def rms_scale(values):
    return values * lax.rsqrt(jnp.mean(values * values, axis=-1, keepdims=True) + norm_eps)


def sigmoid(values):
    return 1.0 / (1.0 + jnp.exp(-values))


def allowed_mask(length):
    row = lax.broadcasted_iota(jnp.int32, (BLK, BLK), 0)
    col = lax.broadcasted_iota(jnp.int32, (BLK, BLK), 1)
    return ((col <= row) & (row < length)).astype(jnp.float32) * (1.0 / BLK)


def dot_nt(left, right):
    return lax.dot_general(
        left, right, (((1,), (1,)), ((), ())), preferred_element_type=jnp.float32
    )


def dot_tn(left, right):
    return lax.dot_general(
        left, right, (((0,), (0,)), ((), ())), preferred_element_type=jnp.float32
    )


def dot_nn(left, right):
    return jnp.dot(left, right, preferred_element_type=jnp.float32)


def silu_slope(values):
    sig = sigmoid(values)
    act = values * sig
    return act, sig + act * (1.0 - sig)


def relative_slot(mask, turn):
    x_far, x_near = (mask >> 3) & 1, ((mask >> 3) ^ (mask >> 2)) & 1
    y_far, y_near = (mask >> 1) & 1, ((mask >> 1) ^ mask) & 1
    bits = (x_near, y_near, x_far, y_far)
    slot = 0
    for step in range(4):
        slot = slot + (bits[(turn + step) % 4] << step)
    return slot


def owner_mask(slot, turn):
    mask = 0
    for step in range(4):
        if slot >> step & 1:
            mask ^= LINK_MASKS[(turn + step) % 4]
    return mask


def place_rows(turn, own, near, far, weight):
    count, rows, _ = near.shape
    for slot in range(2 * count):
        block = near[slot] if slot < count else far[slot - count]
        start = pl.multiple_of((own ^ owner_mask(slot, turn)) * rows, rows)
        weight[pl.ds(start, rows), :] = block


def project_kernel(turn, place, normed, near, far, projected, rest, weight):
    width = projected.shape[2]

    @pl.when(pl.program_id(0) == 0)
    def _():
        place_rows(turn, place[0], near, far, weight)
        rest[...] = weight[:, width:]

    projected[0] = dot_nn(normed[0], weight[:, :width])


def attention_kernel(
    turn, place, lengths, normed, near, far, queries_in, keys_in, values_out, scores, mixed, weight
):
    @pl.when(pl.program_id(0) == 0)
    def _():
        place_rows(turn, place[0], near, far, weight)

    proj = dot_nn(normed[0], weight[...])
    values_out[0] = proj
    allowed = allowed_mask(lengths[pl.program_id(0)])
    for head in range(proj.shape[1] // HEAD_WIDTH):
        part = slice(head * HEAD_WIDTH, (head + 1) * HEAD_WIDTH)
        values, queries, key_part = (
            (block * sigmoid(block)).astype(jnp.bfloat16)
            for block in (proj[:, part], queries_in[0, :, part], keys_in[0, :, part])
        )
        score = dot_nt(queries, key_part) * HEAD_WIDTH ** (-0.5)
        scores[0, head] = score
        attention = (score * sigmoid(score) * allowed).astype(jnp.bfloat16)
        mixed[0, :, part] = dot_nn(attention, values)


def gating_kernel(
    turn, place, normed, near, far, masked, keep, recv, mixed, gating_out, grad_gated, stats, weight
):
    width = keep.shape[0]

    @pl.when(pl.program_id(0) == 0)
    def _():
        place_rows(turn, place[0], near, far, weight)

    proj = dot_nn(normed[0], weight[...])
    gating_out[0] = proj
    core = place[1]
    mine = masked[0, :, pl.ds(pl.multiple_of(core * width, width), width)]
    others = masked[0, :, pl.ds(pl.multiple_of((1 - core) * width, width), width)]
    grad = (dot_nt(mine, keep[...]) + dot_nt(others, recv[...])).astype(jnp.bfloat16)
    grad_gated[0] = grad
    mix = mixed[0]
    square = jnp.sum(mix * mix, axis=1, keepdims=True)
    cross = jnp.sum(
        grad.astype(jnp.float32) * (proj * sigmoid(proj)) * mix, axis=1, keepdims=True
    )
    lane = lax.broadcasted_iota(jnp.int32, (BLK, 128), 1)
    stats[0] = jnp.where(lane == 0, square, cross)


def norm_back_kernel(
    projected, mixed, grad_gated, stats, stats_other, gated, grad_gating, grad_mixed
):
    model_width = 2 * mixed.shape[2]
    total = stats[0] + stats_other[0]
    inv = lax.rsqrt(total[:, 0:1] / model_width + norm_eps)
    back = inv * inv * inv * (total[:, 1:2] / model_width)
    gating, slope = silu_slope(projected[0])
    mix = mixed[0]
    grad = grad_gated[0].astype(jnp.float32)
    scaled = mix * inv
    gated[0] = (scaled * gating).astype(jnp.bfloat16)
    grad_gating[0] = (grad * scaled * slope).astype(jnp.bfloat16)
    grad_mixed[0] = (inv * (grad * gating) - mix * back).astype(jnp.bfloat16)


def attention_back_kernel(
    lengths, values_in, queries_in, keys_in, scores, grad_mixed, grad_values, grad_queries, grad_keys
):
    allowed = allowed_mask(lengths[pl.program_id(0)])
    for head in range(grad_mixed.shape[2] // HEAD_WIDTH):
        part = slice(head * HEAD_WIDTH, (head + 1) * HEAD_WIDTH)
        values, values_slope = silu_slope(values_in[0, :, part])
        queries, queries_slope = silu_slope(queries_in[0, :, part])
        key_part, keys_slope = silu_slope(keys_in[0, :, part])
        act, slope = silu_slope(scores[0, head])
        attention = (act * allowed).astype(jnp.bfloat16)
        grad_head = grad_mixed[0, :, part]
        grad_att = dot_nt(grad_head, values.astype(jnp.bfloat16)).astype(jnp.bfloat16)
        grad_score = (
            grad_att.astype(jnp.float32) * allowed * slope * HEAD_WIDTH ** (-0.5)
        ).astype(jnp.bfloat16)
        for out, grad, side in (
            (grad_values, dot_tn(attention, grad_head), values_slope),
            (grad_queries, dot_nn(grad_score, key_part.astype(jnp.bfloat16)), queries_slope),
            (grad_keys, dot_tn(grad_score, queries.astype(jnp.bfloat16)), keys_slope),
        ):
            held = grad.astype(jnp.bfloat16).astype(jnp.float32)
            out[0, :, part] = (held * side).astype(jnp.bfloat16)


def store_slot(slot, value, columns, near, far):
    count = near.shape[0]

    @pl.when(slot < count)
    def _():
        near[jnp.minimum(slot, count - 1), :, columns] = value

    @pl.when(slot >= count)
    def _():
        far[jnp.maximum(slot - count, 0), :, columns] = value


def term_kernel(turn, place, normed_t, grads, *refs):
    near, far = refs[-2:]
    rows, width = near.shape[1], grads.shape[1]
    term = dot_nn(normed_t[...], grads[...]).astype(jnp.bfloat16)
    step = pl.program_id(0)
    per_step = term.shape[0] // rows
    for block in range(per_step):
        slot = relative_slot((step * per_step + block) ^ place[0], turn)
        store_slot(slot, term[block * rows : (block + 1) * rows], slice(0, width), near, far)
    if len(refs) == 4:
        half = refs[0].shape[0] // rows
        per_step = half // pl.num_programs(0)
        for side, held in ((place[1], refs[0]), (1 - place[1], refs[1])):
            for block in range(per_step):
                at = step * per_step + block
                value = held[pl.ds(pl.multiple_of(at * rows, rows), rows), :]
                slot = relative_slot((side * half + at) ^ place[0], turn)
                store_slot(slot, value, slice(width, width + value.shape[1]), near, far)


def term_out_kernel(place, gated, masked, term):
    term[0] = dot_tn(gated[...], masked[...]).astype(jnp.bfloat16)


def rows_of(*dims):
    return pl.BlockSpec((1, *dims), lambda i, *_: (i,) + (0,) * len(dims))


def whole(*dims):
    return pl.BlockSpec(dims, lambda i, *_: (0,) * len(dims))


def call(kernel, name, grid, prefetch, in_specs, out, inputs, scratch=(), flops=0):
    moved = sum(v.size * v.dtype.itemsize for v in inputs)
    return pl.pallas_call(
        kernel,
        grid_spec=pltpu.PrefetchScalarGridSpec(
            num_scalar_prefetch=len(prefetch),
            grid=grid,
            in_specs=in_specs,
            out_specs=[spec for spec, _, _ in out],
            scratch_shapes=list(scratch),
        ),
        out_shape=[jax.ShapeDtypeStruct(shape, dtype) for _, shape, dtype in out],
        compiler_params=pltpu.CompilerParams(vmem_limit_bytes=40 * 1024 * 1024),
        cost_estimate=pl.CostEstimate(flops=flops, bytes_accessed=moved, transcendentals=0),
        name=name,
    )(*prefetch, *inputs)


def project(turn, place, normed, near, far, width):
    count, rows, depth = normed.shape
    columns = near.shape[2]
    return call(
        functools.partial(project_kernel, turn),
        "project",
        (count,),
        (place,),
        [rows_of(rows, depth), whole(*near.shape), whole(*far.shape)],
        [
            (rows_of(rows, width), (count, rows, width), jnp.float32),
            (whole(depth, columns - width), (depth, columns - width), jnp.bfloat16),
        ],
        (normed, near, far),
        [pltpu.VMEM((depth, columns), jnp.bfloat16)],
        2 * count * rows * depth * width,
    )


def attention_forward(turn, place, lengths, normed, near, far, queries, keys_in):
    count, rows, depth = normed.shape
    width = near.shape[2]
    heads = width // HEAD_WIDTH
    return call(
        functools.partial(attention_kernel, turn),
        "attention_forward",
        (count,),
        (place, lengths),
        [rows_of(rows, depth), whole(*near.shape), whole(*far.shape)] + [rows_of(rows, width)] * 2,
        [
            (rows_of(rows, width), (count, rows, width), jnp.float32),
            (rows_of(heads, rows, rows), (count, heads, rows, rows), jnp.float32),
            (rows_of(rows, width), (count, rows, width), jnp.float32),
        ],
        (normed, near, far, queries, keys_in),
        [pltpu.VMEM((depth, width), jnp.bfloat16)],
        3 * count * rows * depth * width,
    )


def gating_forward(turn, place, normed, near, far, masked, keep, recv, mixed):
    count, rows, depth = normed.shape
    width = near.shape[2]
    return call(
        functools.partial(gating_kernel, turn),
        "gating_forward",
        (count,),
        (place,),
        [
            rows_of(rows, depth),
            whole(*near.shape),
            whole(*far.shape),
            rows_of(rows, depth),
            whole(*keep.shape),
            whole(*recv.shape),
            rows_of(rows, width),
        ],
        [
            (rows_of(rows, width), (count, rows, width), jnp.float32),
            (rows_of(rows, width), (count, rows, width), jnp.bfloat16),
            (rows_of(rows, 128), (count, rows, 128), jnp.float32),
        ],
        (normed, near, far, masked, keep, recv, mixed),
        [pltpu.VMEM((depth, width), jnp.bfloat16)],
        4 * count * rows * depth * width,
    )


def norm_back(projected, mixed, grad_gated, stats, stats_other):
    count, rows, width = projected.shape
    block = rows_of(rows, width)
    return call(
        norm_back_kernel,
        "norm_back",
        (count,),
        (),
        [
            block,
            block,
            block,
            rows_of(rows, 128),
            pl.BlockSpec((1, rows, 128), lambda i, *_: ((i + count // 2) % count, 0, 0)),
        ],
        [(block, projected.shape, jnp.bfloat16)] * 3,
        (projected, mixed, grad_gated, stats, stats_other),
    )


def attention_back(lengths, values, queries, keys_in, scores, grad_mixed):
    count, rows, width = values.shape
    heads = width // HEAD_WIDTH
    block = rows_of(rows, width)
    return call(
        attention_back_kernel,
        "attention_back",
        (count,),
        (lengths,),
        [block, block, block, rows_of(heads, rows, rows), block],
        [(block, values.shape, jnp.bfloat16)] * 3,
        (values, queries, keys_in, scores, grad_mixed),
        flops=8 * count * rows * rows * width,
    )


def term(turn, place, owned, normed_t, grads, extra=None):
    depth, rows = normed_t.shape
    width = grads.shape[1]
    steps = 4
    owners = depth // owned
    columns = width
    in_specs = [
        pl.BlockSpec((depth // steps, rows), lambda i, *_: (i, 0)),
        whole(rows, width),
    ]
    inputs = [normed_t, grads]
    if extra is not None:
        keep, recv, at = extra
        share = keep.shape[1] // 2
        columns += share
        in_specs += [pl.BlockSpec((keep.shape[0], share), lambda i, *_: (0, at))] * 2
        inputs += [keep, recv]
    shape = (owners // 2, owned, columns)
    return call(
        functools.partial(term_kernel, turn),
        "term",
        (steps,),
        (place,),
        in_specs,
        [(whole(*shape), shape, jnp.bfloat16)] * 2,
        inputs,
        flops=2 * depth * rows * width,
    )


def term_out(place, gated, masked):
    rows, width = gated.shape
    return call(
        term_out_kernel,
        "term_out",
        (2,),
        (place,),
        [whole(rows, width), pl.BlockSpec((rows, width), lambda i, s: (0, (i + s[1]) % 2))],
        [(rows_of(width, width), (2, width, width), jnp.bfloat16)],
        (gated, masked),
        flops=4 * rows * width * width,
    )[0]


def adam_parts(gradient, moment, square, clip_factor):
    scaled = gradient * clip_factor
    new_moment = beta_first * moment + (1.0 - beta_first) * scaled
    new_square = beta_second * square + (1.0 - beta_second) * scaled * scaled
    update = (
        new_moment
        / (1.0 - beta_first**step_number)
        / (jnp.sqrt(new_square / (1.0 - beta_second**step_number)) + update_eps)
    )
    return (new_moment, new_square, update)


def trust_step(weight, update):
    weight = weight.astype(jnp.float32)
    weight_sq = jnp.sum(weight * weight, axis=1, keepdims=True)
    update_sq = jnp.sum(update * update, axis=1, keepdims=True)
    trust_ratio = jnp.sqrt(weight_sq) / (jnp.sqrt(update_sq) + ratio_eps)
    return weight - learn_rate * trust_ratio * update


def swap_cores(values):
    return lax.ppermute(values, "c", SWAP)


def over_link(values, link):
    axis, mask = LINKS[link % 4]
    return lax.ppermute(values, axis, [(i, i ^ mask) for i in range(4)])


def gather_parts(parts):
    held = [part[None] for part in parts]
    for step in range(3):
        got = [over_link(part, turn + step) for turn, part in enumerate(held)]
        held = [jnp.concatenate(pair, axis=0) for pair in zip(held, got)]
    return [(part, over_link(part, turn + 3)) for turn, part in enumerate(held)]


def add_halves(mine, got):
    return (mine.astype(jnp.float32) + got.astype(jnp.float32)).astype(jnp.bfloat16)


def scatter_part(turn, near, far):
    for step in (3, 2, 1, 0):
        total = add_halves(near, over_link(far, turn + step))
        near, far = jnp.split(total, 2, axis=0) if step else (total, None)
    return near[0]


def in_core_order(core, mine, other, axis):
    first = jnp.where(core == 0, mine, other)
    second = jnp.where(core == 0, other, mine)
    return jnp.stack([first, second], axis=axis)


def exchange(blocks, axes):
    return lax.all_to_all(blocks, axes, 0, 0, tiled=True)


def per_device(
    tokens,
    cotangent,
    lengths,
    norm_gain,
    weight_in,
    weight_out,
    moment_in,
    square_in,
    moment_out,
    square_out,
):
    slots, rows, model_width = tokens.shape
    half = model_width // 2
    quarter = half // 2
    core = lax.axis_index("c")
    own = lax.axis_index(OWN)
    owners = lax.axis_size(OWN)
    planes = lax.axis_size("z")
    owned = weight_in.shape[0]
    place = jnp.stack([own, core]).astype(jnp.int32)

    mine = lax.dynamic_index_in_dim(
        weight_in.reshape(owned, 4, 2, half), core, axis=2, keepdims=False
    )
    mine_out = lax.dynamic_slice_in_dim(weight_out, core * half, half, axis=1)
    (q_near, q_far), (k_near, k_far), (v_near, v_far), (g_near, g_far) = gather_parts(
        [
            jnp.concatenate([mine[:, 2], mine_out[:, :quarter]], axis=1),
            jnp.concatenate([mine[:, 3], mine_out[:, quarter:]], axis=1),
            mine[:, 1],
            mine[:, 0],
        ]
    )

    normed = (rms_scale(tokens.astype(jnp.float32)) * norm_gain).astype(jnp.bfloat16)
    row_index = jnp.arange(rows, dtype=jnp.int32)
    live = row_index[None, :] < lengths[:, None]
    masked = jnp.where(live[:, :, None], cotangent, jnp.zeros_like(cotangent))
    normed = jnp.concatenate([normed, swap_cores(normed)], axis=0)
    masked = jnp.concatenate([masked, swap_cores(masked)], axis=0)
    lengths = jnp.concatenate([lengths, swap_cores(lengths)], axis=0)
    normed_t = normed.reshape(-1, model_width).T

    queries, out_first = project(0, place, normed, q_near, q_far, half)
    keys_in, out_second = project(1, place, normed, k_near, k_far, half)
    out_cols = jnp.concatenate([out_first, out_second], axis=1).reshape(2, half, half)
    keep = lax.dynamic_index_in_dim(out_cols, core, axis=0, keepdims=False)
    recv = swap_cores(lax.dynamic_index_in_dim(out_cols, 1 - core, axis=0, keepdims=False))
    values, scores, mixed = attention_forward(
        2, place, lengths, normed, v_near, v_far, queries, keys_in
    )
    gating, grad_gated, stats = gating_forward(
        3, place, normed, g_near, g_far, masked, keep, recv, mixed
    )
    gated, grad_gating, grad_mixed = norm_back(
        gating, mixed, grad_gated, stats, swap_cores(stats)
    )

    def flat(part):
        return part.reshape(-1, part.shape[2])

    part_g = scatter_part(0, *term(0, place, owned, normed_t, flat(grad_gating)))
    outer = term_out(place, flat(gated), flat(masked))
    outer_recv = swap_cores(outer[1])
    grad_values, grad_queries, grad_keys = attention_back(
        lengths, values, queries, keys_in, scores, grad_mixed
    )
    part_v = scatter_part(
        1, *term(1, place, owned, normed_t, flat(grad_values), (outer[0], outer_recv, 0))
    )
    part_q = scatter_part(
        2, *term(2, place, owned, normed_t, flat(grad_queries), (outer[0], outer_recv, 1))
    )
    part_k = scatter_part(3, *term(3, place, owned, normed_t, flat(grad_keys)))
    part = jnp.concatenate(
        [part_g, part_v[:, :half], part_q[:, :half], part_k, part_v[:, half:], part_q[:, half:]],
        axis=1,
    )

    piece = jnp.sum(
        exchange(part, "z").reshape(planes, owned // planes, -1).astype(jnp.float32), axis=0
    ).astype(jnp.bfloat16)
    shard = exchange(
        jnp.broadcast_to(piece[None], (planes, *piece.shape)).reshape(owned, -1), "z"
    )
    grad = in_core_order(core, shard.reshape(owned, 5, half), swap_cores(shard).reshape(owned, 5, half), 2)
    grad = grad.astype(jnp.float32)
    grad_in = grad[:, :4].reshape(owned, 4 * model_width)
    grad_out = grad[:, 4].reshape(owned, model_width)

    local_square = jnp.sum(grad * grad)
    squares = exchange(jnp.broadcast_to(local_square, (owners, 8, 128)).reshape(-1, 128), OWN)
    square_total = jnp.sum(squares.reshape(owners, 8, 128)[:, 0, 0])
    clip_factor = jnp.minimum(
        1.0, jnp.sqrt(5.0 * model_width * model_width / (square_total + norm_eps))
    )
    new_moment_in, new_square_in, update_in = adam_parts(grad_in, moment_in, square_in, clip_factor)
    new_moment_out, new_square_out, update_out = adam_parts(
        grad_out, moment_out, square_out, clip_factor
    )
    return (
        trust_step(weight_in, update_in),
        new_moment_in,
        new_square_in,
        trust_step(weight_out, update_out),
        new_moment_out,
        new_square_out,
    )


def solution(mesh):
    fine = Mesh(mesh.devices.reshape(8, 2, 4, 4), ("z", "c", "x", "y"))
    histories = ("z", "c", "x", "y")
    placed = (
        P(histories, None, None),
        P(histories, None, None),
        P(histories),
        P(),
        P(OWN, None),
        P(OWN, None),
        P(OWN, None),
        P(OWN, None),
        P(OWN, None),
        P(OWN, None),
    )
    return jax.shard_map(
        per_device,
        mesh=fine,
        in_specs=placed,
        out_specs=(P(OWN, None),) * 6,
        check_vma=False,
    )
```

```python
import functools

import jax
import jax.numpy as jnp
from jax import lax
from jax.experimental import pallas as pl
from jax.experimental.pallas import tpu as pltpu
from jax.sharding import Mesh
from jax.sharding import PartitionSpec as P

BLK = 256
HEAD_WIDTH = 256

norm_eps = 1e-06
beta_first = 0.9
beta_second = 0.95
learn_rate = 0.01
step_number = 10.0
update_eps = 1e-08
ratio_eps = 1e-06

OWN = ("x", "y")
SWAP = ((0, 1), (1, 0))

LINKS = (("x", 1), ("y", 1), ("x", 3), ("y", 3))
LINK_MASKS = (0b0100, 0b0001, 0b1100, 0b0011)


def rms_scale(values):
    return values * lax.rsqrt(jnp.mean(values * values, axis=-1, keepdims=True) + norm_eps)


def sigmoid(values):
    return 1.0 / (1.0 + jnp.exp(-values))


def allowed_mask(length):
    row = lax.broadcasted_iota(jnp.int32, (BLK, BLK), 0)
    col = lax.broadcasted_iota(jnp.int32, (BLK, BLK), 1)
    return ((col <= row) & (row < length)).astype(jnp.float32) * (1.0 / BLK)


def dot_nt(left, right):
    return lax.dot_general(
        left, right, (((1,), (1,)), ((), ())), preferred_element_type=jnp.float32
    )


def dot_tn(left, right):
    return lax.dot_general(
        left, right, (((0,), (0,)), ((), ())), preferred_element_type=jnp.float32
    )


def dot_nn(left, right):
    return jnp.dot(left, right, preferred_element_type=jnp.float32)


def silu_slope(values):
    sig = sigmoid(values)
    act = values * sig
    return act, sig + act * (1.0 - sig)


def relative_slot(mask, turn):
    x_far, x_near = (mask >> 3) & 1, ((mask >> 3) ^ (mask >> 2)) & 1
    y_far, y_near = (mask >> 1) & 1, ((mask >> 1) ^ mask) & 1
    bits = (x_near, y_near, x_far, y_far)
    slot = 0
    for step in range(4):
        slot = slot + (bits[(turn + step) % 4] << step)
    return slot


def owner_mask(slot, turn):
    mask = 0
    for step in range(4):
        if slot >> step & 1:
            mask ^= LINK_MASKS[(turn + step) % 4]
    return mask


def place_rows(turn, own, near, far, weight):
    count, rows, _ = near.shape
    for slot in range(2 * count):
        block = near[slot] if slot < count else far[slot - count]
        start = pl.multiple_of((own ^ owner_mask(slot, turn)) * rows, rows)
        weight[pl.ds(start, rows), :] = block


def project_kernel(turn, place, normed, near, far, projected, rest, weight):
    width = projected.shape[2]

    @pl.when(pl.program_id(0) == 0)
    def _():
        place_rows(turn, place[0], near, far, weight)
        rest[...] = weight[:, width:]

    projected[0] = dot_nn(normed[0], weight[:, :width])


def attention_kernel(
    turn, place, lengths, normed, near, far, queries_in, keys_in, values_out, scores, mixed, weight
):
    @pl.when(pl.program_id(0) == 0)
    def _():
        place_rows(turn, place[0], near, far, weight)

    proj = dot_nn(normed[0], weight[...])
    values_out[0] = proj
    allowed = allowed_mask(lengths[pl.program_id(0)])
    for head in range(proj.shape[1] // HEAD_WIDTH):
        part = slice(head * HEAD_WIDTH, (head + 1) * HEAD_WIDTH)
        values, queries, key_part = (
            (block * sigmoid(block)).astype(jnp.bfloat16)
            for block in (proj[:, part], queries_in[0, :, part], keys_in[0, :, part])
        )
        score = dot_nt(queries, key_part) * HEAD_WIDTH ** (-0.5)
        scores[0, head] = score
        attention = (score * sigmoid(score) * allowed).astype(jnp.bfloat16)
        mixed[0, :, part] = dot_nn(attention, values)


def gating_kernel(
    turn, place, normed, near, far, masked, keep, recv, mixed, gating_out, grad_gated, stats, weight
):
    width = keep.shape[0]

    @pl.when(pl.program_id(0) == 0)
    def _():
        place_rows(turn, place[0], near, far, weight)

    proj = dot_nn(normed[0], weight[...])
    gating_out[0] = proj
    core = place[1]
    mine = masked[0, :, pl.ds(pl.multiple_of(core * width, width), width)]
    others = masked[0, :, pl.ds(pl.multiple_of((1 - core) * width, width), width)]
    grad = (dot_nt(mine, keep[...]) + dot_nt(others, recv[...])).astype(jnp.bfloat16)
    grad_gated[0] = grad
    mix = mixed[0]
    square = jnp.sum(mix * mix, axis=1, keepdims=True)
    cross = jnp.sum(
        grad.astype(jnp.float32) * (proj * sigmoid(proj)) * mix, axis=1, keepdims=True
    )
    lane = lax.broadcasted_iota(jnp.int32, (BLK, 128), 1)
    stats[0] = jnp.where(lane == 0, square, cross)


def norm_back_kernel(
    projected, mixed, grad_gated, stats, stats_other, gated, grad_gating, grad_mixed
):
    model_width = 2 * mixed.shape[2]
    total = stats[0] + stats_other[0]
    inv = lax.rsqrt(total[:, 0:1] / model_width + norm_eps)
    back = inv * inv * inv * (total[:, 1:2] / model_width)
    gating, slope = silu_slope(projected[0])
    mix = mixed[0]
    grad = grad_gated[0].astype(jnp.float32)
    scaled = mix * inv
    gated[0] = (scaled * gating).astype(jnp.bfloat16)
    grad_gating[0] = (grad * scaled * slope).astype(jnp.bfloat16)
    grad_mixed[0] = (inv * (grad * gating) - mix * back).astype(jnp.bfloat16)


def attention_back_kernel(
    lengths, values_in, queries_in, keys_in, scores, grad_mixed, grad_values, grad_queries, grad_keys
):
    allowed = allowed_mask(lengths[pl.program_id(0)])
    for head in range(grad_mixed.shape[2] // HEAD_WIDTH):
        part = slice(head * HEAD_WIDTH, (head + 1) * HEAD_WIDTH)
        values, values_slope = silu_slope(values_in[0, :, part])
        queries, queries_slope = silu_slope(queries_in[0, :, part])
        key_part, keys_slope = silu_slope(keys_in[0, :, part])
        act, slope = silu_slope(scores[0, head])
        attention = (act * allowed).astype(jnp.bfloat16)
        grad_head = grad_mixed[0, :, part]
        grad_att = dot_nt(grad_head, values.astype(jnp.bfloat16)).astype(jnp.bfloat16)
        grad_score = (
            grad_att.astype(jnp.float32) * allowed * slope * HEAD_WIDTH ** (-0.5)
        ).astype(jnp.bfloat16)
        for out, grad, side in (
            (grad_values, dot_tn(attention, grad_head), values_slope),
            (grad_queries, dot_nn(grad_score, key_part.astype(jnp.bfloat16)), queries_slope),
            (grad_keys, dot_tn(grad_score, queries.astype(jnp.bfloat16)), keys_slope),
        ):
            held = grad.astype(jnp.bfloat16).astype(jnp.float32)
            out[0, :, part] = (held * side).astype(jnp.bfloat16)


def store_slot(slot, value, columns, near, far):
    count = near.shape[0]

    @pl.when(slot < count)
    def _():
        near[jnp.minimum(slot, count - 1), :, columns] = value

    @pl.when(slot >= count)
    def _():
        far[jnp.maximum(slot - count, 0), :, columns] = value


def term_kernel(turn, place, normed_t, grads, *refs):
    near, far = refs[-2:]
    rows, width = near.shape[1], grads.shape[1]
    term = dot_nn(normed_t[...], grads[...]).astype(jnp.bfloat16)
    step = pl.program_id(0)
    per_step = term.shape[0] // rows
    for block in range(per_step):
        slot = relative_slot((step * per_step + block) ^ place[0], turn)
        store_slot(slot, term[block * rows : (block + 1) * rows], slice(0, width), near, far)
    if len(refs) == 4:
        half = refs[0].shape[0] // rows
        per_step = half // pl.num_programs(0)
        for side, held in ((place[1], refs[0]), (1 - place[1], refs[1])):
            for block in range(per_step):
                at = step * per_step + block
                value = held[pl.ds(pl.multiple_of(at * rows, rows), rows), :]
                slot = relative_slot((side * half + at) ^ place[0], turn)
                store_slot(slot, value, slice(width, width + value.shape[1]), near, far)


def term_out_kernel(place, gated, masked, term):
    term[0] = dot_tn(gated[...], masked[...]).astype(jnp.bfloat16)


def rows_of(*dims):
    return pl.BlockSpec((1, *dims), lambda i, *_: (i,) + (0,) * len(dims))


def whole(*dims):
    return pl.BlockSpec(dims, lambda i, *_: (0,) * len(dims))


def call(kernel, name, grid, prefetch, in_specs, out, inputs, scratch=(), flops=0):
    moved = sum(v.size * v.dtype.itemsize for v in inputs)
    return pl.pallas_call(
        kernel,
        grid_spec=pltpu.PrefetchScalarGridSpec(
            num_scalar_prefetch=len(prefetch),
            grid=grid,
            in_specs=in_specs,
            out_specs=[spec for spec, _, _ in out],
            scratch_shapes=list(scratch),
        ),
        out_shape=[jax.ShapeDtypeStruct(shape, dtype) for _, shape, dtype in out],
        compiler_params=pltpu.CompilerParams(vmem_limit_bytes=20 * 1024 * 1024),
        cost_estimate=pl.CostEstimate(flops=1, bytes_accessed=1, transcendentals=0),
        name=name,
    )(*prefetch, *inputs)


def project(turn, place, normed, near, far, width):
    count, rows, depth = normed.shape
    columns = near.shape[2]
    return call(
        functools.partial(project_kernel, turn),
        "project",
        (count,),
        (place,),
        [rows_of(rows, depth), whole(*near.shape), whole(*far.shape)],
        [
            (rows_of(rows, width), (count, rows, width), jnp.float32),
            (whole(depth, columns - width), (depth, columns - width), jnp.bfloat16),
        ],
        (normed, near, far),
        [pltpu.VMEM((depth, columns), jnp.bfloat16)],
        2 * count * rows * depth * width,
    )


def attention_forward(turn, place, lengths, normed, near, far, queries, keys_in):
    count, rows, depth = normed.shape
    width = near.shape[2]
    heads = width // HEAD_WIDTH
    return call(
        functools.partial(attention_kernel, turn),
        "attention_forward",
        (count,),
        (place, lengths),
        [rows_of(rows, depth), whole(*near.shape), whole(*far.shape)] + [rows_of(rows, width)] * 2,
        [
            (rows_of(rows, width), (count, rows, width), jnp.float32),
            (rows_of(heads, rows, rows), (count, heads, rows, rows), jnp.float32),
            (rows_of(rows, width), (count, rows, width), jnp.float32),
        ],
        (normed, near, far, queries, keys_in),
        [pltpu.VMEM((depth, width), jnp.bfloat16)],
        3 * count * rows * depth * width,
    )


def gating_forward(turn, place, normed, near, far, masked, keep, recv, mixed):
    count, rows, depth = normed.shape
    width = near.shape[2]
    return call(
        functools.partial(gating_kernel, turn),
        "gating_forward",
        (count,),
        (place,),
        [
            rows_of(rows, depth),
            whole(*near.shape),
            whole(*far.shape),
            rows_of(rows, depth),
            whole(*keep.shape),
            whole(*recv.shape),
            rows_of(rows, width),
        ],
        [
            (rows_of(rows, width), (count, rows, width), jnp.float32),
            (rows_of(rows, width), (count, rows, width), jnp.bfloat16),
            (rows_of(rows, 128), (count, rows, 128), jnp.float32),
        ],
        (normed, near, far, masked, keep, recv, mixed),
        [pltpu.VMEM((depth, width), jnp.bfloat16)],
        4 * count * rows * depth * width,
    )


def norm_back(projected, mixed, grad_gated, stats, stats_other):
    count, rows, width = projected.shape
    block = rows_of(rows, width)
    return call(
        norm_back_kernel,
        "norm_back",
        (count,),
        (),
        [
            block,
            block,
            block,
            rows_of(rows, 128),
            pl.BlockSpec((1, rows, 128), lambda i, *_: ((i + count // 2) % count, 0, 0)),
        ],
        [(block, projected.shape, jnp.bfloat16)] * 3,
        (projected, mixed, grad_gated, stats, stats_other),
    )


def attention_back(lengths, values, queries, keys_in, scores, grad_mixed):
    count, rows, width = values.shape
    heads = width // HEAD_WIDTH
    block = rows_of(rows, width)
    return call(
        attention_back_kernel,
        "attention_back",
        (count,),
        (lengths,),
        [block, block, block, rows_of(heads, rows, rows), block],
        [(block, values.shape, jnp.bfloat16)] * 3,
        (values, queries, keys_in, scores, grad_mixed),
        flops=8 * count * rows * rows * width,
    )


def term(turn, place, owned, normed_t, grads, extra=None):
    depth, rows = normed_t.shape
    width = grads.shape[1]
    steps = 4
    owners = depth // owned
    columns = width
    in_specs = [
        pl.BlockSpec((depth // steps, rows), lambda i, *_: (i, 0)),
        whole(rows, width),
    ]
    inputs = [normed_t, grads]
    if extra is not None:
        keep, recv, at = extra
        share = keep.shape[1] // 2
        columns += share
        in_specs += [pl.BlockSpec((keep.shape[0], share), lambda i, *_: (0, at))] * 2
        inputs += [keep, recv]
    shape = (owners // 2, owned, columns)
    return call(
        functools.partial(term_kernel, turn),
        "term",
        (steps,),
        (place,),
        in_specs,
        [(whole(*shape), shape, jnp.bfloat16)] * 2,
        inputs,
        flops=2 * depth * rows * width,
    )


def term_out(place, gated, masked):
    rows, width = gated.shape
    return call(
        term_out_kernel,
        "term_out",
        (2,),
        (place,),
        [whole(rows, width), pl.BlockSpec((rows, width), lambda i, s: (0, (i + s[1]) % 2))],
        [(rows_of(width, width), (2, width, width), jnp.bfloat16)],
        (gated, masked),
        flops=4 * rows * width * width,
    )[0]


def sum_squares(values):
    values = values.astype(jnp.float32)
    return jnp.sum(values * values)


def update_kernel(place, squares, mine, other, *refs):
    half = mine.shape[1] // 5
    model_width = 2 * half
    first = place[1] == 0
    owners = squares.shape[0] // 8
    total = sum(squares[8 * i : 8 * i + 1, 0:1] for i in range(owners))
    clip = jnp.minimum(1.0, jnp.sqrt(5.0 * model_width * model_width / (total + norm_eps)))
    for parts, (weight, moment, square, new_weight, new_moment, new_square) in (
        (range(4), (refs[0], refs[1], refs[2], refs[6], refs[7], refs[8])),
        (range(4, 5), (refs[3], refs[4], refs[5], refs[9], refs[10], refs[11])),
    ):
        update_sq = weight_sq = 0.0
        for part in parts:
            at = slice(part * half, (part + 1) * half)
            both = (mine[:, at].astype(jnp.float32), other[:, at].astype(jnp.float32))
            for core in (0, 1):
                grad = jnp.where(first, both[core], both[1 - core]) * clip
                start = (part - parts[0]) * model_width + core * half
                col = slice(start, start + half)
                held = beta_first * moment[:, col] + (1.0 - beta_first) * grad
                held_sq = beta_second * square[:, col] + (1.0 - beta_second) * grad * grad
                new_moment[:, col] = held
                new_square[:, col] = held_sq
                update = (held * (1.0 / (1.0 - beta_first**step_number))) / (
                    jnp.sqrt(held_sq * (1.0 / (1.0 - beta_second**step_number))) + update_eps
                )
                new_weight[:, col] = update
                update_sq += jnp.sum(update * update, axis=1, keepdims=True)
                held = weight[:, col].astype(jnp.float32)
                weight_sq += jnp.sum(held * held, axis=1, keepdims=True)
        ratio = learn_rate * jnp.sqrt(weight_sq) / (jnp.sqrt(update_sq) + ratio_eps)
        new_weight[...] = weight[...].astype(jnp.float32) - ratio * new_weight[...]


def update_rows(place, squares, mine, other, *state):
    rows = 16
    count = mine.shape[0] // rows

    def block(value):
        return pl.BlockSpec((rows, value.shape[1]), lambda i, *_: (i, 0))

    return call(
        update_kernel,
        "update_rows",
        (count,),
        (place,),
        [whole(*squares.shape)] + [block(v) for v in (mine, other, *state)],
        [(block(v), v.shape, jnp.float32) for v in state],
        (squares, mine, other, *state),
    )


def swap_cores(values):
    return lax.ppermute(values, "c", SWAP)


def over_link(values, link):
    axis, mask = LINKS[link % 4]
    return lax.ppermute(values, axis, [(i, i ^ mask) for i in range(4)])


def gather_parts(parts):
    held = [part[None] for part in parts]
    for step in range(3):
        got = [over_link(part, turn + step) for turn, part in enumerate(held)]
        held = [jnp.concatenate(pair, axis=0) for pair in zip(held, got)]
    return [(part, over_link(part, turn + 3)) for turn, part in enumerate(held)]


def add_halves(mine, got):
    return (mine.astype(jnp.float32) + got.astype(jnp.float32)).astype(jnp.bfloat16)


def scatter_parts(pairs):
    for step in (3, 2, 1, 0):
        got = [over_link(far, turn + step) for turn, (_, far) in enumerate(pairs)]
        mine, got = lax.optimization_barrier(([near for near, _ in pairs], got))
        held = [add_halves(*pair) for pair in zip(mine, got)]
        if step:
            pairs = [jnp.split(part, 2, axis=0) for part in held]
    return [part[0] for part in held]


def after(value, done):
    return lax.optimization_barrier((value, done))[0]


def exchange(blocks, axes):
    return lax.all_to_all(blocks, axes, 0, 0, tiled=True)


def per_device(
    tokens,
    cotangent,
    lengths,
    norm_gain,
    weight_in,
    weight_out,
    moment_in,
    square_in,
    moment_out,
    square_out,
):
    slots, rows, model_width = tokens.shape
    half = model_width // 2
    quarter = half // 2
    core = lax.axis_index("c")
    own = lax.axis_index(OWN)
    owners = lax.axis_size(OWN)
    planes = lax.axis_size("z")
    owned = weight_in.shape[0]
    place = jnp.stack([own, core]).astype(jnp.int32)

    mine = [
        lax.dynamic_slice_in_dim(weight_in, part * model_width + core * half, half, axis=1)
        for part in range(4)
    ]
    mine_out = lax.dynamic_slice_in_dim(weight_out, core * half, half, axis=1)
    (q_near, q_far), (k_near, k_far), (v_near, v_far), (g_near, g_far) = gather_parts(
        [
            jnp.concatenate([mine[2], mine_out[:, :quarter]], axis=1),
            jnp.concatenate([mine[3], mine_out[:, quarter:]], axis=1),
            mine[1],
            mine[0],
        ]
    )

    normed = (rms_scale(tokens.astype(jnp.float32)) * norm_gain).astype(jnp.bfloat16)
    row_index = jnp.arange(rows, dtype=jnp.int32)
    live = row_index[None, :] < lengths[:, None]
    masked = jnp.where(live[:, :, None], cotangent, jnp.zeros_like(cotangent))
    normed = jnp.concatenate([normed, swap_cores(normed)], axis=0)
    masked = jnp.concatenate([masked, swap_cores(masked)], axis=0)
    lengths = jnp.concatenate([lengths, swap_cores(lengths)], axis=0)
    normed, masked, normed_t = lax.optimization_barrier(
        (normed, masked, normed.reshape(-1, model_width).T)
    )

    queries, out_first = project(0, place, normed, q_near, q_far, half)
    keys_in, out_second = project(1, place, normed, k_near, k_far, half)
    out_cols = jnp.concatenate([out_first, out_second], axis=1).reshape(2, half, half)
    keep = lax.dynamic_index_in_dim(out_cols, core, axis=0, keepdims=False)
    recv = swap_cores(lax.dynamic_index_in_dim(out_cols, 1 - core, axis=0, keepdims=False))
    values, scores, mixed = attention_forward(
        2, place, lengths, normed, v_near, v_far, queries, keys_in
    )
    gating, grad_gated, stats = gating_forward(
        3, place, normed, g_near, g_far, masked, keep, recv, mixed
    )
    gated, grad_gating, grad_mixed = norm_back(
        gating, mixed, grad_gated, stats, swap_cores(stats)
    )

    def flat(part):
        return part.reshape(-1, part.shape[2])

    term_g = term(0, place, owned, normed_t, flat(grad_gating))
    grad_mixed = after(grad_mixed, term_g)
    outer = term_out(place, flat(gated), flat(masked))
    outer_recv = swap_cores(outer[1])
    grad_values, grad_queries, grad_keys = attention_back(
        lengths, values, queries, keys_in, scores, grad_mixed
    )
    term_v = term(1, place, owned, normed_t, flat(grad_values), (outer[0], outer_recv, 0))
    grad_queries = after(grad_queries, term_v)
    term_q = term(2, place, owned, normed_t, flat(grad_queries), (outer[0], outer_recv, 1))
    grad_keys = after(grad_keys, term_q)
    term_k = term(3, place, owned, normed_t, flat(grad_keys))
    part_g, part_v, part_q, part_k = scatter_parts([term_g, term_v, term_q, term_k])
    part = jnp.concatenate(
        [part_g, part_v[:, :half], part_q[:, :half], part_k, part_v[:, half:], part_q[:, half:]],
        axis=1,
    )

    piece = jnp.sum(
        exchange(part, "z").reshape(planes, owned // planes, -1).astype(jnp.float32), axis=0
    ).astype(jnp.bfloat16)
    shard = exchange(
        jnp.broadcast_to(piece[None], (planes, *piece.shape)).reshape(owned, -1), "z"
    )
    other = swap_cores(shard)
    local_square = sum_squares(shard) + sum_squares(other)
    squares = exchange(jnp.broadcast_to(local_square, (owners * 8, 128)), OWN)
    return update_rows(
        place,
        squares,
        shard,
        other,
        weight_in,
        moment_in,
        square_in,
        weight_out,
        moment_out,
        square_out,
    )


def solution(mesh):
    fine = Mesh(mesh.devices.reshape(8, 2, 4, 4), ("z", "c", "x", "y"))
    histories = ("z", "c", "x", "y")
    placed = (
        P(histories, None, None),
        P(histories, None, None),
        P(histories),
        P(),
        P(OWN, None),
        P(OWN, None),
        P(OWN, None),
        P(OWN, None),
        P(OWN, None),
        P(OWN, None),
    )
    return jax.shard_map(
        per_device,
        mesh=fine,
        in_specs=placed,
        out_specs=(P(OWN, None),) * 6,
        check_vma=False,
    )
```

```python
import functools

import jax
import jax.numpy as jnp
from jax import lax
from jax.experimental import pallas as pl
from jax.experimental.pallas import tpu as pltpu
from jax.sharding import Mesh
from jax.sharding import PartitionSpec as P

BLK = 256
HEAD_WIDTH = 256

norm_eps = 1e-06
beta_first = 0.9
beta_second = 0.95
learn_rate = 0.01
step_number = 10.0
update_eps = 1e-08
ratio_eps = 1e-06

OWN = ("x", "y")
SWAP = ((0, 1), (1, 0))

DIRECT = ("x", "y", "x", "y")
STEPS = ((("y", 1), ("y", 3)), (("x", 1), ("x", 3)), (("y", 3), ("y", 1)), (("x", 3), ("x", 1)))


def rms_scale(values):
    return values * lax.rsqrt(jnp.mean(values * values, axis=-1, keepdims=True) + norm_eps)


def sigmoid(values):
    return 1.0 / (1.0 + jnp.exp(-values))


def allowed_mask(length):
    row = lax.broadcasted_iota(jnp.int32, (BLK, BLK), 0)
    col = lax.broadcasted_iota(jnp.int32, (BLK, BLK), 1)
    return ((col <= row) & (row < length)).astype(jnp.float32) * (1.0 / BLK)


def dot_nt(left, right):
    return lax.dot_general(
        left, right, (((1,), (1,)), ((), ())), preferred_element_type=jnp.float32
    )


def dot_tn(left, right):
    return lax.dot_general(
        left, right, (((0,), (0,)), ((), ())), preferred_element_type=jnp.float32
    )


def dot_nn(left, right):
    return jnp.dot(left, right, preferred_element_type=jnp.float32)


def silu_slope(values):
    sig = sigmoid(values)
    act = values * sig
    return act, sig + act * (1.0 - sig)


def relative_slot(mask, turn):
    direct, other = (mask >> 2, mask & 3) if turn % 2 == 0 else (mask & 3, mask >> 2)
    high, odd = other >> 1, (other >> 1) ^ (other & 1)
    first, second = (odd, high) if turn < 2 else (high, odd)
    return direct + 4 * first + 8 * second


def owner_mask(slot, turn):
    return next(mask for mask in range(16) if relative_slot(mask, turn) == slot)


def place_rows(turn, own, near, far, weight):
    count, rows, _ = near.shape
    for slot in range(2 * count):
        block = near[slot] if slot < count else far[slot - count]
        start = pl.multiple_of((own ^ owner_mask(slot, turn)) * rows, rows)
        weight[pl.ds(start, rows), :] = block


def project_kernel(turn, place, normed, near, far, projected, rest, weight):
    width = projected.shape[2]

    @pl.when(pl.program_id(0) == 0)
    def _():
        place_rows(turn, place[0], near, far, weight)
        rest[...] = weight[:, width:]

    projected[0] = dot_nn(normed[0], weight[:, :width])


def attention_kernel(
    turn, place, lengths, normed, near, far, queries_in, keys_in, values_out, scores, mixed, weight
):
    @pl.when(pl.program_id(0) == 0)
    def _():
        place_rows(turn, place[0], near, far, weight)

    proj = dot_nn(normed[0], weight[...])
    values_out[0] = proj
    allowed = allowed_mask(lengths[pl.program_id(0)])
    for head in range(proj.shape[1] // HEAD_WIDTH):
        part = slice(head * HEAD_WIDTH, (head + 1) * HEAD_WIDTH)
        values, queries, key_part = (
            (block * sigmoid(block)).astype(jnp.bfloat16)
            for block in (proj[:, part], queries_in[0, :, part], keys_in[0, :, part])
        )
        score = dot_nt(queries, key_part) * HEAD_WIDTH ** (-0.5)
        scores[0, head] = score
        attention = (score * sigmoid(score) * allowed).astype(jnp.bfloat16)
        mixed[0, :, part] = dot_nn(attention, values)


def gating_kernel(
    turn, place, normed, near, far, masked, keep, recv, mixed, gating_out, grad_gated, stats, weight
):
    width = keep.shape[0]

    @pl.when(pl.program_id(0) == 0)
    def _():
        place_rows(turn, place[0], near, far, weight)

    proj = dot_nn(normed[0], weight[...])
    gating_out[0] = proj
    core = place[1]
    mine = masked[0, :, pl.ds(pl.multiple_of(core * width, width), width)]
    others = masked[0, :, pl.ds(pl.multiple_of((1 - core) * width, width), width)]
    grad = (dot_nt(mine, keep[...]) + dot_nt(others, recv[...])).astype(jnp.bfloat16)
    grad_gated[0] = grad
    mix = mixed[0]
    square = jnp.sum(mix * mix, axis=1, keepdims=True)
    cross = jnp.sum(
        grad.astype(jnp.float32) * (proj * sigmoid(proj)) * mix, axis=1, keepdims=True
    )
    lane = lax.broadcasted_iota(jnp.int32, (BLK, 128), 1)
    stats[0] = jnp.where(lane == 0, square, cross)


def norm_back_kernel(
    projected, mixed, grad_gated, stats, stats_other, gated, grad_gating, grad_mixed
):
    model_width = 2 * mixed.shape[2]
    total = stats[0] + stats_other[0]
    inv = lax.rsqrt(total[:, 0:1] / model_width + norm_eps)
    back = inv * inv * inv * (total[:, 1:2] / model_width)
    gating, slope = silu_slope(projected[0])
    mix = mixed[0]
    grad = grad_gated[0].astype(jnp.float32)
    scaled = mix * inv
    gated[0] = (scaled * gating).astype(jnp.bfloat16)
    grad_gating[0] = (grad * scaled * slope).astype(jnp.bfloat16)
    grad_mixed[0] = (inv * (grad * gating) - mix * back).astype(jnp.bfloat16)


def attention_back_kernel(
    lengths, values_in, queries_in, keys_in, scores, grad_mixed, grad_values, grad_queries, grad_keys
):
    allowed = allowed_mask(lengths[pl.program_id(0)])
    for head in range(grad_mixed.shape[2] // HEAD_WIDTH):
        part = slice(head * HEAD_WIDTH, (head + 1) * HEAD_WIDTH)
        values, values_slope = silu_slope(values_in[0, :, part])
        queries, queries_slope = silu_slope(queries_in[0, :, part])
        key_part, keys_slope = silu_slope(keys_in[0, :, part])
        act, slope = silu_slope(scores[0, head])
        attention = (act * allowed).astype(jnp.bfloat16)
        grad_head = grad_mixed[0, :, part]
        grad_att = dot_nt(grad_head, values.astype(jnp.bfloat16)).astype(jnp.bfloat16)
        grad_score = (
            grad_att.astype(jnp.float32) * allowed * slope * HEAD_WIDTH ** (-0.5)
        ).astype(jnp.bfloat16)
        for out, grad, side in (
            (grad_values, dot_tn(attention, grad_head), values_slope),
            (grad_queries, dot_nn(grad_score, key_part.astype(jnp.bfloat16)), queries_slope),
            (grad_keys, dot_tn(grad_score, queries.astype(jnp.bfloat16)), keys_slope),
        ):
            held = grad.astype(jnp.bfloat16).astype(jnp.float32)
            out[0, :, part] = (held * side).astype(jnp.bfloat16)


def store_slot(slot, value, columns, near, far):
    count = near.shape[0]

    @pl.when(slot < count)
    def _():
        near[jnp.minimum(slot, count - 1), :, columns] = value

    @pl.when(slot >= count)
    def _():
        far[jnp.maximum(slot - count, 0), :, columns] = value


def term_kernel(turn, place, normed_t, grads, *refs):
    near, far = refs[-2:]
    rows, width = near.shape[1], grads.shape[1]
    term = dot_nn(normed_t[...], grads[...]).astype(jnp.bfloat16)
    step = pl.program_id(0)
    per_step = term.shape[0] // rows
    for block in range(per_step):
        slot = relative_slot((step * per_step + block) ^ place[0], turn)
        store_slot(slot, term[block * rows : (block + 1) * rows], slice(0, width), near, far)
    if len(refs) == 4:
        half = refs[0].shape[0] // rows
        per_step = half // pl.num_programs(0)
        for side, held in ((place[1], refs[0]), (1 - place[1], refs[1])):
            for block in range(per_step):
                at = step * per_step + block
                value = held[pl.ds(pl.multiple_of(at * rows, rows), rows), :]
                slot = relative_slot((side * half + at) ^ place[0], turn)
                store_slot(slot, value, slice(width, width + value.shape[1]), near, far)


def term_out_kernel(place, gated, masked, term):
    term[0] = dot_tn(gated[...], masked[...]).astype(jnp.bfloat16)


def rows_of(*dims):
    return pl.BlockSpec((1, *dims), lambda i, *_: (i,) + (0,) * len(dims))


def whole(*dims):
    return pl.BlockSpec(dims, lambda i, *_: (0,) * len(dims))


def call(kernel, name, grid, prefetch, in_specs, out, inputs, scratch=(), flops=0):
    moved = sum(v.size * v.dtype.itemsize for v in inputs)
    return pl.pallas_call(
        kernel,
        grid_spec=pltpu.PrefetchScalarGridSpec(
            num_scalar_prefetch=len(prefetch),
            grid=grid,
            in_specs=in_specs,
            out_specs=[spec for spec, _, _ in out],
            scratch_shapes=list(scratch),
        ),
        out_shape=[jax.ShapeDtypeStruct(shape, dtype) for _, shape, dtype in out],
        compiler_params=pltpu.CompilerParams(vmem_limit_bytes=20 * 1024 * 1024),
        cost_estimate=pl.CostEstimate(flops=1, bytes_accessed=1, transcendentals=0),
        name=name,
    )(*prefetch, *inputs)


def project(turn, place, normed, near, far, width):
    count, rows, depth = normed.shape
    columns = near.shape[2]
    return call(
        functools.partial(project_kernel, turn),
        "project",
        (count,),
        (place,),
        [rows_of(rows, depth), whole(*near.shape), whole(*far.shape)],
        [
            (rows_of(rows, width), (count, rows, width), jnp.float32),
            (whole(depth, columns - width), (depth, columns - width), jnp.bfloat16),
        ],
        (normed, near, far),
        [pltpu.VMEM((depth, columns), jnp.bfloat16)],
        2 * count * rows * depth * width,
    )


def attention_forward(turn, place, lengths, normed, near, far, queries, keys_in):
    count, rows, depth = normed.shape
    width = near.shape[2]
    heads = width // HEAD_WIDTH
    return call(
        functools.partial(attention_kernel, turn),
        "attention_forward",
        (count,),
        (place, lengths),
        [rows_of(rows, depth), whole(*near.shape), whole(*far.shape)] + [rows_of(rows, width)] * 2,
        [
            (rows_of(rows, width), (count, rows, width), jnp.float32),
            (rows_of(heads, rows, rows), (count, heads, rows, rows), jnp.float32),
            (rows_of(rows, width), (count, rows, width), jnp.float32),
        ],
        (normed, near, far, queries, keys_in),
        [pltpu.VMEM((depth, width), jnp.bfloat16)],
        3 * count * rows * depth * width,
    )


def gating_forward(turn, place, normed, near, far, masked, keep, recv, mixed):
    count, rows, depth = normed.shape
    width = near.shape[2]
    return call(
        functools.partial(gating_kernel, turn),
        "gating_forward",
        (count,),
        (place,),
        [
            rows_of(rows, depth),
            whole(*near.shape),
            whole(*far.shape),
            rows_of(rows, depth),
            whole(*keep.shape),
            whole(*recv.shape),
            rows_of(rows, width),
        ],
        [
            (rows_of(rows, width), (count, rows, width), jnp.float32),
            (rows_of(rows, width), (count, rows, width), jnp.bfloat16),
            (rows_of(rows, 128), (count, rows, 128), jnp.float32),
        ],
        (normed, near, far, masked, keep, recv, mixed),
        [pltpu.VMEM((depth, width), jnp.bfloat16)],
        4 * count * rows * depth * width,
    )


def norm_back(projected, mixed, grad_gated, stats, stats_other):
    count, rows, width = projected.shape
    block = rows_of(rows, width)
    return call(
        norm_back_kernel,
        "norm_back",
        (count,),
        (),
        [
            block,
            block,
            block,
            rows_of(rows, 128),
            pl.BlockSpec((1, rows, 128), lambda i, *_: ((i + count // 2) % count, 0, 0)),
        ],
        [(block, projected.shape, jnp.bfloat16)] * 3,
        (projected, mixed, grad_gated, stats, stats_other),
    )


def attention_back(lengths, values, queries, keys_in, scores, grad_mixed):
    count, rows, width = values.shape
    heads = width // HEAD_WIDTH
    block = rows_of(rows, width)
    return call(
        attention_back_kernel,
        "attention_back",
        (count,),
        (lengths,),
        [block, block, block, rows_of(heads, rows, rows), block],
        [(block, values.shape, jnp.bfloat16)] * 3,
        (values, queries, keys_in, scores, grad_mixed),
        flops=8 * count * rows * rows * width,
    )


def term(turn, place, owned, normed_t, grads, extra=None):
    depth, rows = normed_t.shape
    width = grads.shape[1]
    steps = 4
    owners = depth // owned
    columns = width
    in_specs = [
        pl.BlockSpec((depth // steps, rows), lambda i, *_: (i, 0)),
        whole(rows, width),
    ]
    inputs = [normed_t, grads]
    if extra is not None:
        keep, recv, at = extra
        share = keep.shape[1] // 2
        columns += share
        in_specs += [pl.BlockSpec((keep.shape[0], share), lambda i, *_: (0, at))] * 2
        inputs += [keep, recv]
    shape = (owners // 2, owned, columns)
    return call(
        functools.partial(term_kernel, turn),
        "term",
        (steps,),
        (place,),
        in_specs,
        [(whole(*shape), shape, jnp.bfloat16)] * 2,
        inputs,
        flops=2 * depth * rows * width,
    )


def term_out(place, gated, masked):
    rows, width = gated.shape
    return call(
        term_out_kernel,
        "term_out",
        (2,),
        (place,),
        [whole(rows, width), pl.BlockSpec((rows, width), lambda i, s: (0, (i + s[1]) % 2))],
        [(rows_of(width, width), (2, width, width), jnp.bfloat16)],
        (gated, masked),
        flops=4 * rows * width * width,
    )[0]


def sum_squares(values):
    values = values.astype(jnp.float32)
    return jnp.sum(values * values)


def update_kernel(place, squares, mine, other, *refs):
    half = mine.shape[1] // 5
    model_width = 2 * half
    first = place[1] == 0
    owners = squares.shape[0] // 8
    total = sum(squares[8 * i : 8 * i + 1, 0:1] for i in range(owners))
    clip = jnp.minimum(1.0, jnp.sqrt(5.0 * model_width * model_width / (total + norm_eps)))
    for parts, (weight, moment, square, new_weight, new_moment, new_square) in (
        (range(4), (refs[0], refs[1], refs[2], refs[6], refs[7], refs[8])),
        (range(4, 5), (refs[3], refs[4], refs[5], refs[9], refs[10], refs[11])),
    ):
        update_sq = weight_sq = 0.0
        for part in parts:
            at = slice(part * half, (part + 1) * half)
            both = (mine[:, at].astype(jnp.float32), other[:, at].astype(jnp.float32))
            for core in (0, 1):
                grad = jnp.where(first, both[core], both[1 - core]) * clip
                start = (part - parts[0]) * model_width + core * half
                col = slice(start, start + half)
                held = beta_first * moment[:, col] + (1.0 - beta_first) * grad
                held_sq = beta_second * square[:, col] + (1.0 - beta_second) * grad * grad
                new_moment[:, col] = held
                new_square[:, col] = held_sq
                update = (held * (1.0 / (1.0 - beta_first**step_number))) / (
                    jnp.sqrt(held_sq * (1.0 / (1.0 - beta_second**step_number))) + update_eps
                )
                new_weight[:, col] = update
                update_sq += jnp.sum(update * update, axis=1, keepdims=True)
                held = weight[:, col].astype(jnp.float32)
                weight_sq += jnp.sum(held * held, axis=1, keepdims=True)
        ratio = learn_rate * jnp.sqrt(weight_sq) / (jnp.sqrt(update_sq) + ratio_eps)
        new_weight[...] = weight[...].astype(jnp.float32) - ratio * new_weight[...]


def update_rows(place, squares, mine, other, *state):
    rows = 16
    count = mine.shape[0] // rows

    def block(value):
        return pl.BlockSpec((rows, value.shape[1]), lambda i, *_: (i, 0))

    return call(
        update_kernel,
        "update_rows",
        (count,),
        (place,),
        [whole(*squares.shape)] + [block(v) for v in (mine, other, *state)],
        [(block(v), v.shape, jnp.float32) for v in state],
        (squares, mine, other, *state),
    )


def swap_cores(values):
    return lax.ppermute(values, "c", SWAP)


def over_link(values, axis, mask):
    return lax.ppermute(values, axis, [(i, i ^ mask) for i in range(4)])


def direct_round(blocks_of, groups):
    got = [[None] * 4, [None] * 4]
    for mask in (1, 3, 2):
        for group, axis in enumerate(("x", "y")):
            got[group][mask] = over_link(blocks_of(groups[group], mask), axis, mask)
    return got


def gather_parts(parts, beside):
    groups = [jnp.concatenate([parts[0], parts[2]], axis=1), jnp.concatenate([parts[1], parts[3]], axis=1)]
    got = direct_round(lambda group, mask: group, groups)
    for group, mine in zip(got, groups):
        group[0] = mine
    got = lax.optimization_barrier(got)
    held = []
    for turn in range(4):
        width = parts[turn % 2].shape[1]
        cut = slice(0, width) if turn < 2 else slice(width, None)
        held.append(jnp.stack([block[:, cut] for block in got[turn % 2]]))
    got = [over_link(part, *STEPS[turn][0]) for turn, part in enumerate(held)]
    held, got, beside = lax.optimization_barrier((held, got, beside))
    held = [jnp.concatenate(pair, axis=0) for pair in zip(held, got)]
    return [(part, over_link(part, *STEPS[turn][1])) for turn, part in enumerate(held)], beside


def add_blocks(*blocks):
    return sum(block.astype(jnp.float32) for block in blocks).astype(jnp.bfloat16)


def scatter_parts(pairs):
    for step in (1, 0):
        got = [over_link(far, *STEPS[turn][step]) for turn, (_, far) in enumerate(pairs)]
        mine, got = lax.optimization_barrier(([near for near, _ in pairs], got))
        held = [add_blocks(*pair) for pair in zip(mine, got)]
        if step:
            pairs = [jnp.split(part, 2, axis=0) for part in held]
    groups = [jnp.concatenate([held[0], held[2]], axis=2), jnp.concatenate([held[1], held[3]], axis=2)]
    got = direct_round(lambda group, mask: group[mask], groups)
    return [add_blocks(group[0], *blocks[1:]) for group, blocks in zip(groups, got)]


def after(value, done):
    return lax.optimization_barrier((value, done))[0]


def exchange(blocks, axes):
    return lax.all_to_all(blocks, axes, 0, 0, tiled=True)


def per_device(
    tokens,
    cotangent,
    lengths,
    norm_gain,
    weight_in,
    weight_out,
    moment_in,
    square_in,
    moment_out,
    square_out,
):
    slots, rows, model_width = tokens.shape
    half = model_width // 2
    quarter = half // 2
    core = lax.axis_index("c")
    own = lax.axis_index(OWN)
    owners = lax.axis_size(OWN)
    planes = lax.axis_size("z")
    owned = weight_in.shape[0]
    place = jnp.stack([own, core]).astype(jnp.int32)

    mine = [
        lax.dynamic_slice_in_dim(weight_in, part * model_width + core * half, half, axis=1)
        for part in range(4)
    ]
    mine_out = lax.dynamic_slice_in_dim(weight_out, core * half, half, axis=1)
    normed = (rms_scale(tokens.astype(jnp.float32)) * norm_gain).astype(jnp.bfloat16)
    row_index = jnp.arange(rows, dtype=jnp.int32)
    live = row_index[None, :] < lengths[:, None]
    masked = jnp.where(live[:, :, None], cotangent, jnp.zeros_like(cotangent))
    normed = jnp.concatenate([normed, swap_cores(normed)], axis=0)
    masked = jnp.concatenate([masked, swap_cores(masked)], axis=0)
    lengths = jnp.concatenate([lengths, swap_cores(lengths)], axis=0)
    normed_t = normed.reshape(-1, model_width).T
    parts, (normed, masked, lengths, normed_t) = gather_parts(
        [
            jnp.concatenate([mine[2], mine_out[:, :quarter]], axis=1),
            jnp.concatenate([mine[3], mine_out[:, quarter:]], axis=1),
            mine[1],
            mine[0],
        ],
        (normed, masked, lengths, normed_t),
    )
    (q_near, q_far), (k_near, k_far), (v_near, v_far), (g_near, g_far) = parts

    queries, out_first = project(0, place, normed, q_near, q_far, half)
    keys_in, out_second = project(1, place, normed, k_near, k_far, half)
    out_cols = jnp.concatenate([out_first, out_second], axis=1).reshape(2, half, half)
    keep = lax.dynamic_index_in_dim(out_cols, core, axis=0, keepdims=False)
    recv = swap_cores(lax.dynamic_index_in_dim(out_cols, 1 - core, axis=0, keepdims=False))
    values, scores, mixed = attention_forward(
        2, place, lengths, normed, v_near, v_far, queries, keys_in
    )
    gating, grad_gated, stats = gating_forward(
        3, place, normed, g_near, g_far, masked, keep, recv, mixed
    )
    gated, grad_gating, grad_mixed = norm_back(
        gating, mixed, grad_gated, stats, swap_cores(stats)
    )

    def flat(part):
        return part.reshape(-1, part.shape[2])

    term_g = term(0, place, owned, normed_t, flat(grad_gating))
    grad_mixed = after(grad_mixed, term_g)
    outer = term_out(place, flat(gated), flat(masked))
    outer_recv = swap_cores(outer[1])
    grad_values, grad_queries, grad_keys = attention_back(
        lengths, values, queries, keys_in, scores, grad_mixed
    )
    term_v = term(1, place, owned, normed_t, flat(grad_values), (outer[0], outer_recv, 0))
    grad_queries = after(grad_queries, term_v)
    term_q = term(2, place, owned, normed_t, flat(grad_queries), (outer[0], outer_recv, 1))
    grad_keys = after(grad_keys, term_q)
    term_k = term(3, place, owned, normed_t, flat(grad_keys))
    part_gq, part_vk = scatter_parts([term_g, term_v, term_q, term_k])
    wide = half + quarter
    part = jnp.concatenate(
        [
            part_gq[:, :half],
            part_vk[:, :half],
            part_gq[:, half : 2 * half],
            part_vk[:, wide:],
            part_vk[:, half:wide],
            part_gq[:, 2 * half :],
        ],
        axis=1,
    )

    piece = jnp.sum(
        exchange(part, "z").reshape(planes, owned // planes, -1).astype(jnp.float32), axis=0
    ).astype(jnp.bfloat16)
    shard = exchange(
        jnp.broadcast_to(piece[None], (planes, *piece.shape)).reshape(owned, -1), "z"
    )
    other = swap_cores(shard)
    local_square = sum_squares(shard) + sum_squares(other)
    squares = exchange(jnp.broadcast_to(local_square, (owners * 8, 128)), OWN)
    return update_rows(
        place,
        squares,
        shard,
        other,
        weight_in,
        moment_in,
        square_in,
        weight_out,
        moment_out,
        square_out,
    )


def solution(mesh):
    fine = Mesh(mesh.devices.reshape(8, 2, 4, 4), ("z", "c", "x", "y"))
    histories = ("z", "c", "x", "y")
    placed = (
        P(histories, None, None),
        P(histories, None, None),
        P(histories),
        P(),
        P(OWN, None),
        P(OWN, None),
        P(OWN, None),
        P(OWN, None),
        P(OWN, None),
        P(OWN, None),
    )
    return jax.shard_map(
        per_device,
        mesh=fine,
        in_specs=placed,
        out_specs=(P(OWN, None),) * 6,
        check_vma=False,
    )
```

```python
import functools

import jax
import jax.numpy as jnp
from jax import lax
from jax.experimental import pallas as pl
from jax.experimental.pallas import tpu as pltpu
from jax.sharding import Mesh
from jax.sharding import PartitionSpec as P

BLK = 256
HEAD_WIDTH = 256

norm_eps = 1e-06
beta_first = 0.9
beta_second = 0.95
learn_rate = 0.01
step_number = 10.0
update_eps = 1e-08
ratio_eps = 1e-06

OWN = ("x", "y")
SWAP = ((0, 1), (1, 0))

DIRECT = ("x", "y", "x", "y")
STEPS = ((("y", 1), ("y", 3)), (("x", 1), ("x", 3)), (("y", 3), ("y", 1)), (("x", 3), ("x", 1)))


def rms_scale(values):
    return values * lax.rsqrt(jnp.mean(values * values, axis=-1, keepdims=True) + norm_eps)


def sigmoid(values):
    return 1.0 / (1.0 + jnp.exp(-values))


def allowed_mask(length):
    row = lax.broadcasted_iota(jnp.int32, (BLK, BLK), 0)
    col = lax.broadcasted_iota(jnp.int32, (BLK, BLK), 1)
    return ((col <= row) & (row < length)).astype(jnp.float32) * (1.0 / BLK)


def dot_nt(left, right):
    return lax.dot_general(
        left, right, (((1,), (1,)), ((), ())), preferred_element_type=jnp.float32
    )


def dot_tn(left, right):
    return lax.dot_general(
        left, right, (((0,), (0,)), ((), ())), preferred_element_type=jnp.float32
    )


def dot_nn(left, right):
    return jnp.dot(left, right, preferred_element_type=jnp.float32)


def silu_slope(values):
    sig = sigmoid(values)
    act = values * sig
    return act, sig + act * (1.0 - sig)


def relative_slot(mask, turn):
    direct, other = (mask >> 2, mask & 3) if turn % 2 == 0 else (mask & 3, mask >> 2)
    high, odd = other >> 1, (other >> 1) ^ (other & 1)
    first, second = (odd, high) if turn < 2 else (high, odd)
    return direct + 4 * first + 8 * second


def owner_mask(slot, turn):
    return next(mask for mask in range(16) if relative_slot(mask, turn) == slot)


def gathered(held, forwarded, slot):
    count = held[0].shape[0]
    if slot < 3 * count:
        return held[slot // count][slot % count]
    return jnp.concatenate([part[slot % count] for part in forwarded], axis=1)


def place_rows(turn, own, rows, held, forwarded, store):
    for slot in range(16):
        start = pl.multiple_of((own ^ owner_mask(slot, turn)) * rows, rows)
        store(pl.ds(start, rows), gathered(held, forwarded, slot))


def forward_kernel(
    place,
    lengths,
    normed,
    a0,
    a1,
    a2,
    a_low,
    a_high,
    b0,
    b1,
    b2,
    b_low,
    b_high,
    projected,
    scores,
    mixed,
    outer,
    weight,
):
    width = mixed.shape[2]
    quarter = outer.shape[1] // 2

    @pl.when(pl.program_id(0) == 0)
    def _():
        rows = a0.shape[1]

        def store_a(at, block):
            weight[at, : 2 * width] = block[:, : 2 * width]
            outer[at, :quarter] = block[:, 2 * width :]

        def store_b(at, block):
            weight[at, 2 * width :] = block[:, :width]
            outer[at, quarter:] = block[:, 2 * width :]

        place_rows(0, place[0], rows, (a0, a1, a2), (a_low, a_high), store_a)
        place_rows(1, place[0], rows, (b0, b1, b2), (b_low, b_high), store_b)

    proj = dot_nn(normed[0], weight[...])
    projected[0] = proj
    held = (proj * sigmoid(proj)).astype(jnp.bfloat16)
    allowed = allowed_mask(lengths[pl.program_id(0)])
    for start in range(0, width, HEAD_WIDTH):
        queries, values, key_part = (
            held[:, part * width + start : part * width + start + HEAD_WIDTH] for part in range(3)
        )
        score = dot_nt(queries, key_part) * HEAD_WIDTH ** (-0.5)
        scores[0, start // HEAD_WIDTH] = score
        attention = (score * sigmoid(score) * allowed).astype(jnp.bfloat16)
        mixed[0, :, start : start + HEAD_WIDTH] = dot_nn(attention, values)


def gating_kernel(
    place,
    normed,
    b0,
    b1,
    b2,
    b_high,
    masked,
    keep,
    recv,
    mixed,
    gating_out,
    grad_gated,
    stats,
    weight,
):
    width = keep.shape[0]

    @pl.when(pl.program_id(0) == 0)
    def _():
        def store(at, block):
            weight[at, :] = block

        place_rows(1, place[0], b0.shape[1], (b0, b1, b2), (b_high,), store)

    proj = dot_nn(normed[0], weight[...])
    gating_out[0] = proj
    core = place[1]
    mine = masked[0, :, pl.ds(pl.multiple_of(core * width, width), width)]
    others = masked[0, :, pl.ds(pl.multiple_of((1 - core) * width, width), width)]
    grad = (dot_nt(mine, keep[...]) + dot_nt(others, recv[...])).astype(jnp.bfloat16)
    grad_gated[0] = grad
    mix = mixed[0]
    square = jnp.sum(mix * mix, axis=1, keepdims=True)
    cross = jnp.sum(
        grad.astype(jnp.float32) * (proj * sigmoid(proj)) * mix, axis=1, keepdims=True
    )
    lane = lax.broadcasted_iota(jnp.int32, (BLK, 128), 1)
    stats[0] = jnp.where(lane == 0, square, cross)


def norm_scale(model_width, stats, stats_other):
    total = stats[0] + stats_other[0]
    inv = lax.rsqrt(total[:, 0:1] / model_width + norm_eps)
    return inv, inv * inv * inv * (total[:, 1:2] / model_width)


def outer_kernel(place, projected, mixed, stats, stats_other, masked, term, total):
    width = mixed.shape[2]
    inv, _ = norm_scale(2 * width, stats, stats_other)
    proj = projected[0]
    gated = (mixed[0] * inv * (proj * sigmoid(proj))).astype(jnp.bfloat16)
    step = pl.program_id(0)
    for side in range(2):
        column = (place[1] + side) % 2
        part = masked[0, :, pl.ds(pl.multiple_of(column * width, width), width)]
        value = dot_tn(gated, part)

        @pl.when(step == 0)
        def _():
            total[side] = value

        @pl.when(step > 0)
        def _():
            total[side] += value

    @pl.when(step == pl.num_programs(0) - 1)
    def _():
        term[...] = total[...].astype(jnp.bfloat16)


def backward_kernel(
    lengths, gating_in, projected, scores, mixed, grad_gated, stats, stats_other, grads
):
    width = mixed.shape[2]
    inv, back = norm_scale(2 * width, stats, stats_other)
    gating, slope = silu_slope(gating_in[0])
    mix = mixed[0]
    grad = grad_gated[0].astype(jnp.float32)
    grads[0, :, :width] = (grad * (mix * inv) * slope).astype(jnp.bfloat16)
    grad_mixed = (inv * (grad * gating) - mix * back).astype(jnp.bfloat16)
    allowed = allowed_mask(lengths[pl.program_id(0)])
    for start in range(0, width, HEAD_WIDTH):
        (queries, queries_slope), (values, values_slope), (key_part, keys_slope) = (
            silu_slope(projected[0, :, part * width + start : part * width + start + HEAD_WIDTH])
            for part in range(3)
        )
        act, slope = silu_slope(scores[0, start // HEAD_WIDTH])
        attention = (act * allowed).astype(jnp.bfloat16)
        grad_head = grad_mixed[:, start : start + HEAD_WIDTH]
        grad_att = dot_nt(grad_head, values.astype(jnp.bfloat16)).astype(jnp.bfloat16)
        grad_score = (
            grad_att.astype(jnp.float32) * allowed * slope * HEAD_WIDTH ** (-0.5)
        ).astype(jnp.bfloat16)
        for part, (grad_part, side) in enumerate(
            (
                (dot_tn(attention, grad_head), values_slope),
                (dot_nn(grad_score, key_part.astype(jnp.bfloat16)), queries_slope),
                (dot_tn(grad_score, queries.astype(jnp.bfloat16)), keys_slope),
            ),
            1,
        ):
            held = grad_part.astype(jnp.bfloat16).astype(jnp.float32)
            at = part * width + start
            grads[0, :, at : at + HEAD_WIDTH] = (held * side).astype(jnp.bfloat16)


def store_slot(slot, value, columns, near, far):
    count = near.shape[0]

    @pl.when(slot < count)
    def _():
        near[jnp.minimum(slot, count - 1), :, columns] = value

    @pl.when(slot >= count)
    def _():
        far[jnp.maximum(slot - count, 0), :, columns] = value


def terms_kernel(place, normed_t, grads, keep, recv, *refs):
    outs, held, sems = refs[:8], refs[8:16], refs[16]
    step = pl.program_id(0)
    rows, width = held[0].shape[1], grads.shape[1]
    depth = normed_t.shape[0]
    half = keep.shape[0] // rows

    def copies(turn):
        return [
            pltpu.make_async_copy(held[at], outs[at], sems.at[at])
            for at in (2 * turn, 2 * turn + 1)
        ]

    for turn in range(4):

        @pl.when(step == turn)
        def _(turn=turn):
            near, far = held[2 * turn : 2 * turn + 2]
            for chunk in range(0, depth, BLK):
                term = dot_nn(normed_t[chunk : chunk + BLK, :], grads[...]).astype(jnp.bfloat16)
                for block in range(BLK // rows):
                    slot = relative_slot((chunk // rows + block) ^ place[0], turn)
                    value = term[block * rows : (block + 1) * rows]
                    store_slot(slot, value, slice(0, width), near, far)
            share = near.shape[2] - width
            if share:
                cut = slice((turn - 1) * share, turn * share)
                for side, outer in ((place[1], keep), (1 - place[1], recv)):
                    for block in range(half):
                        value = outer[block * rows : (block + 1) * rows, cut]
                        slot = relative_slot((side * half + block) ^ place[0], turn)
                        store_slot(slot, value, slice(width, width + share), near, far)
            for copy in copies(turn):
                copy.start()

    @pl.when(step == 3)
    def _():
        for turn in range(4):
            for copy in copies(turn):
                copy.wait()


def rows_of(*dims):
    return pl.BlockSpec((1, *dims), lambda i, *_: (i,) + (0,) * len(dims))


def whole(*dims):
    return pl.BlockSpec(dims, lambda i, *_: (0,) * len(dims))


def call(kernel, name, grid, prefetch, in_specs, out, inputs, scratch=()):
    moved = sum(v.size * v.dtype.itemsize for v in inputs)
    return pl.pallas_call(
        kernel,
        grid_spec=pltpu.PrefetchScalarGridSpec(
            num_scalar_prefetch=len(prefetch),
            grid=grid,
            in_specs=in_specs,
            out_specs=[spec for spec, _, _ in out],
            scratch_shapes=list(scratch),
        ),
        out_shape=[jax.ShapeDtypeStruct(shape, dtype) for _, shape, dtype in out],
        compiler_params=pltpu.CompilerParams(vmem_limit_bytes=20 * 1024 * 1024),
        cost_estimate=pl.CostEstimate(flops=1, bytes_accessed=1, transcendentals=0),
        name=name,
    )(*prefetch, *inputs)


def column_block(value, width, at):
    return pl.BlockSpec((*value.shape[:-1], width), lambda i, *_: (0,) * (value.ndim - 1) + (at,))


def attention_forward(place, lengths, normed, held_a, held_b):
    count, rows, depth = normed.shape
    width = held_a[3].shape[2]
    heads = width // HEAD_WIDTH
    held = (*held_a, *held_b)
    return call(
        forward_kernel,
        "attention_forward",
        (count,),
        (place, lengths),
        [rows_of(rows, depth)] + [whole(*part.shape) for part in held],
        [
            (rows_of(rows, 3 * width), (count, rows, 3 * width), jnp.float32),
            (rows_of(heads, rows, rows), (count, heads, rows, rows), jnp.float32),
            (rows_of(rows, width), (count, rows, width), jnp.float32),
            (whole(depth, width), (depth, width), jnp.bfloat16),
        ],
        (normed, *held),
        [pltpu.VMEM((depth, 3 * width), jnp.bfloat16)],
    )


def gating_forward(place, normed, held_b, masked, keep, recv, mixed):
    count, rows, depth = normed.shape
    width = mixed.shape[2]
    low, high = held_b[:3], held_b[4]
    return call(
        gating_kernel,
        "gating_forward",
        (count,),
        (place,),
        [
            rows_of(rows, depth),
            *(column_block(part, width, 1) for part in low),
            column_block(high, width, 0),
            rows_of(rows, depth),
            whole(*keep.shape),
            whole(*recv.shape),
            rows_of(rows, width),
        ],
        [
            (rows_of(rows, width), (count, rows, width), jnp.float32),
            (rows_of(rows, width), (count, rows, width), jnp.bfloat16),
            (rows_of(rows, 128), (count, rows, 128), jnp.float32),
        ],
        (normed, *low, high, masked, keep, recv, mixed),
        [pltpu.VMEM((depth, width), jnp.bfloat16)],
    )


def stats_specs(count, rows):
    return [
        rows_of(rows, 128),
        pl.BlockSpec((1, rows, 128), lambda i, *_: ((i + count // 2) % count, 0, 0)),
    ]


def outer_term(place, gating, mixed, stats, stats_other, masked):
    count, rows, width = mixed.shape
    block = rows_of(rows, width)
    shape = (2, width, width)
    return call(
        outer_kernel,
        "outer_term",
        (count,),
        (place,),
        [block, block, *stats_specs(count, rows), rows_of(rows, 2 * width)],
        [(whole(*shape), shape, jnp.bfloat16)],
        (gating, mixed, stats, stats_other, masked),
        [pltpu.VMEM(shape, jnp.float32)],
    )[0]


def attention_back(lengths, gating, projected, scores, mixed, grad_gated, stats, stats_other):
    count, rows, width = mixed.shape
    heads = width // HEAD_WIDTH
    block = rows_of(rows, width)
    return call(
        backward_kernel,
        "attention_back",
        (count,),
        (lengths,),
        [
            block,
            rows_of(rows, 3 * width),
            rows_of(heads, rows, rows),
            block,
            block,
            *stats_specs(count, rows),
        ],
        [(rows_of(rows, 4 * width), (count, rows, 4 * width), jnp.bfloat16)],
        (gating, projected, scores, mixed, grad_gated, stats, stats_other),
    )[0]


def terms(place, owned, normed_t, grads, keep, recv):
    depth, rows = normed_t.shape
    width = grads.shape[1] // 4
    shapes = []
    for turn in range(4):
        columns = width + (keep.shape[1] // 2 if turn in (1, 2) else 0)
        shapes += [(depth // owned // 2, owned, columns)] * 2
    anywhere = pl.BlockSpec(memory_space=pl.ANY)
    outs = call(
        terms_kernel,
        "terms",
        (4,),
        (place,),
        [
            whole(depth, rows),
            pl.BlockSpec((rows, width), lambda i, *_: (0, i)),
            whole(*keep.shape),
            whole(*recv.shape),
        ],
        [(anywhere, shape, jnp.bfloat16) for shape in shapes],
        (normed_t, grads, keep, recv),
        [pltpu.VMEM(shape, jnp.bfloat16) for shape in shapes] + [pltpu.SemaphoreType.DMA((8,))],
    )
    return [outs[2 * turn : 2 * turn + 2] for turn in range(4)]


def sum_squares(values):
    values = values.astype(jnp.float32)
    return jnp.sum(values * values)


def update_kernel(place, squares, mine, other, *refs):
    half = mine.shape[1] // 5
    model_width = 2 * half
    first = place[1] == 0
    owners = squares.shape[0] // 8
    total = sum(squares[8 * i : 8 * i + 1, 0:1] for i in range(owners))
    clip = jnp.minimum(1.0, jnp.sqrt(5.0 * model_width * model_width / (total + norm_eps)))
    for parts, (weight, moment, square, new_weight, new_moment, new_square) in (
        (range(4), (refs[0], refs[1], refs[2], refs[6], refs[7], refs[8])),
        (range(4, 5), (refs[3], refs[4], refs[5], refs[9], refs[10], refs[11])),
    ):
        update_sq = weight_sq = 0.0
        for part in parts:
            at = slice(part * half, (part + 1) * half)
            both = (mine[:, at].astype(jnp.float32), other[:, at].astype(jnp.float32))
            for core in (0, 1):
                grad = jnp.where(first, both[core], both[1 - core]) * clip
                start = (part - parts[0]) * model_width + core * half
                col = slice(start, start + half)
                held = beta_first * moment[:, col] + (1.0 - beta_first) * grad
                held_sq = beta_second * square[:, col] + (1.0 - beta_second) * grad * grad
                new_moment[:, col] = held
                new_square[:, col] = held_sq
                update = (held * (1.0 / (1.0 - beta_first**step_number))) / (
                    jnp.sqrt(held_sq * (1.0 / (1.0 - beta_second**step_number))) + update_eps
                )
                new_weight[:, col] = update
                update_sq += jnp.sum(update * update, axis=1, keepdims=True)
                held = weight[:, col].astype(jnp.float32)
                weight_sq += jnp.sum(held * held, axis=1, keepdims=True)
        ratio = learn_rate * jnp.sqrt(weight_sq) / (jnp.sqrt(update_sq) + ratio_eps)
        new_weight[...] = weight[...].astype(jnp.float32) - ratio * new_weight[...]


def update_rows(place, squares, mine, other, *state):
    rows = 16
    count = mine.shape[0] // rows

    def block(value):
        return pl.BlockSpec((rows, value.shape[1]), lambda i, *_: (i, 0))

    return call(
        update_kernel,
        "update_rows",
        (count,),
        (place,),
        [whole(*squares.shape)] + [block(v) for v in (mine, other, *state)],
        [(block(v), v.shape, jnp.float32) for v in state],
        (squares, mine, other, *state),
    )


def swap_cores(values):
    return lax.ppermute(values, "c", SWAP)


def over_link(values, axis, mask):
    return lax.ppermute(values, axis, [(i, i ^ mask) for i in range(4)])


def direct_round(blocks_of, groups):
    got = [[None] * 4, [None] * 4]
    for mask in (1, 3, 2):
        for group, axis in enumerate(("x", "y")):
            got[group][mask] = over_link(blocks_of(groups[group], mask), axis, mask)
    return got


def gather_groups(groups, width, prepare):
    got = direct_round(lambda group, mask: group, groups)
    got[0][1], beside = prepare(got[0][1])
    for group, mine in zip(got, groups):
        group[0] = mine
    got = lax.optimization_barrier(got)
    held = [jnp.stack(group) for group in got]
    one = [over_link(part, axis, 1) for part, axis in zip(held, ("y", "x"))]
    three = [over_link(part, axis, 3) for part, axis in zip(held, ("y", "x"))]
    one, three, beside = lax.optimization_barrier((one, three, beside))
    low = [over_link(part[:, :, :width], axis, 3) for part, axis in zip(one, ("y", "x"))]
    high = [over_link(part[:, :, width:], axis, 1) for part, axis in zip(three, ("y", "x"))]
    low, high = lax.optimization_barrier((low, high))
    return list(zip(held, one, three, low, high)), beside


def add_blocks(*blocks):
    return sum(block.astype(jnp.float32) for block in blocks).astype(jnp.bfloat16)


def scatter_parts(pairs):
    for step in (1, 0):
        got = [over_link(far, *STEPS[turn][step]) for turn, (_, far) in enumerate(pairs)]
        mine, got = lax.optimization_barrier(([near for near, _ in pairs], got))
        held = [add_blocks(*pair) for pair in zip(mine, got)]
        if step:
            pairs = [jnp.split(part, 2, axis=0) for part in held]
    groups = [jnp.concatenate([held[0], held[2]], axis=2), jnp.concatenate([held[1], held[3]], axis=2)]
    got = direct_round(lambda group, mask: group[mask], groups)
    return [add_blocks(group[0], *blocks[1:]) for group, blocks in zip(groups, got)]


def exchange(blocks, axes):
    return lax.all_to_all(blocks, axes, 0, 0, tiled=True)


def per_device(
    tokens,
    cotangent,
    lengths,
    norm_gain,
    weight_in,
    weight_out,
    moment_in,
    square_in,
    moment_out,
    square_out,
):
    slots, rows, model_width = tokens.shape
    half = model_width // 2
    quarter = half // 2
    core = lax.axis_index("c")
    own = lax.axis_index(OWN)
    owners = lax.axis_size(OWN)
    planes = lax.axis_size("z")
    owned = weight_in.shape[0]
    place = jnp.stack([own, core]).astype(jnp.int32)

    mine = [
        lax.dynamic_slice_in_dim(weight_in, part * model_width + core * half, half, axis=1)
        for part in range(4)
    ]
    mine_out = lax.dynamic_slice_in_dim(weight_out, core * half, half, axis=1)
    def prepare(got):
        got, token_rows, cot_rows = lax.optimization_barrier((got, tokens, cotangent))
        normed = (rms_scale(token_rows.astype(jnp.float32)) * norm_gain).astype(jnp.bfloat16)
        row_index = jnp.arange(rows, dtype=jnp.int32)
        live = row_index[None, :] < lengths[:, None]
        masked = jnp.where(live[:, :, None], cot_rows, jnp.zeros_like(cot_rows))
        normed = jnp.concatenate([normed, swap_cores(normed)], axis=0)
        masked = jnp.concatenate([masked, swap_cores(masked)], axis=0)
        all_lengths = jnp.concatenate([lengths, swap_cores(lengths)], axis=0)
        return got, (normed, masked, all_lengths, normed.reshape(-1, model_width).T)

    (held_a, held_b), (normed, masked, all_lengths, normed_t) = gather_groups(
        [
            jnp.concatenate([mine[2], mine[1], mine_out[:, :quarter]], axis=1),
            jnp.concatenate([mine[3], mine[0], mine_out[:, quarter:]], axis=1),
        ],
        half,
        prepare,
    )

    projected, scores, mixed, outer_cols = attention_forward(
        place, all_lengths, normed, held_a, held_b
    )
    outer_cols = outer_cols.reshape(2, half, half)
    keep = lax.dynamic_index_in_dim(outer_cols, core, axis=0, keepdims=False)
    recv = swap_cores(lax.dynamic_index_in_dim(outer_cols, 1 - core, axis=0, keepdims=False))
    gating, grad_gated, stats = gating_forward(place, normed, held_b, masked, keep, recv, mixed)
    stats_other = swap_cores(stats)
    outer = outer_term(place, gating, mixed, stats, stats_other, masked)
    outer_recv = swap_cores(outer[1])
    grads = attention_back(
        all_lengths, gating, projected, scores, mixed, grad_gated, stats, stats_other
    )
    term_g, term_v, term_q, term_k = terms(
        place, owned, normed_t, grads.reshape(-1, 4 * half), outer[0], outer_recv
    )
    part_gq, part_vk = scatter_parts([term_g, term_v, term_q, term_k])
    wide = half + quarter
    part = jnp.concatenate(
        [
            part_gq[:, :half],
            part_vk[:, :half],
            part_gq[:, half : 2 * half],
            part_vk[:, wide:],
            part_vk[:, half:wide],
            part_gq[:, 2 * half :],
        ],
        axis=1,
    )

    piece = jnp.sum(
        exchange(part, "z").reshape(planes, owned // planes, -1).astype(jnp.float32), axis=0
    ).astype(jnp.bfloat16)
    shard = exchange(
        jnp.broadcast_to(piece[None], (planes, *piece.shape)).reshape(owned, -1), "z"
    )
    other = swap_cores(shard)
    squares = exchange(
        jnp.broadcast_to(sum_squares(shard), (2 * owners * 8, 128)), ("c", *OWN)
    )
    return update_rows(
        place,
        squares,
        shard,
        other,
        weight_in,
        moment_in,
        square_in,
        weight_out,
        moment_out,
        square_out,
    )


def solution(mesh):
    fine = Mesh(mesh.devices.reshape(8, 2, 4, 4), ("z", "c", "x", "y"))
    histories = ("z", "c", "x", "y")
    placed = (
        P(histories, None, None),
        P(histories, None, None),
        P(histories),
        P(),
        P(OWN, None),
        P(OWN, None),
        P(OWN, None),
        P(OWN, None),
        P(OWN, None),
        P(OWN, None),
    )
    return jax.shard_map(
        per_device,
        mesh=fine,
        in_specs=placed,
        out_specs=(P(OWN, None),) * 6,
        check_vma=False,
    )
```

```python
import functools

import jax
import jax.numpy as jnp
from jax import lax
from jax.experimental import pallas as pl
from jax.experimental.pallas import tpu as pltpu
from jax.sharding import Mesh
from jax.sharding import PartitionSpec as P

BLK = 256
HEAD_WIDTH = 256

norm_eps = 1e-06
beta_first = 0.9
beta_second = 0.95
learn_rate = 0.01
step_number = 10.0
update_eps = 1e-08
ratio_eps = 1e-06

OWN = ("x", "y")
SWAP = ((0, 1), (1, 0))

ROUNDS = (
    (("x", 1), ("x", 3), ("y", 1), ("y", 3)),
    (("y", 1), ("y", 3), ("x", 1), ("x", 3)),
    (("x", 3), ("x", 1), ("y", 3), ("y", 1)),
    (("y", 3), ("y", 1), ("x", 3), ("x", 1)),
)


def rms_scale(values):
    return values * lax.rsqrt(jnp.mean(values * values, axis=-1, keepdims=True) + norm_eps)


def sigmoid(values):
    return 1.0 / (1.0 + jnp.exp(-values))


def allowed_mask(length):
    row = lax.broadcasted_iota(jnp.int32, (BLK, BLK), 0)
    col = lax.broadcasted_iota(jnp.int32, (BLK, BLK), 1)
    return ((col <= row) & (row < length)).astype(jnp.float32) * (1.0 / BLK)


def dot_nt(left, right):
    return lax.dot_general(
        left, right, (((1,), (1,)), ((), ())), preferred_element_type=jnp.float32
    )


def dot_tn(left, right):
    return lax.dot_general(
        left, right, (((0,), (0,)), ((), ())), preferred_element_type=jnp.float32
    )


def dot_nn(left, right):
    return jnp.dot(left, right, preferred_element_type=jnp.float32)


def silu_slope(values):
    sig = sigmoid(values)
    act = values * sig
    return act, sig + act * (1.0 - sig)


def link_bits(place, turn):
    high, odd = place >> 1, (place >> 1) ^ (place & 1)
    return odd + 2 * high if turn < 2 else high + 2 * odd


def gather_slot(mask, turn):
    one, two = (mask >> 2, mask & 3) if turn % 2 == 0 else (mask & 3, mask >> 2)
    return link_bits(one, turn) + 4 * link_bits(two, turn)


def scatter_slot(mask, turn):
    one, two = (mask >> 2, mask & 3) if turn % 2 == 0 else (mask & 3, mask >> 2)
    return one + 4 * link_bits(two, turn)


def place_rows(turn, own, near, far, store):
    count, rows, _ = near.shape
    for mask in range(2 * count):
        slot = gather_slot(mask, turn)
        block = near[slot] if slot < count else far[slot - count]
        store(pl.ds(pl.multiple_of((own ^ mask) * rows, rows), rows), block)


def forward_kernel(
    place,
    lengths,
    normed,
    q_near,
    q_far,
    k_near,
    k_far,
    v_near,
    v_far,
    g_near,
    g_far,
    projected,
    scores,
    mixed,
    outer,
    weight,
):
    count, rows, width = mixed.shape
    share = outer.shape[1] // 4

    @pl.when(pl.program_id(0) == 0)
    def _():
        for turn, near, far, column in (
            (0, q_near, q_far, 0),
            (1, k_near, k_far, 2 * width),
            (2, v_near, v_far, width),
            (3, g_near, g_far, None),
        ):

            def store(at, block, turn=turn, column=column):
                if column is not None:
                    weight[at, column : column + width] = block[:, :width]
                outer[at, turn * share : (turn + 1) * share] = block[:, block.shape[1] - share :]

            place_rows(turn, place[0], near, far, store)

    projected[...] = dot_nn(normed[...].reshape(count * rows, -1), weight[...]).reshape(
        projected.shape
    )
    for item in range(count):
        proj = projected[item]
        held = (proj * sigmoid(proj)).astype(jnp.bfloat16)
        allowed = allowed_mask(lengths[pl.program_id(0) * count + item])
        for start in range(0, width, HEAD_WIDTH):
            queries, values, key_part = (
                held[:, part * width + start : part * width + start + HEAD_WIDTH]
                for part in range(3)
            )
            score = dot_nt(queries, key_part) * HEAD_WIDTH ** (-0.5)
            scores[item, start // HEAD_WIDTH] = score
            attention = (score * sigmoid(score) * allowed).astype(jnp.bfloat16)
            mixed[item, :, start : start + HEAD_WIDTH] = dot_nn(attention, values)


def gating_kernel(
    place,
    normed,
    near,
    far,
    masked,
    keep,
    recv,
    mixed,
    gating_out,
    grad_gated,
    stats,
    weight,
):
    count, rows, width = mixed.shape

    @pl.when(pl.program_id(0) == 0)
    def _():
        def store(at, block):
            weight[at, :] = block

        place_rows(3, place[0], near, far, store)

    proj = dot_nn(normed[...].reshape(count * rows, -1), weight[...])
    gating_out[...] = proj.reshape(gating_out.shape)
    core = place[1]
    mine = masked[:, :, pl.ds(pl.multiple_of(core * width, width), width)]
    others = masked[:, :, pl.ds(pl.multiple_of((1 - core) * width, width), width)]
    grad = (
        dot_nt(mine.reshape(count * rows, width), keep[...])
        + dot_nt(others.reshape(count * rows, width), recv[...])
    ).astype(jnp.bfloat16)
    grad_gated[...] = grad.reshape(grad_gated.shape)
    mix = mixed[...].reshape(count * rows, width)
    square = jnp.sum(mix * mix, axis=1, keepdims=True)
    cross = jnp.sum(
        grad.astype(jnp.float32) * (proj * sigmoid(proj)) * mix, axis=1, keepdims=True
    )
    lane = lax.broadcasted_iota(jnp.int32, (count * rows, 128), 1)
    stats[...] = jnp.where(lane == 0, square, cross).reshape(stats.shape)


def norm_scale(model_width, stats, stats_other):
    total = (stats[...] + stats_other[...]).reshape(-1, stats.shape[2])
    inv = lax.rsqrt(total[:, 0:1] / model_width + norm_eps)
    return inv, inv * inv * inv * (total[:, 1:2] / model_width)


def outer_kernel(place, projected, mixed, stats, stats_other, masked, term, total):
    width = mixed.shape[2]
    inv, _ = norm_scale(2 * width, stats, stats_other)
    proj = projected[...].reshape(-1, width)
    gated = (mixed[...].reshape(-1, width) * inv * (proj * sigmoid(proj))).astype(jnp.bfloat16)
    step = pl.program_id(0)
    for side in range(2):
        column = (place[1] + side) % 2
        part = masked[:, :, pl.ds(pl.multiple_of(column * width, width), width)]
        value = dot_tn(gated, part.reshape(-1, width))

        @pl.when(step == 0)
        def _():
            total[side] = value

        @pl.when(step > 0)
        def _():
            total[side] += value

    @pl.when(step == pl.num_programs(0) - 1)
    def _():
        term[...] = total[...].astype(jnp.bfloat16)


def backward_kernel(
    lengths, gating_in, projected, scores, mixed, grad_gated, stats, stats_other, grads
):
    width = mixed.shape[2]
    inv, back = norm_scale(2 * width, stats, stats_other)
    gating, slope = silu_slope(gating_in[0])
    mix = mixed[0]
    grad = grad_gated[0].astype(jnp.float32)
    grads[0, :, :width] = (grad * (mix * inv) * slope).astype(jnp.bfloat16)
    grad_mixed = (inv * (grad * gating) - mix * back).astype(jnp.bfloat16)
    allowed = allowed_mask(lengths[pl.program_id(0)])
    for start in range(0, width, HEAD_WIDTH):
        (queries, queries_slope), (values, values_slope), (key_part, keys_slope) = (
            silu_slope(projected[0, :, part * width + start : part * width + start + HEAD_WIDTH])
            for part in range(3)
        )
        act, slope = silu_slope(scores[0, start // HEAD_WIDTH])
        attention = (act * allowed).astype(jnp.bfloat16)
        grad_head = grad_mixed[:, start : start + HEAD_WIDTH]
        grad_att = dot_nt(grad_head, values.astype(jnp.bfloat16)).astype(jnp.bfloat16)
        grad_score = (
            grad_att.astype(jnp.float32) * allowed * slope * HEAD_WIDTH ** (-0.5)
        ).astype(jnp.bfloat16)
        for part, (grad_part, side) in enumerate(
            (
                (dot_tn(attention, grad_head), values_slope),
                (dot_nn(grad_score, key_part.astype(jnp.bfloat16)), queries_slope),
                (dot_tn(grad_score, queries.astype(jnp.bfloat16)), keys_slope),
            ),
            1,
        ):
            held = grad_part.astype(jnp.bfloat16).astype(jnp.float32)
            at = part * width + start
            grads[0, :, at : at + HEAD_WIDTH] = (held * side).astype(jnp.bfloat16)


def terms_kernel(place, normed_t, grads, keep, recv, *refs):
    outs, held, sems = refs[:8], refs[8:12], refs[12]
    step = pl.program_id(0)
    slots, rows, _ = held[0].shape
    width = grads.shape[1]
    half = keep.shape[0] // rows

    def copies(turn):
        return [
            pltpu.make_async_copy(
                held[turn].at[pl.ds(side * (slots // 2), slots // 2)],
                outs[2 * turn + side],
                sems.at[2 * turn + side],
            )
            for side in range(2)
        ]

    for turn in range(4):

        @pl.when(step == turn)
        def _(turn=turn):
            term = dot_nn(normed_t[...], grads[...]).astype(jnp.bfloat16)
            for block in range(slots):
                slot = scatter_slot(block ^ place[0], turn)
                held[turn][slot, :, :width] = term[block * rows : (block + 1) * rows]
            share = held[turn].shape[2] - width
            cut = slice(turn * share, (turn + 1) * share)
            for side, outer in ((place[1], keep), (1 - place[1], recv)):
                for block in range(half):
                    slot = scatter_slot((side * half + block) ^ place[0], turn)
                    held[turn][slot, :, width:] = outer[block * rows : (block + 1) * rows, cut]
            for copy in copies(turn):
                copy.start()

    @pl.when(step == 3)
    def _():
        for turn in range(4):
            for copy in copies(turn):
                copy.wait()


def rows_of(*dims, some=1):
    return pl.BlockSpec((some, *dims), lambda i, *_: (i,) + (0,) * len(dims))


def whole(*dims):
    return pl.BlockSpec(
        dims, lambda i, *_: (0,) * len(dims), pipeline_mode=pl.Buffered(buffer_count=1)
    )


def columns_of(value, width, at):
    return pl.BlockSpec(
        (*value.shape[:-1], width),
        lambda i, *_: (0,) * (value.ndim - 1) + (at,),
        pipeline_mode=pl.Buffered(buffer_count=1),
    )


def call(kernel, name, grid, prefetch, in_specs, out, inputs, scratch=(), room=18):
    moved = sum(v.size * v.dtype.itemsize for v in inputs)
    return pl.pallas_call(
        kernel,
        grid_spec=pltpu.PrefetchScalarGridSpec(
            num_scalar_prefetch=len(prefetch),
            grid=grid,
            in_specs=in_specs,
            out_specs=[spec for spec, _, _ in out],
            scratch_shapes=list(scratch),
        ),
        out_shape=[jax.ShapeDtypeStruct(shape, dtype) for _, shape, dtype in out],
        compiler_params=pltpu.CompilerParams(vmem_limit_bytes=room * 1024 * 1024),
        cost_estimate=pl.CostEstimate(flops=1, bytes_accessed=1, transcendentals=0),
        name=name,
    )(*prefetch, *inputs)


def attention_forward(place, lengths, normed, queries, keys_in, values, gating):
    count, rows, depth = normed.shape
    width = depth // 2
    heads = width // HEAD_WIDTH
    held = (*queries, *keys_in, *values)
    return call(
        forward_kernel,
        "attention_forward",
        (count // 2,),
        (place, lengths),
        [rows_of(rows, depth, some=2)]
        + [whole(*part.shape) for part in held]
        + [columns_of(part, width // 4, 4) for part in gating],
        [
            (rows_of(rows, 3 * width, some=2), (count, rows, 3 * width), jnp.float32),
            (rows_of(heads, rows, rows, some=2), (count, heads, rows, rows), jnp.float32),
            (rows_of(rows, width, some=2), (count, rows, width), jnp.float32),
            (whole(depth, width), (depth, width), jnp.bfloat16),
        ],
        (normed, *held, *gating),
        [pltpu.VMEM((depth, 3 * width), jnp.bfloat16)],
        room=28,
    )


def gating_forward(place, normed, gating, masked, keep, recv, mixed):
    count, rows, depth = normed.shape
    width = mixed.shape[2]
    return call(
        gating_kernel,
        "gating_forward",
        (count // 2,),
        (place,),
        [
            rows_of(rows, depth, some=2),
            *(columns_of(part, width, 0) for part in gating),
            rows_of(rows, depth, some=2),
            whole(*keep.shape),
            whole(*recv.shape),
            rows_of(rows, width, some=2),
        ],
        [
            (rows_of(rows, width, some=2), (count, rows, width), jnp.float32),
            (rows_of(rows, width, some=2), (count, rows, width), jnp.bfloat16),
            (rows_of(rows, 128, some=2), (count, rows, 128), jnp.float32),
        ],
        (normed, *gating, masked, keep, recv, mixed),
        [pltpu.VMEM((depth, width), jnp.bfloat16)],
        room=18,
    )


def stats_specs(count, rows, some=1):
    steps = count // some
    return [
        rows_of(rows, 128, some=some),
        pl.BlockSpec((some, rows, 128), lambda i, *_: ((i + steps // 2) % steps, 0, 0)),
    ]


def outer_term(place, gating, mixed, stats, stats_other, masked):
    count, rows, width = mixed.shape
    block = rows_of(rows, width, some=2)
    shape = (2, width, width)
    return call(
        outer_kernel,
        "outer_term",
        (count // 2,),
        (place,),
        [block, block, *stats_specs(count, rows, 2), rows_of(rows, 2 * width, some=2)],
        [(whole(*shape), shape, jnp.bfloat16)],
        (gating, mixed, stats, stats_other, masked),
        [pltpu.VMEM(shape, jnp.float32)],
    )[0]


def attention_back(lengths, gating, projected, scores, mixed, grad_gated, stats, stats_other):
    count, rows, width = mixed.shape
    heads = width // HEAD_WIDTH
    block = rows_of(rows, width)
    return call(
        backward_kernel,
        "attention_back",
        (count,),
        (lengths,),
        [
            block,
            rows_of(rows, 3 * width),
            rows_of(heads, rows, rows),
            block,
            block,
            *stats_specs(count, rows),
        ],
        [(rows_of(rows, 4 * width), (count, rows, 4 * width), jnp.bfloat16)],
        (gating, projected, scores, mixed, grad_gated, stats, stats_other),
    )[0]


def terms(place, owned, normed_t, grads, keep, recv):
    depth, rows = normed_t.shape
    width = grads.shape[1] // 4
    columns = width + keep.shape[1] // 4
    shapes = [(depth // owned // 2, owned, columns)] * 8
    anywhere = pl.BlockSpec(memory_space=pl.ANY)
    outs = call(
        terms_kernel,
        "terms",
        (4,),
        (place,),
        [
            whole(depth, rows),
            pl.BlockSpec((rows, width), lambda i, *_: (0, i)),
            whole(*keep.shape),
            whole(*recv.shape),
        ],
        [(anywhere, shape, jnp.bfloat16) for shape in shapes],
        (normed_t, grads, keep, recv),
        [pltpu.VMEM((2 * half, *rest), jnp.bfloat16) for half, *rest in shapes[::2]]
        + [pltpu.SemaphoreType.DMA((8,))],
    )
    return [outs[2 * turn : 2 * turn + 2] for turn in range(4)]


def sum_squares(values):
    values = values.astype(jnp.float32)
    return jnp.sum(values * values)


def update_kernel(place, squares, mine, other, *refs):
    half = mine.shape[1] // 5
    model_width = 2 * half
    first = place[1] == 0
    owners = squares.shape[0] // 8
    total = sum(squares[8 * i : 8 * i + 1, 0:1] for i in range(owners))
    clip = jnp.minimum(1.0, jnp.sqrt(5.0 * model_width * model_width / (total + norm_eps)))
    for parts, (weight, moment, square, new_weight, new_moment, new_square) in (
        (range(4), (refs[0], refs[1], refs[2], refs[6], refs[7], refs[8])),
        (range(4, 5), (refs[3], refs[4], refs[5], refs[9], refs[10], refs[11])),
    ):
        update_sq = weight_sq = 0.0
        for part in parts:
            at = slice(part * half, (part + 1) * half)
            both = (mine[:, at].astype(jnp.float32), other[:, at].astype(jnp.float32))
            for core in (0, 1):
                grad = jnp.where(first, both[core], both[1 - core]) * clip
                start = (part - parts[0]) * model_width + core * half
                col = slice(start, start + half)
                held = beta_first * moment[:, col] + (1.0 - beta_first) * grad
                held_sq = beta_second * square[:, col] + (1.0 - beta_second) * grad * grad
                new_moment[:, col] = held
                new_square[:, col] = held_sq
                update = (held * (1.0 / (1.0 - beta_first**step_number))) / (
                    jnp.sqrt(held_sq * (1.0 / (1.0 - beta_second**step_number))) + update_eps
                )
                new_weight[:, col] = update
                update_sq += jnp.sum(update * update, axis=1, keepdims=True)
                held = weight[:, col].astype(jnp.float32)
                weight_sq += jnp.sum(held * held, axis=1, keepdims=True)
        ratio = learn_rate * jnp.sqrt(weight_sq) / (jnp.sqrt(update_sq) + ratio_eps)
        new_weight[...] = weight[...].astype(jnp.float32) - ratio * new_weight[...]


def update_rows(place, squares, mine, other, *state):
    rows = 16
    count = mine.shape[0] // rows

    def block(value):
        return pl.BlockSpec((rows, value.shape[1]), lambda i, *_: (i, 0))

    return call(
        update_kernel,
        "update_rows",
        (count,),
        (place,),
        [whole(*squares.shape)] + [block(v) for v in (mine, other, *state)],
        [(block(v), v.shape, jnp.float32) for v in state],
        (squares, mine, other, *state),
    )


def swap_cores(values):
    return lax.ppermute(values, "c", SWAP)


def over_link(values, axis, mask):
    return lax.ppermute(values, axis, [(i, i ^ mask) for i in range(4)])


def direct_round(blocks_of, groups):
    got = [[None] * 4, [None] * 4]
    for mask in (1, 3, 2):
        for group, axis in enumerate(("x", "y")):
            got[group][mask] = over_link(blocks_of(groups[group], mask), axis, mask)
    return got


def gather_parts(parts, prepare, join):
    held = [part[None] for part in parts]
    for step in range(3):
        got = [over_link(part, *ROUNDS[turn][step]) for turn, part in enumerate(held)]
        held = [jnp.concatenate(pair, axis=0) for pair in zip(held, got)]
        if step == 1:
            held, beside = lax.optimization_barrier((held, beside))
        else:
            held = lax.optimization_barrier(held)
        if step == 0:
            held[0], beside = prepare(held[0])
    far = [over_link(part, *ROUNDS[turn][3]) for turn, part in enumerate(held)]
    far, beside = lax.optimization_barrier((far, join(beside)))
    return list(zip(held, far)), beside


def add_blocks(*blocks):
    return sum(block.astype(jnp.float32) for block in blocks).astype(jnp.bfloat16)


def scatter_parts(pairs):
    for step in (1, 0):
        got = [over_link(far, *ROUNDS[turn][2 + step]) for turn, (_, far) in enumerate(pairs)]
        mine, got = lax.optimization_barrier(([near for near, _ in pairs], got))
        held = [add_blocks(*pair) for pair in zip(mine, got)]
        if step:
            pairs = [jnp.split(part, 2, axis=0) for part in held]
    groups = [jnp.concatenate([held[0], held[2]], axis=2), jnp.concatenate([held[1], held[3]], axis=2)]
    got = direct_round(lambda group, mask: group[mask], groups)
    return [add_blocks(group[0], *blocks[1:]) for group, blocks in zip(groups, got)]


def exchange(blocks, axes):
    return lax.all_to_all(blocks, axes, 0, 0, tiled=True)


def per_device(
    tokens,
    cotangent,
    lengths,
    norm_gain,
    weight_in,
    weight_out,
    moment_in,
    square_in,
    moment_out,
    square_out,
):
    slots, rows, model_width = tokens.shape
    half = model_width // 2
    share = half // 4
    core = lax.axis_index("c")
    own = lax.axis_index(OWN)
    owners = lax.axis_size(OWN)
    planes = lax.axis_size("z")
    owned = weight_in.shape[0]
    place = jnp.stack([own, core]).astype(jnp.int32)

    mine = [
        lax.dynamic_slice_in_dim(weight_in, part * model_width + core * half, half, axis=1)
        for part in range(4)
    ]
    mine_out = lax.dynamic_slice_in_dim(weight_out, core * half, half, axis=1)
    def prepare(got):
        got, token_rows, cot_rows, lengths_other = lax.optimization_barrier(
            (got, tokens, cotangent, swap_cores(lengths))
        )
        normed = (rms_scale(token_rows.astype(jnp.float32)) * norm_gain).astype(jnp.bfloat16)
        row_index = jnp.arange(rows, dtype=jnp.int32)
        live = row_index[None, :] < lengths[:, None]
        masked = jnp.where(live[:, :, None], cot_rows, jnp.zeros_like(cot_rows))
        mine = jnp.concatenate([normed, masked], axis=0)
        return got, (mine, swap_cores(mine), lengths_other)

    def join(made):
        mine, other, lengths_other = made
        normed, masked = (
            jnp.concatenate([side[at : at + slots] for side in (mine, other)], axis=0)
            for at in (0, slots)
        )
        all_lengths = jnp.concatenate([lengths, lengths_other], axis=0)
        return normed, masked, all_lengths, normed.reshape(-1, model_width).T

    (queries, keys_in, values, gating), (normed, masked, all_lengths, normed_t) = gather_parts(
        [
            jnp.concatenate([mine[part], mine_out[:, at * share : (at + 1) * share]], axis=1)
            for at, part in enumerate((2, 3, 1, 0))
        ],
        prepare,
        join,
    )

    projected, scores, mixed, outer_cols = attention_forward(
        place, all_lengths, normed, queries, keys_in, values, gating
    )
    outer_cols = outer_cols.reshape(2, half, half)
    keep = lax.dynamic_index_in_dim(outer_cols, core, axis=0, keepdims=False)
    recv = swap_cores(lax.dynamic_index_in_dim(outer_cols, 1 - core, axis=0, keepdims=False))
    gating, grad_gated, stats = gating_forward(place, normed, gating, masked, keep, recv, mixed)
    stats_other = swap_cores(stats)
    outer = outer_term(place, gating, mixed, stats, stats_other, masked)
    outer_recv = swap_cores(outer[1])
    grads = attention_back(
        all_lengths, gating, projected, scores, mixed, grad_gated, stats, stats_other
    )
    term_g, term_v, term_q, term_k = terms(
        place, owned, normed_t, grads.reshape(-1, 4 * half), outer[0], outer_recv
    )
    part_gq, part_vk = scatter_parts([term_g, term_v, term_q, term_k])
    wide = half + share
    sides = (part_gq, part_vk)
    part = jnp.concatenate(
        [side[:, at : at + half] for at in (0, wide) for side in sides]
        + [side[:, at : at + share] for at in (half, wide + half) for side in sides],
        axis=1,
    )

    piece = jnp.sum(
        exchange(part, "z").reshape(planes, owned // planes, -1).astype(jnp.float32), axis=0
    ).astype(jnp.bfloat16)
    shard = exchange(
        jnp.broadcast_to(piece[None], (planes, *piece.shape)).reshape(owned, -1), "z"
    )
    other = swap_cores(shard)
    squares = exchange(
        jnp.broadcast_to(sum_squares(shard), (2 * owners * 8, 128)), ("c", *OWN)
    )
    return update_rows(
        place,
        squares,
        shard,
        other,
        weight_in,
        moment_in,
        square_in,
        weight_out,
        moment_out,
        square_out,
    )


def solution(mesh):
    fine = Mesh(mesh.devices.reshape(8, 2, 4, 4), ("z", "c", "x", "y"))
    histories = ("z", "c", "x", "y")
    placed = (
        P(histories, None, None),
        P(histories, None, None),
        P(histories),
        P(),
        P(OWN, None),
        P(OWN, None),
        P(OWN, None),
        P(OWN, None),
        P(OWN, None),
        P(OWN, None),
    )
    return jax.shard_map(
        per_device,
        mesh=fine,
        in_specs=placed,
        out_specs=(P(OWN, None),) * 6,
        check_vma=False,
    )
```

```python
import functools

import jax
import jax.numpy as jnp
from jax import lax
from jax.experimental import pallas as pl
from jax.experimental.pallas import tpu as pltpu
from jax.sharding import Mesh
from jax.sharding import PartitionSpec as P

BLK = 256
HEAD_WIDTH = 256

norm_eps = 1e-06
beta_first = 0.9
beta_second = 0.95
learn_rate = 0.01
step_number = 10.0
update_eps = 1e-08
ratio_eps = 1e-06

OWN = ("x", "y")
SWAP = ((0, 1), (1, 0))

ROUNDS = (((0, 1), (0, 3), (1, 1), (1, 3)), ((0, 3), (0, 1), (1, 3), (1, 1)))


def rms_scale(values):
    return values * lax.rsqrt(jnp.mean(values * values, axis=-1, keepdims=True) + norm_eps)


def sigmoid(values):
    return 0.5 + 0.5 * jnp.tanh(0.5 * values)


def allowed_mask(length):
    row = lax.broadcasted_iota(jnp.int32, (BLK, BLK), 0)
    col = lax.broadcasted_iota(jnp.int32, (BLK, BLK), 1)
    return ((col <= row) & (row < length)).astype(jnp.float32) * (1.0 / BLK)


def dot_nt(left, right):
    return lax.dot_general(
        left, right, (((1,), (1,)), ((), ())), preferred_element_type=jnp.float32
    )


def dot_tn(left, right):
    return lax.dot_general(
        left, right, (((0,), (0,)), ((), ())), preferred_element_type=jnp.float32
    )


def dot_nn(left, right):
    return jnp.dot(left, right, preferred_element_type=jnp.float32)


def silu_slope(values):
    sig = sigmoid(values)
    act = values * sig
    return act, sig + act * (1.0 - sig)


def scatter_slot(mask, part, core):
    x, y = mask >> 2, mask & 3
    one, two = jnp.where(core == 0, x, y), jnp.where(core == 0, y, x)
    high, odd = two >> 1, (two >> 1) ^ (two & 1)
    return one + 4 * (odd + 2 * high if part == 0 else high + 2 * odd)


def gather_mask(slot, part, core):
    links = (1, 3) if part == 0 else (3, 1)
    one, two = (
        (links[0] if bits & 1 else 0) ^ (links[1] if bits & 2 else 0)
        for bits in (slot & 3, slot >> 2)
    )
    return jnp.where(core == 0, 4 * one + two, 4 * two + one)


def place_rows(part, place, held, store):
    count, rows, _ = held[0].shape
    for slot in range(4 * count):
        block = held[slot // count][slot % count]
        owner = place[0] ^ gather_mask(slot, part, place[1])
        store(pl.ds(pl.multiple_of(owner * rows, rows), rows), block)


def forward_kernel(
    place,
    lengths,
    normed,
    *refs,
):
    projected, scores, mixed, outer, weight = refs[8:]
    count, rows, width = mixed.shape
    share = outer.shape[1] // 2

    @pl.when(pl.program_id(0) == 0)
    def _():
        def store_0(at, block):
            weight[at, :width] = block[:, :width]
            weight[at, 2 * width :] = block[:, width : 2 * width]
            outer[at, :share] = block[:, 2 * width :]

        def store_1(at, block):
            weight[at, width : 2 * width] = block[:, :width]
            outer[at, share:] = block[:, 2 * width :]

        place_rows(0, place, refs[:4], store_0)
        place_rows(1, place, refs[4:8], store_1)

    projected[...] = dot_nn(normed[...].reshape(count * rows, -1), weight[...]).reshape(
        projected.shape
    )
    for item in range(count):
        proj = projected[item]
        held = (proj * sigmoid(proj)).astype(jnp.bfloat16)
        allowed = allowed_mask(lengths[pl.program_id(0) * count + item])
        for start in range(0, width, HEAD_WIDTH):
            queries, values, key_part = (
                held[:, part * width + start : part * width + start + HEAD_WIDTH]
                for part in range(3)
            )
            score = dot_nt(queries, key_part) * HEAD_WIDTH ** (-0.5)
            scores[item, start // HEAD_WIDTH] = score
            attention = (score * sigmoid(score) * allowed).astype(jnp.bfloat16)
            mixed[item, :, start : start + HEAD_WIDTH] = dot_nn(attention, values)


def gating_kernel(
    place,
    normed,
    held_0,
    held_1,
    held_2,
    held_3,
    masked,
    keep,
    recv,
    mixed,
    gating_out,
    grad_gated,
    stats,
    weight,
):
    count, rows, width = mixed.shape

    @pl.when(pl.program_id(0) == 0)
    def _():
        def store(at, block):
            weight[at, :] = block

        place_rows(1, place, (held_0, held_1, held_2, held_3), store)

    proj = dot_nn(normed[...].reshape(count * rows, -1), weight[...])
    gating_out[...] = proj.reshape(gating_out.shape)
    core = place[1]
    mine = masked[:, :, pl.ds(pl.multiple_of(core * width, width), width)]
    others = masked[:, :, pl.ds(pl.multiple_of((1 - core) * width, width), width)]
    grad = (
        dot_nt(mine.reshape(count * rows, width), keep[...])
        + dot_nt(others.reshape(count * rows, width), recv[...])
    ).astype(jnp.bfloat16)
    grad_gated[...] = grad.reshape(grad_gated.shape)
    mix = mixed[...].reshape(count * rows, width)
    square = jnp.sum(mix * mix, axis=1, keepdims=True)
    cross = jnp.sum(
        grad.astype(jnp.float32) * (proj * sigmoid(proj)) * mix, axis=1, keepdims=True
    )
    lane = lax.broadcasted_iota(jnp.int32, (count * rows, 128), 1)
    stats[...] = jnp.where(lane == 0, square, cross).reshape(stats.shape)


def norm_scale(model_width, stats, stats_other):
    total = (stats[...] + stats_other[...]).reshape(-1, stats.shape[2])
    inv = lax.rsqrt(total[:, 0:1] / model_width + norm_eps)
    return inv, inv * inv * inv * (total[:, 1:2] / model_width)


def outer_kernel(place, projected, mixed, stats, stats_other, masked, term, total):
    width = mixed.shape[2]
    inv, _ = norm_scale(2 * width, stats, stats_other)
    proj = projected[...].reshape(-1, width)
    gated = (mixed[...].reshape(-1, width) * inv * (proj * sigmoid(proj))).astype(jnp.bfloat16)
    step = pl.program_id(0)
    for side in range(2):
        column = (place[1] + side) % 2
        part = masked[:, :, pl.ds(pl.multiple_of(column * width, width), width)]
        value = dot_tn(gated, part.reshape(-1, width))

        @pl.when(step == 0)
        def _():
            total[side] = value

        @pl.when(step > 0)
        def _():
            total[side] += value

    @pl.when(step == pl.num_programs(0) - 1)
    def _():
        term[...] = total[...].astype(jnp.bfloat16)


def backward_kernel(
    lengths, gating_in, projected, scores, mixed, grad_gated, stats, stats_other, grads
):
    width = mixed.shape[2]
    inv, back = norm_scale(2 * width, stats, stats_other)
    gating, slope = silu_slope(gating_in[0])
    mix = mixed[0]
    grad = grad_gated[0].astype(jnp.float32)
    grads[0, :, :width] = (grad * (mix * inv) * slope).astype(jnp.bfloat16)
    grad_mixed = (inv * (grad * gating) - mix * back).astype(jnp.bfloat16)
    allowed = allowed_mask(lengths[pl.program_id(0)])
    for start in range(0, width, HEAD_WIDTH):
        (queries, queries_slope), (values, values_slope), (key_part, keys_slope) = (
            silu_slope(projected[0, :, part * width + start : part * width + start + HEAD_WIDTH])
            for part in range(3)
        )
        act, slope = silu_slope(scores[0, start // HEAD_WIDTH])
        attention = (act * allowed).astype(jnp.bfloat16)
        grad_head = grad_mixed[:, start : start + HEAD_WIDTH]
        grad_att = dot_nt(grad_head, values.astype(jnp.bfloat16)).astype(jnp.bfloat16)
        grad_score = (
            grad_att.astype(jnp.float32) * allowed * slope * HEAD_WIDTH ** (-0.5)
        ).astype(jnp.bfloat16)
        for part, (grad_part, side) in enumerate(
            (
                (dot_tn(attention, grad_head), values_slope),
                (dot_nn(grad_score, key_part.astype(jnp.bfloat16)), queries_slope),
                (dot_tn(grad_score, queries.astype(jnp.bfloat16)), keys_slope),
            ),
            1,
        ):
            held = grad_part.astype(jnp.bfloat16).astype(jnp.float32)
            at = part * width + start
            grads[0, :, at : at + HEAD_WIDTH] = (held * side).astype(jnp.bfloat16)


def terms_kernel(place, normed_t, grads, keep, recv, *refs):
    outs, held, sems = refs[:8], refs[8:10], refs[10]
    step = pl.program_id(0)
    slots, rows, _ = held[0].shape
    width = grads.shape[1]
    half = keep.shape[0] // rows
    core = place[1]

    def copies(turn):
        part, columns = turn // 2, (slice(width, None) if turn % 2 else slice(0, width))
        span = pl.ds(columns.start, (held[0].shape[2] if turn % 2 else width) - columns.start)
        return [
            pltpu.make_async_copy(
                held[part].at[pl.ds(group * (slots // 4), slots // 4), :, span],
                outs[4 * part + group].at[:, :, span],
                sems.at[4 * turn + group],
            )
            for group in range(4)
        ]

    for turn in range(4):

        @pl.when(step == turn)
        def _(turn=turn):
            part, start = turn // 2, (turn % 2) * width
            term = dot_nn(normed_t[...], grads[...]).astype(jnp.bfloat16)
            for block in range(slots):
                slot = scatter_slot(block ^ place[0], part, core)
                held[part][slot, :, start : start + width] = term[block * rows : (block + 1) * rows]
            if turn % 2:
                share = held[part].shape[2] - 2 * width
                cut = slice(part * share, (part + 1) * share)
                for side, outer in ((core, keep), (1 - core, recv)):
                    for block in range(half):
                        slot = scatter_slot((side * half + block) ^ place[0], part, core)
                        value = outer[block * rows : (block + 1) * rows, cut]
                        held[part][slot, :, 2 * width :] = value
            for copy in copies(turn):
                copy.start()

    @pl.when(step == 3)
    def _():
        for turn in range(4):
            for copy in copies(turn):
                copy.wait()


def rows_of(*dims, some=1):
    return pl.BlockSpec((some, *dims), lambda i, *_: (i,) + (0,) * len(dims))


def whole(*dims, buffers=1):
    return pl.BlockSpec(
        dims, lambda i, *_: (0,) * len(dims), pipeline_mode=pl.Buffered(buffer_count=buffers)
    )


def columns_of(value, width, at):
    return pl.BlockSpec(
        (*value.shape[:-1], width),
        lambda i, *_: (0,) * (value.ndim - 1) + (at,),
        pipeline_mode=pl.Buffered(buffer_count=1),
    )


def call(kernel, name, grid, prefetch, in_specs, out, inputs, scratch=(), room=18):
    moved = sum(v.size * v.dtype.itemsize for v in inputs)
    return pl.pallas_call(
        kernel,
        grid_spec=pltpu.PrefetchScalarGridSpec(
            num_scalar_prefetch=len(prefetch),
            grid=grid,
            in_specs=in_specs,
            out_specs=[spec for spec, _, _ in out],
            scratch_shapes=list(scratch),
        ),
        out_shape=[jax.ShapeDtypeStruct(shape, dtype) for _, shape, dtype in out],
        compiler_params=pltpu.CompilerParams(vmem_limit_bytes=room * 1024 * 1024),
        cost_estimate=pl.CostEstimate(flops=1, bytes_accessed=1, transcendentals=0),
        name=name,
    )(*prefetch, *inputs)


def attention_forward(place, lengths, normed, held):
    count, rows, depth = normed.shape
    width = depth // 2
    heads = width // HEAD_WIDTH
    return call(
        forward_kernel,
        "attention_forward",
        (count // 2,),
        (place, lengths),
        [rows_of(rows, depth, some=2)]
        + [whole(*part.shape) for part in held],
        [
            (rows_of(rows, 3 * width, some=2), (count, rows, 3 * width), jnp.float32),
            (rows_of(heads, rows, rows, some=2), (count, heads, rows, rows), jnp.float32),
            (rows_of(rows, width, some=2), (count, rows, width), jnp.float32),
            (whole(depth, width), (depth, width), jnp.bfloat16),
        ],
        (normed, *held),
        [pltpu.VMEM((depth, 3 * width), jnp.bfloat16)],
        room=28,
    )


def gating_forward(place, normed, gating, masked, keep, recv, mixed):
    count, rows, depth = normed.shape
    width = mixed.shape[2]
    return call(
        gating_kernel,
        "gating_forward",
        (count // 2,),
        (place,),
        [
            rows_of(rows, depth, some=2),
            *(columns_of(part, width, 1) for part in gating),
            rows_of(rows, depth, some=2),
            whole(*keep.shape),
            whole(*recv.shape),
            rows_of(rows, width, some=2),
        ],
        [
            (rows_of(rows, width, some=2), (count, rows, width), jnp.float32),
            (rows_of(rows, width, some=2), (count, rows, width), jnp.bfloat16),
            (rows_of(rows, 128, some=2), (count, rows, 128), jnp.float32),
        ],
        (normed, *gating, masked, keep, recv, mixed),
        [pltpu.VMEM((depth, width), jnp.bfloat16)],
        room=18,
    )


def stats_specs(count, rows, some=1):
    steps = count // some
    return [
        rows_of(rows, 128, some=some),
        pl.BlockSpec((some, rows, 128), lambda i, *_: ((i + steps // 2) % steps, 0, 0)),
    ]


def outer_term(place, gating, mixed, stats, stats_other, masked):
    count, rows, width = mixed.shape
    block = rows_of(rows, width, some=2)
    shape = (2, width, width)
    return call(
        outer_kernel,
        "outer_term",
        (count // 2,),
        (place,),
        [block, block, *stats_specs(count, rows, 2), rows_of(rows, 2 * width, some=2)],
        [(whole(*shape), shape, jnp.bfloat16)],
        (gating, mixed, stats, stats_other, masked),
        [pltpu.VMEM(shape, jnp.float32)],
    )[0]


def attention_back(lengths, gating, projected, scores, mixed, grad_gated, stats, stats_other):
    count, rows, width = mixed.shape
    heads = width // HEAD_WIDTH
    block = rows_of(rows, width)
    return call(
        backward_kernel,
        "attention_back",
        (count,),
        (lengths,),
        [
            block,
            rows_of(rows, 3 * width),
            rows_of(heads, rows, rows),
            block,
            block,
            *stats_specs(count, rows),
        ],
        [(rows_of(rows, 4 * width), (count, rows, 4 * width), jnp.bfloat16)],
        (gating, projected, scores, mixed, grad_gated, stats, stats_other),
    )[0]


def terms(place, owned, normed_t, grads, keep, recv):
    depth, rows = normed_t.shape
    width = grads.shape[1] // 4
    shapes = [(depth // owned // 4, owned, 2 * width + keep.shape[1] // 2)] * 8
    anywhere = pl.BlockSpec(memory_space=pl.ANY)
    outs = call(
        terms_kernel,
        "terms",
        (4,),
        (place,),
        [
            whole(depth, rows, buffers=2),
            pl.BlockSpec((rows, width), lambda i, *_: (0, i)),
            whole(*keep.shape, buffers=2),
            whole(*recv.shape, buffers=2),
        ],
        [(anywhere, shape, jnp.bfloat16) for shape in shapes],
        (normed_t, grads, keep, recv),
        [pltpu.VMEM((4 * count, *rest), jnp.bfloat16) for count, *rest in shapes[::4]]
        + [pltpu.SemaphoreType.DMA((16,))],
    )
    return [outs[:4], outs[4:]]


def sum_squares(values):
    values = values.astype(jnp.float32)
    return jnp.sum(values * values)


def update_kernel(place, squares, mine, other, *refs):
    half = mine.shape[1] // 5
    model_width = 2 * half
    first = place[1] == 0
    owners = squares.shape[0] // 8
    total = sum(squares[8 * i : 8 * i + 1, 0:1] for i in range(owners))
    clip = jnp.minimum(1.0, jnp.sqrt(5.0 * model_width * model_width / (total + norm_eps)))
    for parts, (weight, moment, square, new_weight, new_moment, new_square) in (
        (range(4), (refs[0], refs[1], refs[2], refs[6], refs[7], refs[8])),
        (range(4, 5), (refs[3], refs[4], refs[5], refs[9], refs[10], refs[11])),
    ):
        update_sq = weight_sq = 0.0
        for part in parts:
            at = slice(part * half, (part + 1) * half)
            both = (mine[:, at].astype(jnp.float32), other[:, at].astype(jnp.float32))
            for core in (0, 1):
                grad = jnp.where(first, both[core], both[1 - core]) * clip
                start = (part - parts[0]) * model_width + core * half
                col = slice(start, start + half)
                held = beta_first * moment[:, col] + (1.0 - beta_first) * grad
                held_sq = beta_second * square[:, col] + (1.0 - beta_second) * grad * grad
                new_moment[:, col] = held
                new_square[:, col] = held_sq
                update = (held * (1.0 / (1.0 - beta_first**step_number))) / (
                    jnp.sqrt(held_sq * (1.0 / (1.0 - beta_second**step_number))) + update_eps
                )
                new_weight[:, col] = update
                update_sq += jnp.sum(update * update, axis=1, keepdims=True)
                held = weight[:, col].astype(jnp.float32)
                weight_sq += jnp.sum(held * held, axis=1, keepdims=True)
        ratio = learn_rate * jnp.sqrt(weight_sq) / (jnp.sqrt(update_sq) + ratio_eps)
        new_weight[...] = weight[...].astype(jnp.float32) - ratio * new_weight[...]


def update_rows(place, squares, mine, other, *state):
    rows = 16
    count = mine.shape[0] // rows

    def block(value):
        return pl.BlockSpec((rows, value.shape[1]), lambda i, *_: (i, 0))

    return call(
        update_kernel,
        "update_rows",
        (count,),
        (place,),
        [whole(*squares.shape)] + [block(v) for v in (mine, other, *state)],
        [(block(v), v.shape, jnp.float32) for v in state],
        (squares, mine, other, *state),
    )


def swap_cores(values):
    return lax.ppermute(values, "c", SWAP)


def over_link(values, axis, mask):
    pairs = []
    for core in range(2):
        shift = mask << 2 if axis == core else mask
        pairs += [(16 * core + own, 16 * core + (own ^ shift)) for own in range(16)]
    return lax.ppermute(values, ("c", *OWN), pairs)


def gather_parts(parts, prepare, join):
    held = [part[None] for part in parts]
    for step in range(2):
        got = [over_link(part, *ROUNDS[turn][step]) for turn, part in enumerate(held)]
        held = [jnp.concatenate(pair, axis=0) for pair in zip(held, got)]
        if step == 0:
            held = lax.optimization_barrier(held)
            held[0], beside = prepare(held[0])
        else:
            held, beside = lax.optimization_barrier((held, beside))
    first = [over_link(part, *ROUNDS[turn][2]) for turn, part in enumerate(held)]
    second = [over_link(part, *ROUNDS[turn][3]) for turn, part in enumerate(held)]
    first, second = lax.optimization_barrier((first, second))
    both = [over_link(part, *ROUNDS[turn][3]) for turn, part in enumerate(first)]
    both, beside = lax.optimization_barrier((both, join(beside)))
    return list(zip(held, first, second, both)), beside


def add_blocks(*blocks):
    return sum(block.astype(jnp.float32) for block in blocks).astype(jnp.bfloat16)


def scatter_parts(parts):
    mine, first, second, both = zip(*parts)
    both = [over_link(part, *ROUNDS[turn][3]) for turn, part in enumerate(both)]
    second = [over_link(part, *ROUNDS[turn][3]) for turn, part in enumerate(second)]
    first, both, second = lax.optimization_barrier((first, both, second))
    first = [add_blocks(*pair) for pair in zip(first, both)]
    first = [over_link(part, *ROUNDS[turn][2]) for turn, part in enumerate(first)]
    mine, first, second = lax.optimization_barrier((mine, first, second))
    held = [add_blocks(*blocks) for blocks in zip(mine, first, second)]
    held = jnp.concatenate(held, axis=2)
    return add_blocks(held[0], *(over_link(held[mask], 0, mask) for mask in (1, 3, 2)))


def exchange(blocks, axes):
    return lax.all_to_all(blocks, axes, 0, 0, tiled=True)


def per_device(
    tokens,
    cotangent,
    lengths,
    norm_gain,
    weight_in,
    weight_out,
    moment_in,
    square_in,
    moment_out,
    square_out,
):
    slots, rows, model_width = tokens.shape
    half = model_width // 2
    share = half // 4
    core = lax.axis_index("c")
    own = lax.axis_index(OWN)
    owners = lax.axis_size(OWN)
    planes = lax.axis_size("z")
    owned = weight_in.shape[0]
    place = jnp.stack([own, core]).astype(jnp.int32)

    mine = [
        lax.dynamic_slice_in_dim(weight_in, part * model_width + core * half, half, axis=1)
        for part in range(4)
    ]
    mine_out = lax.dynamic_slice_in_dim(weight_out, core * half, half, axis=1)
    def prepare(got):
        got, token_rows, cot_rows, lengths_other = lax.optimization_barrier(
            (got, tokens, cotangent, swap_cores(lengths))
        )
        normed = (rms_scale(token_rows.astype(jnp.float32)) * norm_gain).astype(jnp.bfloat16)
        row_index = jnp.arange(rows, dtype=jnp.int32)
        live = row_index[None, :] < lengths[:, None]
        masked = jnp.where(live[:, :, None], cot_rows, jnp.zeros_like(cot_rows))
        mine = jnp.concatenate([normed, masked], axis=0)
        return got, (mine, swap_cores(mine), lengths_other)

    def join(made):
        mine, other, lengths_other = made
        normed, masked = (
            jnp.concatenate([side[at : at + slots] for side in (mine, other)], axis=0)
            for at in (0, slots)
        )
        all_lengths = jnp.concatenate([lengths, lengths_other], axis=0)
        return normed, masked, all_lengths, normed.reshape(-1, model_width).T

    parts, (normed, masked, all_lengths, normed_t) = gather_parts(
        [
            jnp.concatenate([mine[2], mine[3], mine_out[:, : half // 2]], axis=1),
            jnp.concatenate([mine[1], mine[0], mine_out[:, half // 2 :]], axis=1),
        ],
        prepare,
        join,
    )

    projected, scores, mixed, outer_cols = attention_forward(
        place, all_lengths, normed, (*parts[0], *parts[1])
    )
    outer_cols = outer_cols.reshape(2, half, half)
    keep = lax.dynamic_index_in_dim(outer_cols, core, axis=0, keepdims=False)
    recv = swap_cores(lax.dynamic_index_in_dim(outer_cols, 1 - core, axis=0, keepdims=False))
    gating, grad_gated, stats = gating_forward(place, normed, parts[1], masked, keep, recv, mixed)
    stats_other = swap_cores(stats)
    outer = outer_term(place, gating, mixed, stats, stats_other, masked)
    outer_recv = swap_cores(outer[1])
    grads = attention_back(
        all_lengths, gating, projected, scores, mixed, grad_gated, stats, stats_other
    )
    part = scatter_parts(
        terms(place, owned, normed_t, grads.reshape(-1, 4 * half), outer[0], outer_recv)
    )
    wide = part.shape[1] // 2
    part = jnp.concatenate(
        [part[:, : 2 * half], part[:, wide : wide + 2 * half]]
        + [part[:, at + 2 * half : at + wide] for at in (0, wide)],
        axis=1,
    )

    piece = jnp.sum(
        exchange(part, "z").reshape(planes, owned // planes, -1).astype(jnp.float32), axis=0
    ).astype(jnp.bfloat16)
    shard = exchange(
        jnp.broadcast_to(piece[None], (planes, *piece.shape)).reshape(owned, -1), "z"
    )
    other = swap_cores(shard)
    squares = exchange(
        jnp.broadcast_to(sum_squares(shard), (2 * owners * 8, 128)), ("c", *OWN)
    )
    return update_rows(
        place,
        squares,
        shard,
        other,
        weight_in,
        moment_in,
        square_in,
        weight_out,
        moment_out,
        square_out,
    )


def solution(mesh):
    fine = Mesh(mesh.devices.reshape(8, 2, 4, 4), ("z", "c", "x", "y"))
    histories = ("z", "c", "x", "y")
    placed = (
        P(histories, None, None),
        P(histories, None, None),
        P(histories),
        P(),
        P(OWN, None),
        P(OWN, None),
        P(OWN, None),
        P(OWN, None),
        P(OWN, None),
        P(OWN, None),
    )
    return jax.shard_map(
        per_device,
        mesh=fine,
        in_specs=placed,
        out_specs=(P(OWN, None),) * 6,
        check_vma=False,
    )
```

```python
import functools

import jax
import jax.numpy as jnp
from jax import lax
from jax.experimental import pallas as pl
from jax.experimental.pallas import tpu as pltpu
from jax.sharding import Mesh
from jax.sharding import PartitionSpec as P

BLK = 256
HEAD_WIDTH = 256

norm_eps = 1e-06
beta_first = 0.9
beta_second = 0.95
learn_rate = 0.01
step_number = 10.0
update_eps = 1e-08
ratio_eps = 1e-06

OWN = ("x", "y")
SWAP = ((0, 1), (1, 0))

ROUNDS = (((0, 1), (0, 3), (1, 1), (1, 3)), ((0, 3), (0, 1), (1, 3), (1, 1)))


def rms_scale(values):
    return values * lax.rsqrt(jnp.mean(values * values, axis=-1, keepdims=True) + norm_eps)


def sigmoid(values):
    return 0.5 + 0.5 * jnp.tanh(0.5 * values)


def allowed_mask(length):
    row = lax.broadcasted_iota(jnp.int32, (BLK, BLK), 0)
    col = lax.broadcasted_iota(jnp.int32, (BLK, BLK), 1)
    return ((col <= row) & (row < length)).astype(jnp.float32) * (1.0 / BLK)


def dot_nt(left, right):
    return lax.dot_general(
        left, right, (((1,), (1,)), ((), ())), preferred_element_type=jnp.float32
    )


def dot_tn(left, right):
    return lax.dot_general(
        left, right, (((0,), (0,)), ((), ())), preferred_element_type=jnp.float32
    )


def dot_nn(left, right):
    return jnp.dot(left, right, preferred_element_type=jnp.float32)


def silu_slope(values):
    sig = sigmoid(values)
    act = values * sig
    return act, sig + act * (1.0 - sig)


def scatter_slot(mask, part, core):
    x, y = mask >> 2, mask & 3
    one, two = jnp.where(core == 0, x, y), jnp.where(core == 0, y, x)
    high, odd = two >> 1, (two >> 1) ^ (two & 1)
    return one + 4 * (odd + 2 * high if part == 0 else high + 2 * odd)


def gather_mask(slot, part, core):
    links = (1, 3) if part == 0 else (3, 1)
    one, two = (
        (links[0] if bits & 1 else 0) ^ (links[1] if bits & 2 else 0)
        for bits in (slot & 3, slot >> 2)
    )
    return jnp.where(core == 0, 4 * one + two, 4 * two + one)


def place_rows(part, place, held, store):
    count, rows, _ = held[0].shape
    for slot in range(4 * count):
        block = held[slot // count][slot % count]
        owner = place[0] ^ gather_mask(slot, part, place[1])
        store(pl.ds(pl.multiple_of(owner * rows, rows), rows), block)


def forward_kernel(
    place,
    lengths,
    normed,
    *refs,
):
    projected, gating, scores, mixed, outer, weight = refs[8:]
    count, rows, width = mixed.shape
    share = outer.shape[1] // 2

    @pl.when(pl.program_id(0) == 0)
    def _():
        def store_0(at, block):
            weight[at, :width] = block[:, :width]
            weight[at, 2 * width : 3 * width] = block[:, width : 2 * width]
            outer[at, :share] = block[:, 2 * width :]

        def store_1(at, block):
            weight[at, width : 2 * width] = block[:, :width]
            weight[at, 3 * width :] = block[:, width : 2 * width]
            outer[at, share:] = block[:, 2 * width :]

        place_rows(0, place, refs[:4], store_0)
        place_rows(1, place, refs[4:8], store_1)

    lines = normed[...].reshape(count * rows, -1)
    projected[...] = dot_nn(lines, weight[:, : 3 * width]).reshape(projected.shape)
    gating[...] = dot_nn(lines, weight[:, 3 * width :]).reshape(gating.shape)
    for item in range(count):
        proj = projected[item]
        held = (proj * sigmoid(proj)).astype(jnp.bfloat16)
        allowed = allowed_mask(lengths[pl.program_id(0) * count + item])
        for start in range(0, width, HEAD_WIDTH):
            queries, values, key_part = (
                held[:, part * width + start : part * width + start + HEAD_WIDTH]
                for part in range(3)
            )
            score = dot_nt(queries, key_part) * HEAD_WIDTH ** (-0.5)
            scores[item, start // HEAD_WIDTH] = score
            attention = (score * sigmoid(score) * allowed).astype(jnp.bfloat16)
            mixed[item, :, start : start + HEAD_WIDTH] = dot_nn(attention, values)


def gating_kernel(place, gating, masked, keep, recv, mixed, grad_gated, stats):
    count, rows, width = mixed.shape
    proj = gating[...].reshape(count * rows, width)
    core = place[1]
    mine = masked[:, :, pl.ds(pl.multiple_of(core * width, width), width)]
    others = masked[:, :, pl.ds(pl.multiple_of((1 - core) * width, width), width)]
    grad = (
        dot_nt(mine.reshape(count * rows, width), keep[...])
        + dot_nt(others.reshape(count * rows, width), recv[...])
    ).astype(jnp.bfloat16)
    grad_gated[...] = grad.reshape(grad_gated.shape)
    mix = mixed[...].reshape(count * rows, width)
    square = jnp.sum(mix * mix, axis=1, keepdims=True)
    cross = jnp.sum(
        grad.astype(jnp.float32) * (proj * sigmoid(proj)) * mix, axis=1, keepdims=True
    )
    lane = lax.broadcasted_iota(jnp.int32, (count * rows, 128), 1)
    stats[...] = jnp.where(lane == 0, square, cross).reshape(stats.shape)


def norm_scale(model_width, stats, stats_other):
    total = (stats[...] + stats_other[...]).reshape(-1, stats.shape[2])
    inv = lax.rsqrt(total[:, 0:1] / model_width + norm_eps)
    return inv, inv * inv * inv * (total[:, 1:2] / model_width)


def outer_kernel(place, projected, mixed, stats, stats_other, masked, term, total):
    width = mixed.shape[2]
    inv, _ = norm_scale(2 * width, stats, stats_other)
    proj = projected[...].reshape(-1, width)
    gated = (mixed[...].reshape(-1, width) * inv * (proj * sigmoid(proj))).astype(jnp.bfloat16)
    step = pl.program_id(0)
    for side in range(2):
        column = (place[1] + side) % 2
        part = masked[:, :, pl.ds(pl.multiple_of(column * width, width), width)]
        value = dot_tn(gated, part.reshape(-1, width))

        @pl.when(step == 0)
        def _():
            total[side] = value

        @pl.when(step > 0)
        def _():
            total[side] += value

    @pl.when(step == pl.num_programs(0) - 1)
    def _():
        term[...] = total[...].astype(jnp.bfloat16)


def backward_kernel(
    lengths, gating_in, projected, scores, mixed, grad_gated, stats, stats_other, grads
):
    width = mixed.shape[2]
    inv, back = norm_scale(2 * width, stats, stats_other)
    gating, slope = silu_slope(gating_in[0])
    mix = mixed[0]
    grad = grad_gated[0].astype(jnp.float32)
    grads[0, :, :width] = (grad * (mix * inv) * slope).astype(jnp.bfloat16)
    grad_mixed = (inv * (grad * gating) - mix * back).astype(jnp.bfloat16)
    allowed = allowed_mask(lengths[pl.program_id(0)])
    for start in range(0, width, HEAD_WIDTH):
        (queries, queries_slope), (values, values_slope), (key_part, keys_slope) = (
            silu_slope(projected[0, :, part * width + start : part * width + start + HEAD_WIDTH])
            for part in range(3)
        )
        act, slope = silu_slope(scores[0, start // HEAD_WIDTH])
        attention = (act * allowed).astype(jnp.bfloat16)
        grad_head = grad_mixed[:, start : start + HEAD_WIDTH]
        grad_att = dot_nt(grad_head, values.astype(jnp.bfloat16)).astype(jnp.bfloat16)
        grad_score = (
            grad_att.astype(jnp.float32) * allowed * slope * HEAD_WIDTH ** (-0.5)
        ).astype(jnp.bfloat16)
        for part, (grad_part, side) in enumerate(
            (
                (dot_tn(attention, grad_head), values_slope),
                (dot_nn(grad_score, key_part.astype(jnp.bfloat16)), queries_slope),
                (dot_tn(grad_score, queries.astype(jnp.bfloat16)), keys_slope),
            ),
            1,
        ):
            held = grad_part.astype(jnp.bfloat16).astype(jnp.float32)
            at = part * width + start
            grads[0, :, at : at + HEAD_WIDTH] = (held * side).astype(jnp.bfloat16)


def terms_kernel(place, normed_t, grads, keep, recv, *refs):
    outs, held, sems = refs[:8], refs[8:10], refs[10]
    step = pl.program_id(0)
    slots, rows, _ = held[0].shape
    width = grads.shape[1]
    half = keep.shape[0] // rows
    core = place[1]

    def copies(turn):
        part, columns = turn // 2, (slice(width, None) if turn % 2 else slice(0, width))
        span = pl.ds(columns.start, (held[0].shape[2] if turn % 2 else width) - columns.start)
        return [
            pltpu.make_async_copy(
                held[part].at[pl.ds(group * (slots // 4), slots // 4), :, span],
                outs[4 * part + group].at[:, :, span],
                sems.at[4 * turn + group],
            )
            for group in range(4)
        ]

    for turn in range(4):

        @pl.when(step == turn)
        def _(turn=turn):
            part, start = turn // 2, (turn % 2) * width
            term = dot_nn(normed_t[...], grads[...]).astype(jnp.bfloat16)
            for block in range(slots):
                slot = scatter_slot(block ^ place[0], part, core)
                held[part][slot, :, start : start + width] = term[block * rows : (block + 1) * rows]
            if turn % 2:
                share = held[part].shape[2] - 2 * width
                cut = slice(part * share, (part + 1) * share)
                for side, outer in ((core, keep), (1 - core, recv)):
                    for block in range(half):
                        slot = scatter_slot((side * half + block) ^ place[0], part, core)
                        value = outer[block * rows : (block + 1) * rows, cut]
                        held[part][slot, :, 2 * width :] = value
            for copy in copies(turn):
                copy.start()

    @pl.when(step == 3)
    def _():
        for turn in range(4):
            for copy in copies(turn):
                copy.wait()


def rows_of(*dims, some=1):
    return pl.BlockSpec((some, *dims), lambda i, *_: (i,) + (0,) * len(dims))


def whole(*dims, buffers=1):
    return pl.BlockSpec(
        dims, lambda i, *_: (0,) * len(dims), pipeline_mode=pl.Buffered(buffer_count=buffers)
    )


def call(kernel, name, grid, prefetch, in_specs, out, inputs, scratch=(), room=18):
    moved = sum(v.size * v.dtype.itemsize for v in inputs)
    return pl.pallas_call(
        kernel,
        grid_spec=pltpu.PrefetchScalarGridSpec(
            num_scalar_prefetch=len(prefetch),
            grid=grid,
            in_specs=in_specs,
            out_specs=[spec for spec, _, _ in out],
            scratch_shapes=list(scratch),
        ),
        out_shape=[jax.ShapeDtypeStruct(shape, dtype) for _, shape, dtype in out],
        compiler_params=pltpu.CompilerParams(vmem_limit_bytes=room * 1024 * 1024),
        cost_estimate=pl.CostEstimate(flops=1, bytes_accessed=1, transcendentals=0),
        name=name,
    )(*prefetch, *inputs)


def attention_forward(place, lengths, normed, held):
    count, rows, depth = normed.shape
    width = depth // 2
    heads = width // HEAD_WIDTH
    return call(
        forward_kernel,
        "attention_forward",
        (count // 2,),
        (place, lengths),
        [rows_of(rows, depth, some=2)]
        + [whole(*part.shape) for part in held],
        [
            (rows_of(rows, 3 * width, some=2), (count, rows, 3 * width), jnp.float32),
            (rows_of(rows, width, some=2), (count, rows, width), jnp.float32),
            (rows_of(heads, rows, rows, some=2), (count, heads, rows, rows), jnp.float32),
            (rows_of(rows, width, some=2), (count, rows, width), jnp.float32),
            (whole(depth, width), (depth, width), jnp.bfloat16),
        ],
        (normed, *held),
        [pltpu.VMEM((depth, 4 * width), jnp.bfloat16)],
        room=30,
    )


def gating_forward(place, gating, masked, keep, recv, mixed):
    count, rows, width = mixed.shape
    return call(
        gating_kernel,
        "gating_forward",
        (count // 2,),
        (place,),
        [
            rows_of(rows, width, some=2),
            rows_of(rows, 2 * width, some=2),
            whole(*keep.shape),
            whole(*recv.shape),
            rows_of(rows, width, some=2),
        ],
        [
            (rows_of(rows, width, some=2), (count, rows, width), jnp.bfloat16),
            (rows_of(rows, 128, some=2), (count, rows, 128), jnp.float32),
        ],
        (gating, masked, keep, recv, mixed),
        room=18,
    )


def stats_specs(count, rows, some=1):
    steps = count // some
    return [
        rows_of(rows, 128, some=some),
        pl.BlockSpec((some, rows, 128), lambda i, *_: ((i + steps // 2) % steps, 0, 0)),
    ]


def outer_term(place, gating, mixed, stats, stats_other, masked):
    count, rows, width = mixed.shape
    block = rows_of(rows, width, some=2)
    shape = (2, width, width)
    return call(
        outer_kernel,
        "outer_term",
        (count // 2,),
        (place,),
        [
            rows_of(rows, width, some=2),
            block,
            *stats_specs(count, rows, 2),
            rows_of(rows, 2 * width, some=2),
        ],
        [(whole(*shape), shape, jnp.bfloat16)],
        (gating, mixed, stats, stats_other, masked),
        [pltpu.VMEM(shape, jnp.float32)],
    )[0]


def attention_back(lengths, gating, projected, scores, mixed, grad_gated, stats, stats_other):
    count, rows, width = mixed.shape
    heads = width // HEAD_WIDTH
    block = rows_of(rows, width)
    return call(
        backward_kernel,
        "attention_back",
        (count,),
        (lengths,),
        [
            block,
            rows_of(rows, 3 * width),
            rows_of(heads, rows, rows),
            block,
            block,
            *stats_specs(count, rows),
        ],
        [(rows_of(rows, 4 * width), (count, rows, 4 * width), jnp.bfloat16)],
        (gating, projected, scores, mixed, grad_gated, stats, stats_other),
    )[0]


def terms(place, owned, normed_t, grads, keep, recv):
    depth, rows = normed_t.shape
    width = grads.shape[1] // 4
    shapes = [(depth // owned // 4, owned, 2 * width + keep.shape[1] // 2)] * 8
    anywhere = pl.BlockSpec(memory_space=pl.ANY)
    outs = call(
        terms_kernel,
        "terms",
        (4,),
        (place,),
        [
            whole(depth, rows, buffers=2),
            pl.BlockSpec((rows, width), lambda i, *_: (0, i)),
            whole(*keep.shape, buffers=2),
            whole(*recv.shape, buffers=2),
        ],
        [(anywhere, shape, jnp.bfloat16) for shape in shapes],
        (normed_t, grads, keep, recv),
        [pltpu.VMEM((4 * count, *rest), jnp.bfloat16) for count, *rest in shapes[::4]]
        + [pltpu.SemaphoreType.DMA((16,))],
    )
    return [outs[:4], outs[4:]]


def sum_squares(values):
    values = values.astype(jnp.float32)
    return jnp.sum(values * values)


def update_kernel(place, squares, mine, other, *refs):
    half = mine.shape[1] // 5
    model_width = 2 * half
    first = place[1] == 0
    owners = squares.shape[0] // 8
    total = sum(squares[8 * i : 8 * i + 1, 0:1] for i in range(owners))
    clip = jnp.minimum(1.0, jnp.sqrt(5.0 * model_width * model_width / (total + norm_eps)))
    for parts, (weight, moment, square, new_weight, new_moment, new_square) in (
        (range(4), (refs[0], refs[1], refs[2], refs[6], refs[7], refs[8])),
        (range(4, 5), (refs[3], refs[4], refs[5], refs[9], refs[10], refs[11])),
    ):
        update_sq = weight_sq = 0.0
        for part in parts:
            at = slice(part * half, (part + 1) * half)
            both = (mine[:, at].astype(jnp.float32), other[:, at].astype(jnp.float32))
            for core in (0, 1):
                grad = jnp.where(first, both[core], both[1 - core]) * clip
                start = (part - parts[0]) * model_width + core * half
                col = slice(start, start + half)
                held = beta_first * moment[:, col] + (1.0 - beta_first) * grad
                held_sq = beta_second * square[:, col] + (1.0 - beta_second) * grad * grad
                new_moment[:, col] = held
                new_square[:, col] = held_sq
                update = (held * (1.0 / (1.0 - beta_first**step_number))) / (
                    jnp.sqrt(held_sq * (1.0 / (1.0 - beta_second**step_number))) + update_eps
                )
                new_weight[:, col] = update
                update_sq += jnp.sum(update * update, axis=1, keepdims=True)
                held = weight[:, col].astype(jnp.float32)
                weight_sq += jnp.sum(held * held, axis=1, keepdims=True)
        ratio = learn_rate * jnp.sqrt(weight_sq) / (jnp.sqrt(update_sq) + ratio_eps)
        new_weight[...] = weight[...].astype(jnp.float32) - ratio * new_weight[...]


def update_rows(place, squares, mine, other, *state):
    rows = 16
    count = mine.shape[0] // rows

    def block(value):
        return pl.BlockSpec((rows, value.shape[1]), lambda i, *_: (i, 0))

    return call(
        update_kernel,
        "update_rows",
        (count,),
        (place,),
        [whole(*squares.shape)] + [block(v) for v in (mine, other, *state)],
        [(block(v), v.shape, jnp.float32) for v in state],
        (squares, mine, other, *state),
    )


def swap_cores(values):
    return lax.ppermute(values, "c", SWAP)


def over_link(values, axis, mask):
    pairs = []
    for core in range(2):
        shift = mask << 2 if axis == core else mask
        pairs += [(16 * core + own, 16 * core + (own ^ shift)) for own in range(16)]
    return lax.ppermute(values, ("c", *OWN), pairs)


def gather_parts(parts, prepare, join):
    held = [part[None] for part in parts]
    for step in range(2):
        got = [over_link(part, *ROUNDS[turn][step]) for turn, part in enumerate(held)]
        held = [jnp.concatenate(pair, axis=0) for pair in zip(held, got)]
        if step == 0:
            held = lax.optimization_barrier(held)
            held[0], beside = prepare(held[0])
        else:
            held, beside = lax.optimization_barrier((held, beside))
    first = [over_link(part, *ROUNDS[turn][2]) for turn, part in enumerate(held)]
    second = [over_link(part, *ROUNDS[turn][3]) for turn, part in enumerate(held)]
    first = lax.optimization_barrier(first)
    both = [over_link(part, *ROUNDS[turn][3]) for turn, part in enumerate(first)]
    second, both, beside = lax.optimization_barrier((second, both, join(beside)))
    return list(zip(held, first, second, both)), beside


def add_blocks(*blocks):
    return sum(block.astype(jnp.float32) for block in blocks).astype(jnp.bfloat16)


def scatter_parts(parts):
    mine, first, second, both = zip(*parts)
    both = [over_link(part, *ROUNDS[turn][3]) for turn, part in enumerate(both)]
    second = [over_link(part, *ROUNDS[turn][3]) for turn, part in enumerate(second)]
    first, both = lax.optimization_barrier((first, both))
    first = [add_blocks(*pair) for pair in zip(first, both)]
    first = [over_link(part, *ROUNDS[turn][2]) for turn, part in enumerate(first)]
    mine, first, second = lax.optimization_barrier((mine, first, second))
    held = [add_blocks(*blocks) for blocks in zip(mine, first, second)]
    held = jnp.concatenate(held, axis=2)
    return add_blocks(held[0], *(over_link(held[mask], 0, mask) for mask in (1, 3, 2)))


def exchange(blocks, axes):
    return lax.all_to_all(blocks, axes, 0, 0, tiled=True)


def per_device(
    tokens,
    cotangent,
    lengths,
    norm_gain,
    weight_in,
    weight_out,
    moment_in,
    square_in,
    moment_out,
    square_out,
):
    slots, rows, model_width = tokens.shape
    half = model_width // 2
    share = half // 4
    core = lax.axis_index("c")
    own = lax.axis_index(OWN)
    owners = lax.axis_size(OWN)
    planes = lax.axis_size("z")
    owned = weight_in.shape[0]
    place = jnp.stack([own, core]).astype(jnp.int32)

    mine = [
        lax.dynamic_slice_in_dim(weight_in, part * model_width + core * half, half, axis=1)
        for part in range(4)
    ]
    mine_out = lax.dynamic_slice_in_dim(weight_out, core * half, half, axis=1)
    def prepare(got):
        got, token_rows, cot_rows, lengths_other = lax.optimization_barrier(
            (got, tokens, cotangent, swap_cores(lengths))
        )
        normed = (rms_scale(token_rows.astype(jnp.float32)) * norm_gain).astype(jnp.bfloat16)
        row_index = jnp.arange(rows, dtype=jnp.int32)
        live = row_index[None, :] < lengths[:, None]
        masked = jnp.where(live[:, :, None], cot_rows, jnp.zeros_like(cot_rows))
        mine = jnp.concatenate([normed, masked], axis=0)
        return got, (mine, swap_cores(mine), lengths_other)

    def join(made):
        mine, other, lengths_other = made
        normed, masked = (
            jnp.concatenate([side[at : at + slots] for side in (mine, other)], axis=0)
            for at in (0, slots)
        )
        all_lengths = jnp.concatenate([lengths, lengths_other], axis=0)
        return normed, masked, all_lengths, normed.reshape(-1, model_width).T

    parts, (normed, masked, all_lengths, normed_t) = gather_parts(
        [
            jnp.concatenate([mine[2], mine[3], mine_out[:, : half // 2]], axis=1),
            jnp.concatenate([mine[1], mine[0], mine_out[:, half // 2 :]], axis=1),
        ],
        prepare,
        join,
    )

    projected, gating, scores, mixed, outer_cols = attention_forward(
        place, all_lengths, normed, (*parts[0], *parts[1])
    )
    outer_cols = outer_cols.reshape(2, half, half)
    keep = lax.dynamic_index_in_dim(outer_cols, core, axis=0, keepdims=False)
    recv = swap_cores(lax.dynamic_index_in_dim(outer_cols, 1 - core, axis=0, keepdims=False))
    grad_gated, stats = gating_forward(place, gating, masked, keep, recv, mixed)
    stats_other = swap_cores(stats)
    outer = outer_term(place, gating, mixed, stats, stats_other, masked)
    outer_recv = swap_cores(outer[1])
    grads = attention_back(
        all_lengths, gating, projected, scores, mixed, grad_gated, stats, stats_other
    )
    part = scatter_parts(
        terms(place, owned, normed_t, grads.reshape(-1, 4 * half), outer[0], outer_recv)
    )
    wide = part.shape[1] // 2
    part = jnp.concatenate(
        [part[:, : 2 * half], part[:, wide : wide + 2 * half]]
        + [part[:, at + 2 * half : at + wide] for at in (0, wide)],
        axis=1,
    )

    piece = jnp.sum(
        exchange(part, "z").reshape(planes, owned // planes, -1).astype(jnp.float32), axis=0
    ).astype(jnp.bfloat16)
    shard = exchange(
        jnp.broadcast_to(piece[None], (planes, *piece.shape)).reshape(owned, -1), "z"
    )
    other = swap_cores(shard)
    squares = exchange(
        jnp.broadcast_to(sum_squares(shard), (2 * owners * 8, 128)), ("c", *OWN)
    )
    return update_rows(
        place,
        squares,
        shard,
        other,
        weight_in,
        moment_in,
        square_in,
        weight_out,
        moment_out,
        square_out,
    )


def solution(mesh):
    fine = Mesh(mesh.devices.reshape(8, 2, 4, 4), ("z", "c", "x", "y"))
    histories = ("z", "c", "x", "y")
    placed = (
        P(histories, None, None),
        P(histories, None, None),
        P(histories),
        P(),
        P(OWN, None),
        P(OWN, None),
        P(OWN, None),
        P(OWN, None),
        P(OWN, None),
        P(OWN, None),
    )
    return jax.shard_map(
        per_device,
        mesh=fine,
        in_specs=placed,
        out_specs=(P(OWN, None),) * 6,
        check_vma=False,
    )
```

```python
import functools

import jax
import jax.numpy as jnp
from jax import lax
from jax.experimental import pallas as pl
from jax.experimental.pallas import tpu as pltpu
from jax.sharding import Mesh
from jax.sharding import PartitionSpec as P

BLK = 256
HEAD_WIDTH = 256

norm_eps = 1e-06
beta_first = 0.9
beta_second = 0.95
learn_rate = 0.01
step_number = 10.0
update_eps = 1e-08
ratio_eps = 1e-06

OWN = ("x", "y")
SWAP = ((0, 1), (1, 0))

ROUNDS = (((0, 1), (0, 3), (1, 1), (1, 3)), ((0, 3), (0, 1), (1, 3), (1, 1)))


def rms_scale(values):
    return values * lax.rsqrt(jnp.mean(values * values, axis=-1, keepdims=True) + norm_eps)


def sigmoid(values):
    return 0.5 + 0.5 * jnp.tanh(0.5 * values)


def allowed_mask(length):
    row = lax.broadcasted_iota(jnp.int32, (BLK, BLK), 0)
    col = lax.broadcasted_iota(jnp.int32, (BLK, BLK), 1)
    return ((col <= row) & (row < length)).astype(jnp.float32) * (1.0 / BLK)


def dot_nt(left, right):
    return lax.dot_general(
        left, right, (((1,), (1,)), ((), ())), preferred_element_type=jnp.float32
    )


def dot_tn(left, right):
    return lax.dot_general(
        left, right, (((0,), (0,)), ((), ())), preferred_element_type=jnp.float32
    )


def dot_nn(left, right):
    return jnp.dot(left, right, preferred_element_type=jnp.float32)


def silu_slope(values):
    sig = sigmoid(values)
    act = values * sig
    return act, sig + act * (1.0 - sig)


def scatter_slot(mask, part, core):
    x, y = mask >> 2, mask & 3
    one, two = jnp.where(core == 0, x, y), jnp.where(core == 0, y, x)
    high, odd = two >> 1, (two >> 1) ^ (two & 1)
    return one + 4 * (odd + 2 * high if part == 0 else high + 2 * odd)


def gather_mask(slot, part, core):
    links = (1, 3) if part == 0 else (3, 1)
    one, two = (
        (links[0] if bits & 1 else 0) ^ (links[1] if bits & 2 else 0)
        for bits in (slot & 3, slot >> 2)
    )
    return jnp.where(core == 0, 4 * one + two, 4 * two + one)


def place_rows(part, place, held, store):
    count, rows, _ = held[0].shape
    for slot in range(4 * count):
        block = held[slot // count][slot % count]
        owner = place[0] ^ gather_mask(slot, part, place[1])
        store(pl.ds(pl.multiple_of(owner * rows, rows), rows), block)


def forward_kernel(
    place,
    lengths,
    normed,
    *refs,
):
    projected, gating, scores, mixed, outer, weight = refs[8:]
    count, rows, width = mixed.shape
    share = outer.shape[1] // 2

    @pl.when(pl.program_id(0) == 0)
    def _():
        def store_0(at, block):
            weight[at, :width] = block[:, :width]
            weight[at, 2 * width : 3 * width] = block[:, width : 2 * width]
            outer[at, :share] = block[:, 2 * width :]

        def store_1(at, block):
            weight[at, width : 2 * width] = block[:, :width]
            weight[at, 3 * width :] = block[:, width : 2 * width]
            outer[at, share:] = block[:, 2 * width :]

        place_rows(0, place, refs[:4], store_0)
        place_rows(1, place, refs[4:8], store_1)

    lines = normed[...].reshape(count * rows, -1)
    projected[...] = dot_nn(lines, weight[:, : 3 * width]).reshape(projected.shape)
    gating[...] = dot_nn(lines, weight[:, 3 * width :]).reshape(gating.shape)
    for item in range(count):
        proj = projected[item]
        held = (proj * sigmoid(proj)).astype(jnp.bfloat16)
        allowed = allowed_mask(lengths[pl.program_id(0) * count + item])
        for start in range(0, width, HEAD_WIDTH):
            queries, values, key_part = (
                held[:, part * width + start : part * width + start + HEAD_WIDTH]
                for part in range(3)
            )
            score = dot_nt(queries, key_part) * HEAD_WIDTH ** (-0.5)
            scores[item, start // HEAD_WIDTH] = score
            attention = (score * sigmoid(score) * allowed).astype(jnp.bfloat16)
            mixed[item, :, start : start + HEAD_WIDTH] = dot_nn(attention, values)


def gating_kernel(place, gating, masked, keep, recv, mixed, grad_gated, stats):
    count, rows, width = mixed.shape
    proj = gating[...].reshape(count * rows, width)
    core = place[1]
    mine = masked[:, :, pl.ds(pl.multiple_of(core * width, width), width)]
    others = masked[:, :, pl.ds(pl.multiple_of((1 - core) * width, width), width)]
    grad = (
        dot_nt(mine.reshape(count * rows, width), keep[...])
        + dot_nt(others.reshape(count * rows, width), recv[...])
    ).astype(jnp.bfloat16)
    grad_gated[...] = grad.reshape(grad_gated.shape)
    mix = mixed[...].reshape(count * rows, width)
    square = jnp.sum(mix * mix, axis=1, keepdims=True)
    cross = jnp.sum(
        grad.astype(jnp.float32) * (proj * sigmoid(proj)) * mix, axis=1, keepdims=True
    )
    lane = lax.broadcasted_iota(jnp.int32, (count * rows, 128), 1)
    stats[...] = jnp.where(lane == 0, square, cross).reshape(stats.shape)


def norm_scale(model_width, stats, stats_other):
    total = (stats[...] + stats_other[...]).reshape(-1, stats.shape[2])
    inv = lax.rsqrt(total[:, 0:1] / model_width + norm_eps)
    return inv, inv * inv * inv * (total[:, 1:2] / model_width)


def outer_kernel(place, projected, mixed, stats, stats_other, masked, term, total):
    width = mixed.shape[2]
    inv, _ = norm_scale(2 * width, stats, stats_other)
    proj = projected[...].reshape(-1, width)
    gated = (mixed[...].reshape(-1, width) * inv * (proj * sigmoid(proj))).astype(jnp.bfloat16)
    step = pl.program_id(0)
    for side in range(2):
        column = (place[1] + side) % 2
        part = masked[:, :, pl.ds(pl.multiple_of(column * width, width), width)]
        value = dot_tn(gated, part.reshape(-1, width))

        @pl.when(step == 0)
        def _():
            total[side] = value

        @pl.when(step > 0)
        def _():
            total[side] += value

    @pl.when(step == pl.num_programs(0) - 1)
    def _():
        term[...] = total[...].astype(jnp.bfloat16)


def backward_kernel(
    lengths, gating_in, projected, scores, mixed, grad_gated, stats, stats_other, grads
):
    width = mixed.shape[2]
    inv, back = norm_scale(2 * width, stats, stats_other)
    gating, slope = silu_slope(gating_in[0])
    mix = mixed[0]
    grad = grad_gated[0].astype(jnp.float32)
    grads[0, :, :width] = (grad * (mix * inv) * slope).astype(jnp.bfloat16)
    grad_mixed = (inv * (grad * gating) - mix * back).astype(jnp.bfloat16)
    allowed = allowed_mask(lengths[pl.program_id(0)])
    for start in range(0, width, HEAD_WIDTH):
        (queries, queries_slope), (values, values_slope), (key_part, keys_slope) = (
            silu_slope(projected[0, :, part * width + start : part * width + start + HEAD_WIDTH])
            for part in range(3)
        )
        act, slope = silu_slope(scores[0, start // HEAD_WIDTH])
        attention = (act * allowed).astype(jnp.bfloat16)
        grad_head = grad_mixed[:, start : start + HEAD_WIDTH]
        grad_att = dot_nt(grad_head, values.astype(jnp.bfloat16)).astype(jnp.bfloat16)
        grad_score = (
            grad_att.astype(jnp.float32) * allowed * slope * HEAD_WIDTH ** (-0.5)
        ).astype(jnp.bfloat16)
        for part, (grad_part, side) in enumerate(
            (
                (dot_tn(attention, grad_head), values_slope),
                (dot_nn(grad_score, key_part.astype(jnp.bfloat16)), queries_slope),
                (dot_tn(grad_score, queries.astype(jnp.bfloat16)), keys_slope),
            ),
            1,
        ):
            held = grad_part.astype(jnp.bfloat16).astype(jnp.float32)
            at = part * width + start
            grads[0, :, at : at + HEAD_WIDTH] = (held * side).astype(jnp.bfloat16)


def terms_kernel(place, normed_t, grads, keep, recv, *refs):
    outs, held, sems = refs[:8], refs[8:10], refs[10]
    step = pl.program_id(0)
    slots, rows, _ = held[0].shape
    width = grads.shape[1]
    half = keep.shape[0] // rows
    core = place[1]

    def copies(turn):
        part, columns = turn // 2, (slice(width, None) if turn % 2 else slice(0, width))
        span = pl.ds(columns.start, (held[0].shape[2] if turn % 2 else width) - columns.start)
        return [
            pltpu.make_async_copy(
                held[part].at[pl.ds(group * (slots // 4), slots // 4), :, span],
                outs[4 * part + group].at[:, :, span],
                sems.at[4 * turn + group],
            )
            for group in range(4)
        ]

    for turn in range(4):

        @pl.when(step == turn)
        def _(turn=turn):
            part, start = turn // 2, (turn % 2) * width
            term = dot_nn(normed_t[...], grads[...]).astype(jnp.bfloat16)
            for block in range(slots):
                slot = scatter_slot(block ^ place[0], part, core)
                held[part][slot, :, start : start + width] = term[block * rows : (block + 1) * rows]
            if turn % 2:
                share = held[part].shape[2] - 2 * width
                cut = slice(part * share, (part + 1) * share)
                for side, outer in ((core, keep), (1 - core, recv)):
                    for block in range(half):
                        slot = scatter_slot((side * half + block) ^ place[0], part, core)
                        value = outer[block * rows : (block + 1) * rows, cut]
                        held[part][slot, :, 2 * width :] = value
            for copy in copies(turn):
                copy.start()

    @pl.when(step == 3)
    def _():
        for turn in range(4):
            for copy in copies(turn):
                copy.wait()


def rows_of(*dims, some=1):
    return pl.BlockSpec((some, *dims), lambda i, *_: (i,) + (0,) * len(dims))


def whole(*dims, buffers=1):
    return pl.BlockSpec(
        dims, lambda i, *_: (0,) * len(dims), pipeline_mode=pl.Buffered(buffer_count=buffers)
    )


def call(kernel, name, grid, prefetch, in_specs, out, inputs, scratch=(), room=18):
    moved = sum(v.size * v.dtype.itemsize for v in inputs)
    return pl.pallas_call(
        kernel,
        grid_spec=pltpu.PrefetchScalarGridSpec(
            num_scalar_prefetch=len(prefetch),
            grid=grid,
            in_specs=in_specs,
            out_specs=[spec for spec, _, _ in out],
            scratch_shapes=list(scratch),
        ),
        out_shape=[jax.ShapeDtypeStruct(shape, dtype) for _, shape, dtype in out],
        compiler_params=pltpu.CompilerParams(vmem_limit_bytes=room * 1024 * 1024),
        cost_estimate=pl.CostEstimate(flops=1, bytes_accessed=1, transcendentals=0),
        name=name,
    )(*prefetch, *inputs)


def attention_forward(place, lengths, normed, held):
    count, rows, depth = normed.shape
    width = depth // 2
    heads = width // HEAD_WIDTH
    return call(
        forward_kernel,
        "attention_forward",
        (count // 2,),
        (place, lengths),
        [rows_of(rows, depth, some=2)]
        + [whole(*part.shape) for part in held],
        [
            (rows_of(rows, 3 * width, some=2), (count, rows, 3 * width), jnp.float32),
            (rows_of(rows, width, some=2), (count, rows, width), jnp.float32),
            (rows_of(heads, rows, rows, some=2), (count, heads, rows, rows), jnp.float32),
            (rows_of(rows, width, some=2), (count, rows, width), jnp.float32),
            (whole(depth, width), (depth, width), jnp.bfloat16),
        ],
        (normed, *held),
        [pltpu.VMEM((depth, 4 * width), jnp.bfloat16)],
        room=30,
    )


def gating_forward(place, gating, masked, keep, recv, mixed):
    count, rows, width = mixed.shape
    return call(
        gating_kernel,
        "gating_forward",
        (count // 2,),
        (place,),
        [
            rows_of(rows, width, some=2),
            rows_of(rows, 2 * width, some=2),
            whole(*keep.shape),
            whole(*recv.shape),
            rows_of(rows, width, some=2),
        ],
        [
            (rows_of(rows, width, some=2), (count, rows, width), jnp.bfloat16),
            (rows_of(rows, 128, some=2), (count, rows, 128), jnp.float32),
        ],
        (gating, masked, keep, recv, mixed),
        room=18,
    )


def stats_specs(count, rows, some=1):
    steps = count // some
    return [
        rows_of(rows, 128, some=some),
        pl.BlockSpec((some, rows, 128), lambda i, *_: ((i + steps // 2) % steps, 0, 0)),
    ]


def outer_term(place, gating, mixed, stats, stats_other, masked):
    count, rows, width = mixed.shape
    block = rows_of(rows, width, some=2)
    shape = (2, width, width)
    return call(
        outer_kernel,
        "outer_term",
        (count // 2,),
        (place,),
        [
            rows_of(rows, width, some=2),
            block,
            *stats_specs(count, rows, 2),
            rows_of(rows, 2 * width, some=2),
        ],
        [(whole(*shape), shape, jnp.bfloat16)],
        (gating, mixed, stats, stats_other, masked),
        [pltpu.VMEM(shape, jnp.float32)],
    )[0]


def attention_back(lengths, gating, projected, scores, mixed, grad_gated, stats, stats_other):
    count, rows, width = mixed.shape
    heads = width // HEAD_WIDTH
    block = rows_of(rows, width)
    return call(
        backward_kernel,
        "attention_back",
        (count,),
        (lengths,),
        [
            block,
            rows_of(rows, 3 * width),
            rows_of(heads, rows, rows),
            block,
            block,
            *stats_specs(count, rows),
        ],
        [(rows_of(rows, 4 * width), (count, rows, 4 * width), jnp.bfloat16)],
        (gating, projected, scores, mixed, grad_gated, stats, stats_other),
    )[0]


def terms(place, owned, normed_t, grads, keep, recv):
    depth, rows = normed_t.shape
    width = grads.shape[1] // 4
    shapes = [(depth // owned // 4, owned, 2 * width + keep.shape[1] // 2)] * 8
    anywhere = pl.BlockSpec(memory_space=pl.ANY)
    outs = call(
        terms_kernel,
        "terms",
        (4,),
        (place,),
        [
            whole(depth, rows, buffers=2),
            pl.BlockSpec((rows, width), lambda i, *_: (0, i)),
            whole(*keep.shape, buffers=2),
            whole(*recv.shape, buffers=2),
        ],
        [(anywhere, shape, jnp.bfloat16) for shape in shapes],
        (normed_t, grads, keep, recv),
        [pltpu.VMEM((4 * count, *rest), jnp.bfloat16) for count, *rest in shapes[::4]]
        + [pltpu.SemaphoreType.DMA((16,))],
    )
    return [outs[:4], outs[4:]]


def sum_squares(values):
    values = values.astype(jnp.float32)
    return jnp.sum(values * values)


def update_kernel(place, squares, mine, other, *refs):
    half = mine.shape[1] // 5
    model_width = 2 * half
    first = place[1] == 0
    owners = squares.shape[0] // 8
    total = sum(squares[8 * i : 8 * i + 1, 0:1] for i in range(owners))
    clip = jnp.minimum(1.0, jnp.sqrt(5.0 * model_width * model_width / (total + norm_eps)))
    for parts, (weight, moment, square, new_weight, new_moment, new_square) in (
        (range(4), (refs[0], refs[1], refs[2], refs[6], refs[7], refs[8])),
        (range(4, 5), (refs[3], refs[4], refs[5], refs[9], refs[10], refs[11])),
    ):
        update_sq = weight_sq = 0.0
        for part in parts:
            at = slice(part * half, (part + 1) * half)
            both = (mine[:, at].astype(jnp.float32), other[:, at].astype(jnp.float32))
            for core in (0, 1):
                grad = jnp.where(first, both[core], both[1 - core]) * clip
                start = (part - parts[0]) * model_width + core * half
                col = slice(start, start + half)
                held = beta_first * moment[:, col] + (1.0 - beta_first) * grad
                held_sq = beta_second * square[:, col] + (1.0 - beta_second) * grad * grad
                new_moment[:, col] = held
                new_square[:, col] = held_sq
                update = (held * (1.0 / (1.0 - beta_first**step_number))) / (
                    jnp.sqrt(held_sq * (1.0 / (1.0 - beta_second**step_number))) + update_eps
                )
                new_weight[:, col] = update
                update_sq += jnp.sum(update * update, axis=1, keepdims=True)
                held = weight[:, col].astype(jnp.float32)
                weight_sq += jnp.sum(held * held, axis=1, keepdims=True)
        ratio = learn_rate * jnp.sqrt(weight_sq) / (jnp.sqrt(update_sq) + ratio_eps)
        new_weight[...] = weight[...].astype(jnp.float32) - ratio * new_weight[...]


def update_rows(place, squares, mine, other, *state):
    rows = 16
    count = mine.shape[0] // rows

    def block(value):
        return pl.BlockSpec((rows, value.shape[1]), lambda i, *_: (i, 0))

    return call(
        update_kernel,
        "update_rows",
        (count,),
        (place,),
        [whole(*squares.shape)] + [block(v) for v in (mine, other, *state)],
        [(block(v), v.shape, jnp.float32) for v in state],
        (squares, mine, other, *state),
    )


def swap_cores(values):
    return lax.ppermute(values, "c", SWAP)


def over_link(values, axis, mask):
    pairs = []
    for core in range(2):
        shift = mask << 2 if axis == core else mask
        pairs += [(16 * core + own, 16 * core + (own ^ shift)) for own in range(16)]
    return lax.ppermute(values, ("c", *OWN), pairs)


def gather_parts(parts, prepare, join):
    held = [part[None] for part in parts]
    for step in range(2):
        got = [over_link(part, *ROUNDS[turn][step]) for turn, part in enumerate(held)]
        held = [jnp.concatenate(pair, axis=0) for pair in zip(held, got)]
        held = lax.optimization_barrier(held)
        if step == 0:
            held[0], beside = prepare(held[0])
    first = [over_link(part, *ROUNDS[turn][2]) for turn, part in enumerate(held)]
    second = [over_link(part, *ROUNDS[turn][3]) for turn, part in enumerate(held)]
    first = lax.optimization_barrier(first)
    both = [over_link(part, *ROUNDS[turn][3]) for turn, part in enumerate(first)]
    second, both, beside = lax.optimization_barrier((second, both, join(beside)))
    return list(zip(held, first, second, both)), beside


def add_blocks(*blocks):
    return sum(block.astype(jnp.float32) for block in blocks).astype(jnp.bfloat16)


def scatter_parts(parts):
    mine, first, second, both = zip(*parts)
    both = [over_link(part, *ROUNDS[turn][3]) for turn, part in enumerate(both)]
    second = [over_link(part, *ROUNDS[turn][3]) for turn, part in enumerate(second)]
    first, both = lax.optimization_barrier((first, both))
    first = [add_blocks(*pair) for pair in zip(first, both)]
    first = [over_link(part, *ROUNDS[turn][2]) for turn, part in enumerate(first)]
    mine, first, second = lax.optimization_barrier((mine, first, second))
    held = [add_blocks(*blocks) for blocks in zip(mine, first, second)]
    held = jnp.concatenate(held, axis=2)
    return add_blocks(held[0], *(over_link(held[mask], 0, mask) for mask in (1, 3, 2)))


def exchange(blocks, axes):
    return lax.all_to_all(blocks, axes, 0, 0, tiled=True)


def per_device(
    tokens,
    cotangent,
    lengths,
    norm_gain,
    weight_in,
    weight_out,
    moment_in,
    square_in,
    moment_out,
    square_out,
):
    slots, rows, model_width = tokens.shape
    half = model_width // 2
    share = half // 4
    core = lax.axis_index("c")
    own = lax.axis_index(OWN)
    owners = lax.axis_size(OWN)
    planes = lax.axis_size("z")
    owned = weight_in.shape[0]
    place = jnp.stack([own, core]).astype(jnp.int32)

    mine = [
        lax.dynamic_slice_in_dim(weight_in, part * model_width + core * half, half, axis=1)
        for part in range(4)
    ]
    mine_out = lax.dynamic_slice_in_dim(weight_out, core * half, half, axis=1)
    def prepare(got):
        got, token_rows, cot_rows, lengths_other = lax.optimization_barrier(
            (got, tokens, cotangent, swap_cores(lengths))
        )
        normed = (rms_scale(token_rows.astype(jnp.float32)) * norm_gain).astype(jnp.bfloat16)
        row_index = jnp.arange(rows, dtype=jnp.int32)
        live = row_index[None, :] < lengths[:, None]
        masked = jnp.where(live[:, :, None], cot_rows, jnp.zeros_like(cot_rows))
        pairs = (normed, swap_cores(normed)), (masked, swap_cores(masked)), (lengths, lengths_other)
        return got, pairs

    def join(pairs):
        normed, masked, all_lengths = (jnp.concatenate(pair, axis=0) for pair in pairs)
        return normed, masked, all_lengths, normed.reshape(-1, model_width).T

    parts, (normed, masked, all_lengths, normed_t) = gather_parts(
        [
            jnp.concatenate([mine[2], mine[3], mine_out[:, : half // 2]], axis=1),
            jnp.concatenate([mine[1], mine[0], mine_out[:, half // 2 :]], axis=1),
        ],
        prepare,
        join,
    )

    projected, gating, scores, mixed, outer_cols = attention_forward(
        place, all_lengths, normed, (*parts[0], *parts[1])
    )
    outer_cols = outer_cols.reshape(2, half, half)
    keep = lax.dynamic_index_in_dim(outer_cols, core, axis=0, keepdims=False)
    recv = swap_cores(lax.dynamic_index_in_dim(outer_cols, 1 - core, axis=0, keepdims=False))
    grad_gated, stats = gating_forward(place, gating, masked, keep, recv, mixed)
    stats_other = swap_cores(stats)
    outer = outer_term(place, gating, mixed, stats, stats_other, masked)
    outer_recv = swap_cores(outer[1])
    grads = attention_back(
        all_lengths, gating, projected, scores, mixed, grad_gated, stats, stats_other
    )
    part = scatter_parts(
        terms(place, owned, normed_t, grads.reshape(-1, 4 * half), outer[0], outer_recv)
    )
    wide = part.shape[1] // 2
    part = jnp.concatenate(
        [part[:, : 2 * half], part[:, wide : wide + 2 * half]]
        + [part[:, at + 2 * half : at + wide] for at in (0, wide)],
        axis=1,
    )

    piece = jnp.sum(
        exchange(part, "z").reshape(planes, owned // planes, -1).astype(jnp.float32), axis=0
    ).astype(jnp.bfloat16)
    shard = exchange(
        jnp.broadcast_to(piece[None], (planes, *piece.shape)).reshape(owned, -1), "z"
    )
    other = swap_cores(shard)
    squares = exchange(
        jnp.broadcast_to(sum_squares(shard), (2 * owners * 8, 128)), ("c", *OWN)
    )
    return update_rows(
        place,
        squares,
        shard,
        other,
        weight_in,
        moment_in,
        square_in,
        weight_out,
        moment_out,
        square_out,
    )


def solution(mesh):
    fine = Mesh(mesh.devices.reshape(8, 2, 4, 4), ("z", "c", "x", "y"))
    histories = ("z", "c", "x", "y")
    placed = (
        P(histories, None, None),
        P(histories, None, None),
        P(histories),
        P(),
        P(OWN, None),
        P(OWN, None),
        P(OWN, None),
        P(OWN, None),
        P(OWN, None),
        P(OWN, None),
    )
    return jax.shard_map(
        per_device,
        mesh=fine,
        in_specs=placed,
        out_specs=(P(OWN, None),) * 6,
        check_vma=False,
    )
```
